32 devices in a mesh: dp: 4 (over z), tm: 4 (over y, core), head: 2 (over x).
Axes of the slice: x: 2, y: 2, z: 4, core: 2. Of those that a mesh axis runs over, the one named last changes fastest.
Arguments:
- queries: bfloat16 [128, 32, 3072], P(('dp', 'tm'), None, 'head'), parts along dimension 0, may hold values from -16 to 16
- keys: bfloat16 [128, 32, 3072], P(('dp', 'tm'), None, 'head'), parts along dimension 0, may hold values from -16 to 16
- values: bfloat16 [128, 32, 3072], P(('dp', 'tm'), None, 'head'), parts along dimension 0, may hold values from -6 to 6
- out_grad: bfloat16 [128, 32, 3072], P(('dp', 'tm'), None, 'head'), parts along dimension 0, may hold values from -6 to 6
- out_weight: bfloat16 [3072, 3072], P('tm', 'head'), may hold values from -0.109375 to 0.109375
- lists: int32 [32, 8], P(('dp', 'tm')), parts along dimension 0, may hold values from 0 to 31, as said below
Outputs:
- query_grad: bfloat16 [128, 32, 3072], P(('dp', 'tm'), None, 'head'), parts along dimension 0
- key_grad: bfloat16 [128, 32, 3072], P(('dp', 'tm'), None, 'head'), parts along dimension 0
- value_grad: bfloat16 [128, 32, 3072], P(('dp', 'tm'), None, 'head'), parts along dimension 0
- weight_grad: float32 [12288, 3072], P(('dp', 'tm'), 'head'), parts along dimension 0
The draws below stay inside these ranges and needn't reach their ends.
There are 4 independent parts, one for each index of `dp`. The reference program is written for one: setup_inputs(seed, part) draws one part's arguments, and reference() takes and returns one part's arrays. A program takes and returns all parts, laid end to end along the dimension named above; an argument that names none is the same for every part. Nothing has to cross between parts.
Inputs may be any that keep to these rules, and one draw needn't show every extreme that they name: `lists`: each group names 8 different frames of its rollout. Among the 4 list entries of one time shard's groups, at most 4 name frames owned by any one time shard, and those name at most 2 distinct frame; in every draw, every time shard has some owner for which both bounds are reached.
All inputs are finite; a program needn't handle non-finite values.
Results may differ from the reference program's by a relative error of at most 0.039.
Values may be sent and summed in bfloat16 or wider, within the bound.
A program may use at most 128 MiB of HBM per device.

```python
import jax
import jax.numpy as jnp
from jax import lax

HEADS = 24
HD = 128
D = 3072
FTOK = 32
CF = 4
GROUPS_DEV = 2
RET = 8
HF = 3072
FR_DEV = 8
FRAMES = 32
GROUPS = 8
N_TM = 4


def draw_queries(key, part):
    own_key = jax.random.fold_in(key, 5)
    shape = (FRAMES, FTOK, HEADS * HD)
    return jnp.clip(jax.random.normal(own_key, shape, jnp.float32), -6.0, 6.0).astype(jnp.bfloat16)


def draw_keys(key, part):
    own_key = jax.random.fold_in(key, 7)
    shape = (FRAMES, FTOK, HEADS * HD)
    return jnp.clip(jax.random.normal(own_key, shape, jnp.float32), -6.0, 6.0).astype(jnp.bfloat16)


def draw_lists(key, part):
    key = jax.random.fold_in(key, 11)
    key_start, key_base = jax.random.split(key)
    per_owner = max(1, RET // N_TM)
    spread = FR_DEV // per_owner
    start_owner = jax.random.randint(key_start, (), 0, N_TM)
    base_frame = jax.random.randint(key_base, (N_TM, N_TM), 0, spread)
    group_ids = jnp.arange(GROUPS, dtype=jnp.int32)
    device_ids = group_ids // GROUPS_DEV
    within = group_ids % GROUPS_DEV
    entry_ids = jnp.arange(RET, dtype=jnp.int32)
    offset = within[:, None] * (RET // 2) + entry_ids[None, :]
    owner_ids = (start_owner + offset) % N_TM
    repeat = offset // N_TM % per_owner
    local_ids = base_frame[device_ids[:, None], owner_ids] + repeat * spread
    return (owner_ids * FR_DEV + local_ids).astype(jnp.int32)


def strengthened(drawn, key, source, target, blocks, factor):
    def block_of(dim):
        return (jnp.arange(drawn.shape[dim]) // (drawn.shape[dim] // blocks)).reshape((-1,) + (1,) * (drawn.ndim - 1 - dim))

    near = jax.random.permutation(key, blocks)[block_of(target)]
    other_side = (block_of(target) + blocks // 2) % blocks
    return jnp.where((block_of(source) == near) | (block_of(source) == other_side), factor * drawn, drawn)


def steps_of(key, extent, shards, least, high):
    gain = 1.0
    for dim, blocks in shards:
        draws = jax.random.uniform(jax.random.fold_in(jax.random.fold_in(key, 6), dim), (blocks,), jnp.float32, least / len(shards), high / len(shards))
        gain = gain * jnp.repeat(jnp.exp(draws), extent[dim] // blocks).reshape((-1,) + (1,) * (len(extent) - 1 - dim))
    return gain


def scatter_about(key, dims, scale, limit, cuts=(), kind=jnp.bfloat16):
    factor_of = steps_of(key, dims, cuts, -0.22, 0.18) if cuts else 1.0
    values = jax.random.normal(key, dims, jnp.float32) * scale * factor_of
    return jnp.minimum(jnp.maximum(values, -limit), limit).astype(kind)


def bell_draw_with(rng, shape, deviation, most, pieces, heavy, kind=jnp.bfloat16):
    drawn = deviation * jax.random.normal(rng, shape, jnp.float32)
    if pieces:
        drawn = drawn * steps_of(rng, shape, pieces, -0.22, 0.18)
    return jnp.clip(strengthened(drawn, jax.random.fold_in(rng, 3), *heavy), -most, most).astype(kind)


def setup_inputs(seed: int = 0, part: int = 0) -> dict:
    seeds = jax.random.split(jax.random.key(seed), 7)
    part_splits = jax.random.split(jax.random.fold_in(seeds[6], part), 7)
    return {
        "queries": draw_queries(jax.random.fold_in(jax.random.fold_in(seeds[6], part), 71), part),
        "keys": draw_keys(jax.random.fold_in(jax.random.fold_in(seeds[6], part), 71), part),
        "values": scatter_about(part_splits[2], (FRAMES, FTOK, HF), 1.0, 6.0, ((0, 4), (2, 2))),
        "out_grad": bell_draw_with(part_splits[3], (FRAMES, FTOK, D), 1.0, 6.0, ((0, 4), (2, 2)), (0, 2, 4, 2.0)),
        "out_weight": scatter_about(seeds[4], (D, HF), HF ** -0.5, 0.109375, ((0, 4), (1, 2))),
        "lists": draw_lists(jax.random.fold_in(jax.random.fold_in(seeds[6], part), 71), part),
    }


def rounded(array):
    return lax.optimization_barrier(array.astype(jnp.bfloat16)).astype(jnp.float32)


def group_backward(query_rows, own_keys, own_values, far_keys, far_values, grad_rows):
    factor = HD ** -0.5
    key_set = jnp.concatenate([own_keys, far_keys], axis=0).astype(jnp.float32)
    value_set = jnp.concatenate([own_values, far_values], axis=0).astype(jnp.float32)
    query_set = query_rows.astype(jnp.float32)
    grad_set = grad_rows.astype(jnp.float32)
    scores = jnp.einsum("qhd,khd->hqk", query_set, key_set) * factor
    row_top = jnp.max(scores, axis=2, keepdims=True)
    weighted = jnp.exp(scores - row_top)
    prob = weighted / jnp.sum(weighted, axis=2, keepdims=True)
    prob_low = rounded(prob)
    attn_out = rounded(jnp.einsum("hqk,khd->qhd", prob_low, value_set))
    row_dot = jnp.sum(grad_set * attn_out, axis=2)
    prob_grad = jnp.einsum("qhd,khd->hqk", grad_set, value_set)
    score_grad = rounded(prob * (prob_grad - jnp.transpose(row_dot)[:, :, None]))
    query_grad = (jnp.einsum("hqk,khd->qhd", score_grad, key_set) * factor).astype(jnp.bfloat16)
    key_term = jnp.einsum("hqk,qhd->khd", score_grad, query_set) * factor
    value_term = jnp.einsum("hqk,qhd->khd", prob_low, grad_set)
    return attn_out.astype(jnp.bfloat16), query_grad, key_term, value_term


def reference(queries, keys, values, out_grad, out_weight, lists):
    group_rows = CF * FTOK
    grad_flat = out_grad.reshape(FRAMES * FTOK, D)
    attn_grad = jnp.dot(grad_flat, out_weight, preferred_element_type=jnp.float32).astype(jnp.bfloat16)
    attn_grad = attn_grad.reshape(FRAMES, FTOK, HF)

    def one_group(group_inputs):
        group_id, picks = group_inputs
        first_frame = (group_id * CF).astype(jnp.int32)
        own_q = lax.dynamic_slice_in_dim(queries, first_frame, CF, 0).reshape(group_rows, HEADS, HD)
        own_k = lax.dynamic_slice_in_dim(keys, first_frame, CF, 0).reshape(group_rows, HEADS, HD)
        own_v = lax.dynamic_slice_in_dim(values, first_frame, CF, 0).reshape(group_rows, HEADS, HD)
        own_g = lax.dynamic_slice_in_dim(attn_grad, first_frame, CF, 0).reshape(group_rows, HEADS, HD)
        far_k = jnp.take(keys, picks.astype(jnp.int32), axis=0).reshape(RET * FTOK, HEADS, HD)
        far_v = jnp.take(values, picks.astype(jnp.int32), axis=0).reshape(RET * FTOK, HEADS, HD)
        return group_backward(own_q, own_k, own_v, far_k, far_v, own_g)

    attn_all, query_grad, key_term, value_term = lax.map(one_group, (jnp.arange(GROUPS, dtype=jnp.int32), lists))
    entry_count = GROUPS_DEV * RET
    wanted = lists.reshape(N_TM, entry_count).astype(jnp.int32)
    same_frame = wanted[:, :, None] == wanted[:, None, :]
    position = jnp.arange(entry_count, dtype=jnp.int32)
    before = position[:, None] < position[None, :]
    first_seen = jnp.logical_not(jnp.any(same_frame & before[None], axis=1))
    same_float = same_frame.astype(jnp.float32)

    def gathered(terms):
        own_part = terms[:, :group_rows].reshape(FRAMES, FTOK * HF)
        far_part = terms[:, group_rows:].reshape(N_TM, entry_count, FTOK * HF)
        summed = jnp.einsum("rij,rjx->rix", same_float, far_part, precision=lax.Precision.HIGHEST)
        kept = jnp.where(first_seen[:, :, None], rounded(summed), jnp.zeros_like(summed))
        total = jnp.zeros((FRAMES, FTOK * HF), jnp.float32).at[wanted.reshape(-1)].add(kept.reshape(-1, FTOK * HF))
        return (own_part + total).astype(jnp.bfloat16).reshape(FRAMES, FTOK, HF)

    key_grad = gathered(key_term)
    value_grad = gathered(value_term)
    attn_shards = attn_all.reshape(N_TM, FR_DEV * FTOK, HF)
    grad_shards = grad_flat.reshape(N_TM, FR_DEV * FTOK, D)

    def add_shard(running, shard_pair):
        grad_rows, attn_rows = shard_pair
        term = lax.dot_general(grad_rows, attn_rows, (((0,), (0,)), ((), ())), preferred_element_type=jnp.float32)
        return running + rounded(term), None

    weight_grad, unused = lax.scan(add_shard, jnp.zeros((D, HF), jnp.float32), (grad_shards, attn_shards))
    return query_grad.reshape(FRAMES, FTOK, HF), key_grad, value_grad, weight_grad
```

```python
import functools

import jax
import jax.numpy as jnp
from jax import lax
from jax.experimental import pallas as pl
from jax.experimental.pallas import tpu as pltpu
from jax.sharding import PartitionSpec as P

HD = 128
CF = 4
RET = 8


def slot_tables(owners, local_frame, slot_index, occupied, myself, capacity):
    slot_range = jnp.arange(capacity, dtype=jnp.int32)
    matches = (
        occupied[:, None, :]
        & (owners[:, None, :] == myself)
        & (slot_index[:, None, :] == slot_range[None, :, None])
    )
    source = jnp.sum(jnp.where(matches, local_frame[:, None, :], 0), axis=2)
    filled = jnp.any(matches, axis=2)
    return (source.reshape(-1), filled.reshape(-1))


def pack_slots(frame_rows, source, filled):
    picked = jnp.take(frame_rows, source, axis=0)
    return jnp.where(filled[:, None, None], picked, jnp.zeros_like(picked))


def per_device(queries, keys, values, out_grad, out_weight, lists):
    frames_dev, frame_tokens, width = queries.shape
    heads_dev = width // HD
    tm_count = lax.axis_size("tm")
    myself = lax.axis_index("tm")
    groups_dev = frames_dev // CF
    entry_count = groups_dev * RET
    token_rows = frames_dev * frame_tokens
    group_rows = CF * frame_tokens
    score_factor = HD ** (-0.5)
    per_owner = max(1, RET // tm_count)
    every_list = lax.all_gather(lists, "tm", axis=0, tiled=True)
    wanted = every_list.reshape(tm_count, entry_count)
    owners = wanted // frames_dev
    local_frame = wanted - owners * frames_dev
    position = jnp.arange(entry_count, dtype=jnp.int32)
    before = (position[:, None] < position[None, :])[None]
    same_owner = owners[:, :, None] == owners[:, None, :]
    same_frame = wanted[:, :, None] == wanted[:, None, :]
    first_seen = jnp.logical_not(jnp.any(same_frame & before, axis=1))
    entry_slot = jnp.sum(same_owner & before, axis=1)
    frame_first = jnp.sum(same_owner & before & first_seen[:, :, None], axis=1)
    frame_slot = jnp.sum(
        jnp.where(same_frame & first_seen[:, :, None], frame_first[:, :, None], 0), axis=1
    )
    my_owner = lax.dynamic_index_in_dim(owners, myself, 0, keepdims=False)
    my_entry_slot = lax.dynamic_index_in_dim(entry_slot, myself, 0, keepdims=False)
    my_frame_slot = lax.dynamic_index_in_dim(frame_slot, myself, 0, keepdims=False)
    frame_source, frame_filled = slot_tables(
        owners, local_frame, frame_slot, first_seen, myself, per_owner
    )
    capacity = groups_dev * per_owner
    source, filled = slot_tables(
        owners, local_frame, entry_slot, jnp.ones_like(first_seen), myself, capacity
    )
    got_keys, got_values = (
        lax.all_to_all(
            pack_slots(keys, source, filled), "tm", split_axis=0, concat_axis=0, tiled=True
        ),
        lax.all_to_all(
            pack_slots(values, source, filled), "tm", split_axis=0, concat_axis=0, tiled=True
        ),
    )
    lookup = my_owner * capacity + my_entry_slot
    grad_full = lax.all_gather(out_grad, "head", axis=2, tiled=True)
    grad_rows = grad_full.reshape(token_rows, grad_full.shape[2])
    columns = grad_rows
    attn_grad = jnp.dot(
        columns,
        lax.all_gather(out_weight, "tm", axis=0, tiled=True),
        preferred_element_type=jnp.float32,
    ).astype(jnp.bfloat16)
    far_keys = jnp.take(got_keys, lookup, axis=0)
    far_values = jnp.take(got_values, lookup, axis=0)
    far_span = RET * frame_tokens
    query_blocks = queries.reshape(groups_dev, group_rows, heads_dev, HD)
    key_set = jnp.concatenate(
        [
            keys.reshape(groups_dev, group_rows, heads_dev, HD),
            far_keys.reshape(groups_dev, far_span, heads_dev, HD),
        ],
        axis=1,
    )
    value_set = jnp.concatenate(
        [
            values.reshape(groups_dev, group_rows, heads_dev, HD),
            far_values.reshape(groups_dev, far_span, heads_dev, HD),
        ],
        axis=1,
    )
    scores = (
        jnp.einsum("cqhd,ckhd->chqk", query_blocks, key_set, preferred_element_type=jnp.float32)
        * score_factor
    )
    row_top = jnp.max(scores, axis=3, keepdims=True)
    weighted = jnp.exp(scores - row_top)
    prob = weighted / jnp.sum(weighted, axis=3, keepdims=True)
    prob_low = prob.astype(jnp.bfloat16)
    attn_out = jnp.einsum(
        "chqk,ckhd->cqhd", prob_low, value_set, preferred_element_type=jnp.float32
    ).astype(jnp.bfloat16)
    grad_blocks = attn_grad.reshape(groups_dev, group_rows, heads_dev, HD)
    row_dot = jnp.sum(grad_blocks.astype(jnp.float32) * attn_out.astype(jnp.float32), axis=3)
    row_dot = jnp.transpose(row_dot, (0, 2, 1))[..., None]
    prob_grad = jnp.einsum(
        "cqhd,ckhd->chqk", grad_blocks, value_set, preferred_element_type=jnp.float32
    )
    score_grad = (prob * (prob_grad - row_dot)).astype(jnp.bfloat16)
    query_grad = (
        jnp.einsum("chqk,ckhd->cqhd", score_grad, key_set, preferred_element_type=jnp.float32)
        * score_factor
    ).astype(jnp.bfloat16)
    key_term = (
        jnp.einsum("chqk,cqhd->ckhd", score_grad, query_blocks, preferred_element_type=jnp.float32)
        * score_factor
    )
    value_term = jnp.einsum(
        "chqk,cqhd->ckhd", prob_low, grad_blocks, preferred_element_type=jnp.float32
    )
    own_dk = key_term[:, :group_rows].reshape(frames_dev, frame_tokens, width)
    own_dv = value_term[:, :group_rows].reshape(frames_dev, frame_tokens, width)
    far_dk = key_term[:, group_rows:].reshape(entry_count, frame_tokens, width)
    far_dv = value_term[:, group_rows:].reshape(entry_count, frame_tokens, width)
    back_slot = my_owner * per_owner + my_frame_slot
    empty = jnp.zeros((tm_count * per_owner, frame_tokens, width), jnp.float32)
    back_keys = empty.at[back_slot].add(far_dk).astype(jnp.bfloat16)
    back_values = empty.at[back_slot].add(far_dv).astype(jnp.bfloat16)
    came_keys, came_values = (
        lax.all_to_all(back_keys, "tm", split_axis=0, concat_axis=0, tiled=True),
        lax.all_to_all(back_values, "tm", split_axis=0, concat_axis=0, tiled=True),
    )
    selector = (
        (frame_source[None, :] == jnp.arange(frames_dev, dtype=jnp.int32)[:, None])
        & frame_filled[None, :]
    ).astype(jnp.bfloat16)
    into_keys = jnp.dot(
        selector, came_keys.reshape(tm_count * per_owner, -1), preferred_element_type=jnp.float32
    )
    into_values = jnp.dot(
        selector, came_values.reshape(tm_count * per_owner, -1), preferred_element_type=jnp.float32
    )
    key_grad = (own_dk + into_keys.reshape(frames_dev, frame_tokens, width)).astype(jnp.bfloat16)
    value_grad = (own_dv + into_values.reshape(frames_dev, frame_tokens, width)).astype(
        jnp.bfloat16
    )
    attn_rows = attn_out.reshape(token_rows, width)
    columns = grad_rows
    weight_grad = lax.psum_scatter(
        lax.dot_general(
            columns, attn_rows, (((0,), (0,)), ((), ())), preferred_element_type=jnp.float32
        ).astype(jnp.bfloat16),
        "tm",
        scatter_dimension=0,
        tiled=True,
    ).astype(jnp.float32)
    return (query_grad.reshape(frames_dev, frame_tokens, width), key_grad, value_grad, weight_grad)


SELF, MATE, PARTNER, DIAG = 0, 1, 2, 3
F32 = jnp.float32
BF16 = jnp.bfloat16
NT = (((1,), (1,)), ((), ()))
TN = (((0,), (0,)), ((), ()))


def dot(a, b):
    return jnp.dot(a, b, preferred_element_type=F32)


def dotx(a, b, dims):
    return lax.dot_general(a, b, dims, preferred_element_type=F32)


def fused_kernel(
    slots, q_ref, k_ref, v_ref, og_ref, w_ref, lists_ref,
    dq_ref, dk_ref, dv_ref, dw_ref,
    every_list, present, pick, send_k, send_v, far_k, far_v, og_halves, columns, columns_t,
    part_a, part_b, mate_out, mate_in, pair_out, pair_in, grad, attn, prob,
    own_k, own_v, back_k, back_v, came_k, came_v, send_sem, recv_sem,
):
    rows, width = q_ref.shape
    heads = width // HD
    entries = lists_ref.shape[0]
    frame_tokens = 32
    group_rows = CF * frame_tokens
    groups = rows // group_rows
    far_rows = slots * frame_tokens
    depth = w_ref.shape[0]
    scale = HD ** (-0.5)
    t = lax.axis_index("tm")
    h = lax.axis_index("head")
    mate = t + 1 - 2 * (t % 2)
    partner = (t + 2) % 4
    diag = (mate + 2) % 4
    peers = (t, mate, partner, diag)

    barrier = pltpu.get_barrier_semaphore()
    for kind in (MATE, PARTNER, DIAG):
        pl.semaphore_signal(barrier, inc=1, device_id={"tm": peers[kind]})
    pl.semaphore_signal(barrier, inc=1, device_id={"head": 1 - h})
    pl.semaphore_wait(barrier, 4)

    started = []

    def send(src, dst, target):
        number = len(started)
        copy = pltpu.make_async_remote_copy(
            src_ref=src, dst_ref=dst, send_sem=send_sem.at[number], recv_sem=recv_sem.at[number],
            device_id=target,
        )
        copy.start()
        started.append(copy)
        return copy

    def to(kind):
        return {"tm": peers[kind]}

    lists_in = [
        send(lists_ref, every_list.at[kind], to(kind)) for kind in (PARTNER, DIAG, MATE)
    ]
    halves_in = []
    for part in range(2):
        og_halves[h, part] = og_ref[:, part * depth : (part + 1) * depth]
    for part in range(2):
        halves_in.append(
            send(og_halves.at[h, part], og_halves.at[h, part], {"head": 1 - h})
        )
    every_list[SELF] = lists_ref[...]
    for copy in lists_in:
        copy.wait_recv()

    lanes = lax.broadcasted_iota(jnp.int32, (entries, rows), 1)
    my_frame = t * (rows // frame_tokens) + lax.shift_right_logical(lanes, 5)
    for kind in range(4):
        named = jnp.max((every_list[kind] == my_frame).astype(F32), axis=0, keepdims=True)
        present[kind * frame_tokens : (kind + 1) * frame_tokens, :] = jnp.broadcast_to(
            named, (frame_tokens, rows)
        ).astype(BF16)
    above = lax.broadcasted_iota(jnp.int32, (rows, rows), 0)
    below = lax.broadcasted_iota(jnp.int32, (rows, rows), 1)
    earlier = (
        ((above & 31) == 0)
        & (lax.shift_right_logical(above, 5) < lax.shift_right_logical(below, 5))
    ).astype(F32).astype(BF16)
    rank = dot(present[...], earlier)
    token = lax.broadcasted_iota(jnp.int32, (frame_tokens, rows), 0)
    column_token = lax.broadcasted_iota(jnp.int32, (frame_tokens, rows), 1) & 31
    same_token = (token == column_token).astype(F32)
    for kind in range(4):
        span = slice(kind * frame_tokens, (kind + 1) * frame_tokens)
        here = present[span, :].astype(F32) * same_token
        for slot in range(slots):
            first = (kind * slots + slot) * frame_tokens
            pick[first : first + frame_tokens, :] = (
                here * (rank[span, :] == slot).astype(F32)
            ).astype(BF16)

    tile = 512

    def tiled(body):
        def step(i, carry):
            body(pl.ds(pl.multiple_of(i * tile, tile), tile))
            return carry

        lax.fori_loop(0, width // tile, step, 0)

    def span_of(kind):
        return pl.ds(kind * far_rows, far_rows)

    def pick_keys(cols):
        send_k[:, cols] = dot(pick[...], k_ref[:, cols]).astype(BF16)

    def pick_values(cols):
        send_v[:, cols] = dot(pick[...], v_ref[:, cols]).astype(BF16)

    frames_in = []
    tiled(pick_keys)
    for kind in (PARTNER, DIAG, MATE):
        frames_in.append(send(send_k.at[span_of(kind)], far_k.at[span_of(kind)], to(kind)))
    tiled(pick_values)
    for kind in (PARTNER, DIAG, MATE):
        frames_in.append(send(send_v.at[span_of(kind)], far_v.at[span_of(kind)], to(kind)))
    far_k[0:far_rows, :] = send_k[0:far_rows, :]
    far_v[0:far_rows, :] = send_v[0:far_rows, :]

    for copy in halves_in:
        copy.wait_recv()
    columns_in = {}
    for kind in (PARTNER, DIAG, MATE):
        peer = peers[kind]
        columns_in[kind] = send(
            og_halves.at[peer // 2, peer % 2], columns.at[pl.ds(kind * rows, rows)], to(kind)
        )
    columns[0:rows, :] = og_halves[t // 2, t % 2]

    for copy in frames_in:
        copy.wait_recv()

    def forward(i, carry):
        cols = pl.ds(pl.multiple_of(i * HD, HD), HD)
        fk = far_k[:, cols]
        fv = far_v[:, cols]
        for g in range(groups):
            span = slice(g * group_rows, (g + 1) * group_rows)
            q = q_ref[span, cols]
            near = dotx(q, k_ref[span, cols], NT) * scale
            far = dotx(q, fk, NT) * scale
            top = jnp.maximum(
                jnp.max(near, axis=1, keepdims=True), jnp.max(far, axis=1, keepdims=True)
            )
            near = jnp.exp(near - top)
            far = jnp.exp(far - top)
            total = jnp.sum(near, axis=1, keepdims=True) + jnp.sum(far, axis=1, keepdims=True)
            near = near / total
            far = far / total
            prob[i, span, 0:group_rows] = near
            prob[i, span, group_rows:] = far
            out = dot(near.astype(BF16), v_ref[span, cols]) + dot(far.astype(BF16), fv)
            attn[span, cols] = out.astype(BF16)
        return carry

    lax.fori_loop(0, heads, forward, 0)
    own = attn.at[pl.ds(0, rows)]
    attn_partner = send(own, attn.at[pl.ds(PARTNER * rows, rows)], to(PARTNER))
    attn_mate = send(own, attn.at[pl.ds(MATE * rows, rows)], to(MATE))

    def block(kind):
        return slice(kind * rows, (kind + 1) * rows)

    columns_in[DIAG].wait_recv()

    def diag_part(cols):
        mate_out[1, :, cols] = dot(columns[block(DIAG), :], w_ref[:, cols]).astype(BF16)

    tiled(diag_part)
    diag_in = send(mate_out.at[1], mate_in.at[1], to(MATE))
    columns_in[PARTNER].wait_recv()

    def partner_part(cols):
        part_b[:, cols] = dot(columns[block(PARTNER), :], w_ref[:, cols])

    tiled(partner_part)
    diag_in.wait_recv()

    def pair_sum(cols):
        pair_out[:, cols] = (part_b[:, cols] + mate_in[1, :, cols].astype(F32)).astype(BF16)

    tiled(pair_sum)
    pair = send(pair_out, pair_in, to(PARTNER))
    columns_in[MATE].wait_recv()

    def mate_part(cols):
        mate_out[0, :, cols] = dot(columns[block(MATE), :], w_ref[:, cols]).astype(BF16)

    tiled(mate_part)
    mate_sum = send(mate_out.at[0], mate_in.at[0], to(MATE))

    def own_part(cols):
        part_a[:, cols] = dot(columns[block(SELF), :], w_ref[:, cols])

    tiled(own_part)
    attn_partner.wait_recv()
    held = attn.at[pl.ds(PARTNER * rows, rows)]
    attn_diag = send(held, attn.at[pl.ds(DIAG * rows, rows)], to(MATE))
    for kind in range(4):
        columns_t[:, block(kind)] = columns[block(kind), :].T
    mate_sum.wait_recv()
    pair.wait_recv()

    def total_part(cols):
        grad[:, cols] = (
            part_a[:, cols] + mate_in[0, :, cols].astype(F32) + pair_in[:, cols].astype(F32)
        ).astype(BF16)

    tiled(total_part)

    def backward(i, carry):
        cols = pl.ds(pl.multiple_of(i * HD, HD), HD)
        fk = far_k[:, cols]
        fv = far_v[:, cols]
        far_dk = None
        far_dv = None
        for g in range(groups):
            span = slice(g * group_rows, (g + 1) * group_rows)
            q = q_ref[span, cols]
            do = grad[span, cols]
            row_dot = jnp.sum(
                do.astype(F32) * attn[span, cols].astype(F32), axis=1, keepdims=True
            )
            near = prob[i, span, 0:group_rows]
            far = prob[i, span, group_rows:]
            near_ds = (near * (dotx(do, v_ref[span, cols], NT) - row_dot)).astype(BF16)
            far_ds = (far * (dotx(do, fv, NT) - row_dot)).astype(BF16)
            near_p = near.astype(BF16)
            far_p = far.astype(BF16)
            dq_ref[span, cols] = (
                (dot(near_ds, k_ref[span, cols]) + dot(far_ds, fk)) * scale
            ).astype(BF16)
            own_k[span, cols] = dotx(near_ds, q, TN) * scale
            own_v[span, cols] = dotx(near_p, do, TN)
            more_k = dotx(far_ds, q, TN)
            more_v = dotx(far_p, do, TN)
            far_dk = more_k if g == 0 else far_dk + more_k
            far_dv = more_v if g == 0 else far_dv + more_v
        back_k[:, cols] = (far_dk * scale).astype(BF16)
        back_v[:, cols] = far_dv.astype(BF16)
        return carry

    returned = []
    chunks = 2
    for chunk in range(chunks):
        each = heads // chunks
        lax.fori_loop(chunk * each, (chunk + 1) * each, backward, 0)
        cols = pl.ds(chunk * each * HD, each * HD)
        for kind in (PARTNER, DIAG, MATE):
            for out, into in ((back_k, came_k), (back_v, came_v)):
                returned.append(
                    send(out.at[span_of(kind), cols], into.at[span_of(kind), cols], to(kind))
                )
    came_k[0:far_rows, :] = back_k[0:far_rows, :]
    came_v[0:far_rows, :] = back_v[0:far_rows, :]
    attn_mate.wait_recv()
    attn_diag.wait_recv()

    def weight_part(cols):
        dw_ref[:, cols] = dot(columns_t[...], attn[:, cols])

    tiled(weight_part)
    for copy in returned:
        copy.wait_recv()

    def add_returned(cols):
        dk_ref[:, cols] = (own_k[:, cols] + dotx(pick[...], came_k[:, cols], TN)).astype(BF16)
        dv_ref[:, cols] = (own_v[:, cols] + dotx(pick[...], came_v[:, cols], TN)).astype(BF16)

    tiled(add_returned)
    for copy in started:
        copy.wait_send()


def fused(queries, keys, values, out_grad, out_weight, lists):
    frames, frame_tokens, width = queries.shape
    rows = frames * frame_tokens
    depth = out_weight.shape[0]
    slots = RET // 4
    heads = width // HD
    flat = [x.reshape(rows, width) for x in (queries, keys, values, out_grad)]
    spread = jnp.broadcast_to(lists.reshape(-1, 1), (lists.size, rows))
    vmem = pl.BlockSpec(memory_space=pltpu.VMEM)
    far = 4 * slots * frame_tokens

    def low(*shape):
        return pltpu.VMEM(shape, BF16)

    def wide(*shape):
        return pltpu.VMEM(shape, F32)

    dq, dk, dv, dw = pl.pallas_call(
        functools.partial(fused_kernel, slots),
        out_shape=[jax.ShapeDtypeStruct((rows, width), BF16)] * 3
        + [jax.ShapeDtypeStruct((depth, width), F32)],
        in_specs=[vmem] * 6,
        out_specs=[vmem] * 4,
        scratch_shapes=[
            pltpu.VMEM((4, lists.size, rows), jnp.int32),
            low(4 * frame_tokens, rows),
            low(far, rows),
            low(far, width),
            low(far, width),
            low(far, width),
            low(far, width),
            low(2, 2, rows, depth),
            low(4 * rows, depth),
            low(depth, 4 * rows),
            wide(rows, width),
            wide(rows, width),
            low(2, rows, width),
            low(2, rows, width),
            low(rows, width),
            low(rows, width),
            low(rows, width),
            low(4 * rows, width),
            wide(heads, rows, CF * frame_tokens + far),
            wide(rows, width),
            wide(rows, width),
            low(far, width),
            low(far, width),
            low(far, width),
            low(far, width),
            pltpu.SemaphoreType.DMA((48,)),
            pltpu.SemaphoreType.DMA((48,)),
        ],
        compiler_params=pltpu.CompilerParams(
            collective_id=0, has_side_effects=True, vmem_limit_bytes=60 * 1024 * 1024
        ),
        cost_estimate=pl.CostEstimate(
            flops=7 * 10**9, bytes_accessed=16 * 10**6, transcendentals=10**6
        ),
    )(*flat, out_weight, spread)
    back = [x.reshape(frames, frame_tokens, width) for x in (dq, dk, dv)]
    return (*back, dw)


def solution(mesh):
    whole_fits = mesh.shape["tm"] == 4 and mesh.shape["head"] == 2
    return jax.shard_map(
        fused if whole_fits else per_device,
        mesh=mesh,
        in_specs=(
            P(("dp", "tm"), None, "head"),
            P(("dp", "tm"), None, "head"),
            P(("dp", "tm"), None, "head"),
            P(("dp", "tm"), None, "head"),
            P("tm", "head"),
            P(("dp", "tm"), None),
        ),
        out_specs=(
            P(("dp", "tm"), None, "head"),
            P(("dp", "tm"), None, "head"),
            P(("dp", "tm"), None, "head"),
            P(("dp", "tm"), "head"),
        ),
        check_vma=False,
    )
```

```python
import functools

import jax
import jax.numpy as jnp
from jax import lax
from jax.experimental import pallas as pl
from jax.experimental.pallas import tpu as pltpu
from jax.sharding import PartitionSpec as P

HD = 128
CF = 4
RET = 8


def slot_tables(owners, local_frame, slot_index, occupied, myself, capacity):
    slot_range = jnp.arange(capacity, dtype=jnp.int32)
    matches = (
        occupied[:, None, :]
        & (owners[:, None, :] == myself)
        & (slot_index[:, None, :] == slot_range[None, :, None])
    )
    source = jnp.sum(jnp.where(matches, local_frame[:, None, :], 0), axis=2)
    filled = jnp.any(matches, axis=2)
    return (source.reshape(-1), filled.reshape(-1))


def pack_slots(frame_rows, source, filled):
    picked = jnp.take(frame_rows, source, axis=0)
    return jnp.where(filled[:, None, None], picked, jnp.zeros_like(picked))


def per_device(queries, keys, values, out_grad, out_weight, lists):
    frames_dev, frame_tokens, width = queries.shape
    heads_dev = width // HD
    tm_count = lax.axis_size("tm")
    myself = lax.axis_index("tm")
    groups_dev = frames_dev // CF
    entry_count = groups_dev * RET
    token_rows = frames_dev * frame_tokens
    group_rows = CF * frame_tokens
    score_factor = HD ** (-0.5)
    per_owner = max(1, RET // tm_count)
    every_list = lax.all_gather(lists, "tm", axis=0, tiled=True)
    wanted = every_list.reshape(tm_count, entry_count)
    owners = wanted // frames_dev
    local_frame = wanted - owners * frames_dev
    position = jnp.arange(entry_count, dtype=jnp.int32)
    before = (position[:, None] < position[None, :])[None]
    same_owner = owners[:, :, None] == owners[:, None, :]
    same_frame = wanted[:, :, None] == wanted[:, None, :]
    first_seen = jnp.logical_not(jnp.any(same_frame & before, axis=1))
    entry_slot = jnp.sum(same_owner & before, axis=1)
    frame_first = jnp.sum(same_owner & before & first_seen[:, :, None], axis=1)
    frame_slot = jnp.sum(
        jnp.where(same_frame & first_seen[:, :, None], frame_first[:, :, None], 0), axis=1
    )
    my_owner = lax.dynamic_index_in_dim(owners, myself, 0, keepdims=False)
    my_entry_slot = lax.dynamic_index_in_dim(entry_slot, myself, 0, keepdims=False)
    my_frame_slot = lax.dynamic_index_in_dim(frame_slot, myself, 0, keepdims=False)
    frame_source, frame_filled = slot_tables(
        owners, local_frame, frame_slot, first_seen, myself, per_owner
    )
    capacity = groups_dev * per_owner
    source, filled = slot_tables(
        owners, local_frame, entry_slot, jnp.ones_like(first_seen), myself, capacity
    )
    got_keys, got_values = (
        lax.all_to_all(
            pack_slots(keys, source, filled), "tm", split_axis=0, concat_axis=0, tiled=True
        ),
        lax.all_to_all(
            pack_slots(values, source, filled), "tm", split_axis=0, concat_axis=0, tiled=True
        ),
    )
    lookup = my_owner * capacity + my_entry_slot
    grad_full = lax.all_gather(out_grad, "head", axis=2, tiled=True)
    grad_rows = grad_full.reshape(token_rows, grad_full.shape[2])
    columns = grad_rows
    attn_grad = jnp.dot(
        columns,
        lax.all_gather(out_weight, "tm", axis=0, tiled=True),
        preferred_element_type=jnp.float32,
    ).astype(jnp.bfloat16)
    far_keys = jnp.take(got_keys, lookup, axis=0)
    far_values = jnp.take(got_values, lookup, axis=0)
    far_span = RET * frame_tokens
    query_blocks = queries.reshape(groups_dev, group_rows, heads_dev, HD)
    key_set = jnp.concatenate(
        [
            keys.reshape(groups_dev, group_rows, heads_dev, HD),
            far_keys.reshape(groups_dev, far_span, heads_dev, HD),
        ],
        axis=1,
    )
    value_set = jnp.concatenate(
        [
            values.reshape(groups_dev, group_rows, heads_dev, HD),
            far_values.reshape(groups_dev, far_span, heads_dev, HD),
        ],
        axis=1,
    )
    scores = (
        jnp.einsum("cqhd,ckhd->chqk", query_blocks, key_set, preferred_element_type=jnp.float32)
        * score_factor
    )
    row_top = jnp.max(scores, axis=3, keepdims=True)
    weighted = jnp.exp(scores - row_top)
    prob = weighted / jnp.sum(weighted, axis=3, keepdims=True)
    prob_low = prob.astype(jnp.bfloat16)
    attn_out = jnp.einsum(
        "chqk,ckhd->cqhd", prob_low, value_set, preferred_element_type=jnp.float32
    ).astype(jnp.bfloat16)
    grad_blocks = attn_grad.reshape(groups_dev, group_rows, heads_dev, HD)
    row_dot = jnp.sum(grad_blocks.astype(jnp.float32) * attn_out.astype(jnp.float32), axis=3)
    row_dot = jnp.transpose(row_dot, (0, 2, 1))[..., None]
    prob_grad = jnp.einsum(
        "cqhd,ckhd->chqk", grad_blocks, value_set, preferred_element_type=jnp.float32
    )
    score_grad = (prob * (prob_grad - row_dot)).astype(jnp.bfloat16)
    query_grad = (
        jnp.einsum("chqk,ckhd->cqhd", score_grad, key_set, preferred_element_type=jnp.float32)
        * score_factor
    ).astype(jnp.bfloat16)
    key_term = (
        jnp.einsum("chqk,cqhd->ckhd", score_grad, query_blocks, preferred_element_type=jnp.float32)
        * score_factor
    )
    value_term = jnp.einsum(
        "chqk,cqhd->ckhd", prob_low, grad_blocks, preferred_element_type=jnp.float32
    )
    own_dk = key_term[:, :group_rows].reshape(frames_dev, frame_tokens, width)
    own_dv = value_term[:, :group_rows].reshape(frames_dev, frame_tokens, width)
    far_dk = key_term[:, group_rows:].reshape(entry_count, frame_tokens, width)
    far_dv = value_term[:, group_rows:].reshape(entry_count, frame_tokens, width)
    back_slot = my_owner * per_owner + my_frame_slot
    empty = jnp.zeros((tm_count * per_owner, frame_tokens, width), jnp.float32)
    back_keys = empty.at[back_slot].add(far_dk).astype(jnp.bfloat16)
    back_values = empty.at[back_slot].add(far_dv).astype(jnp.bfloat16)
    came_keys, came_values = (
        lax.all_to_all(back_keys, "tm", split_axis=0, concat_axis=0, tiled=True),
        lax.all_to_all(back_values, "tm", split_axis=0, concat_axis=0, tiled=True),
    )
    selector = (
        (frame_source[None, :] == jnp.arange(frames_dev, dtype=jnp.int32)[:, None])
        & frame_filled[None, :]
    ).astype(jnp.bfloat16)
    into_keys = jnp.dot(
        selector, came_keys.reshape(tm_count * per_owner, -1), preferred_element_type=jnp.float32
    )
    into_values = jnp.dot(
        selector, came_values.reshape(tm_count * per_owner, -1), preferred_element_type=jnp.float32
    )
    key_grad = (own_dk + into_keys.reshape(frames_dev, frame_tokens, width)).astype(jnp.bfloat16)
    value_grad = (own_dv + into_values.reshape(frames_dev, frame_tokens, width)).astype(
        jnp.bfloat16
    )
    attn_rows = attn_out.reshape(token_rows, width)
    columns = grad_rows
    weight_grad = lax.psum_scatter(
        lax.dot_general(
            columns, attn_rows, (((0,), (0,)), ((), ())), preferred_element_type=jnp.float32
        ).astype(jnp.bfloat16),
        "tm",
        scatter_dimension=0,
        tiled=True,
    ).astype(jnp.float32)
    return (query_grad.reshape(frames_dev, frame_tokens, width), key_grad, value_grad, weight_grad)


SELF, MATE, PARTNER, DIAG = 0, 1, 2, 3
F32 = jnp.float32
BF16 = jnp.bfloat16
NT = (((1,), (1,)), ((), ()))
TN = (((0,), (0,)), ((), ()))


def dot(a, b):
    return jnp.dot(a, b, preferred_element_type=F32)


def dotx(a, b, dims):
    return lax.dot_general(a, b, dims, preferred_element_type=F32)


def fused_kernel(
    slots, line, lists_ref, q_ref, k_ref, v_ref, og_ref, w_ref,
    dq_ref, dk_ref, dv_ref, dw_ref,
    my_list, every_list, present, pick, send_k, send_v, far_k, far_v, og_halves, columns,
    columns_t, w_in, grad, attn, prob,
    own_k, own_v, back_k, back_v, came_k, came_v,
    send_sem, recv_sem, up_send, up_recv, down_send, down_recv,
):
    rows, width = q_ref.shape
    heads = width // HD
    entries = my_list.shape[0]
    frame_tokens = 32
    group_rows = CF * frame_tokens
    groups = rows // group_rows
    far_rows = slots * frame_tokens
    depth = w_ref.shape[0]
    chunks = 2
    span_width = width // chunks
    piece = depth // line
    half_rows = rows // 2
    scale = HD ** (-0.5)
    t = lax.axis_index("tm")
    h = lax.axis_index("head")
    z = lax.axis_index("dp")
    mate = t + 1 - 2 * (t % 2)
    partner = (t + 2) % 4
    diag = (mate + 2) % 4
    peers = (t, mate, partner, diag)

    barrier = pltpu.get_barrier_semaphore()
    for kind in (MATE, PARTNER, DIAG):
        pl.semaphore_signal(barrier, inc=1, device_id={"tm": peers[kind]})
    pl.semaphore_signal(barrier, inc=1, device_id={"head": 1 - h})

    for move in (1, line - 1):
        pl.semaphore_signal(barrier, inc=1, device_id={"dp": (z + move) % line})

    for entry in range(entries):
        named = lists_ref[entry // RET, entry % RET]
        my_list[entry : entry + 1, :] = jnp.full((1, rows), named, jnp.int32)
        every_list[SELF, entry : entry + 1, :] = jnp.full((1, rows), named, jnp.int32)
    pl.semaphore_wait(barrier, 6)

    started = []

    def send(src, dst, target):
        number = len(started)
        copy = pltpu.make_async_remote_copy(
            src_ref=src, dst_ref=dst, send_sem=send_sem.at[number], recv_sem=recv_sem.at[number],
            device_id=target,
        )
        copy.start()
        started.append(copy)
        return copy

    def to(kind):
        return {"tm": peers[kind]}

    lists_in = [
        send(my_list, every_list.at[kind], to(kind)) for kind in (PARTNER, DIAG, MATE)
    ]

    def chunk_cols(chunk):
        return pl.ds(chunk * span_width, span_width)

    def piece_rows(index):
        return pl.ds(pl.multiple_of(index * piece, piece), piece)

    crossing = []
    for chunk in range(chunks):
        crossing.append(
            send(
                w_ref.at[piece_rows(z), chunk_cols(chunk)],
                w_in.at[PARTNER, chunk, piece_rows(z)],
                to(PARTNER),
            )
        )
    mate_w = [
        send(w_ref.at[:, chunk_cols(chunk)], w_in.at[MATE, chunk], to(MATE))
        for chunk in range(chunks)
    ]

    def hop(chunk, step, upward):
        move = 1 if upward else -1
        index = z - step if upward else z + step
        index = jnp.clip(index, 0, line - 1)
        held = w_in.at[PARTNER, chunk, piece_rows(index)]
        sends, recvs = (up_send, up_recv) if upward else (down_send, down_recv)
        return pltpu.make_async_remote_copy(
            src_ref=held, dst_ref=held, send_sem=sends.at[chunk, step],
            recv_sem=recvs.at[chunk, step], device_id={"dp": z + move},
        )

    def hop_sent(step, upward):
        if upward:
            return (z - step >= 0) & (z < line - 1)
        return (z + step < line) & (z > 0)

    def hop_received(step, upward):
        if upward:
            return z - 1 - step >= 0
        return z + 1 + step < line

    def hop_wait(chunk, step):
        for upward in (True, False):

            @pl.when(hop_received(step, upward))
            def arrived():
                hop(chunk, step, upward).wait_recv()

    def hop_start(chunk, step):
        if step == 0:
            crossing[chunk].wait_recv()
        else:
            hop_wait(chunk, step - 1)
        for upward in (True, False):

            @pl.when(hop_sent(step, upward))
            def onward():
                hop(chunk, step, upward).start()

    halves_in = []
    for part in range(2):
        og_halves[h, part] = og_ref[:, part * depth : (part + 1) * depth]
    for part in range(2):
        halves_in.append(
            send(og_halves.at[h, part], og_halves.at[h, part], {"head": 1 - h})
        )
    for copy in lists_in:
        copy.wait_recv()

    lanes = lax.broadcasted_iota(jnp.int32, (entries, rows), 1)
    my_frame = t * (rows // frame_tokens) + lax.shift_right_logical(lanes, 5)
    for kind in range(4):
        named = jnp.max((every_list[kind] == my_frame).astype(F32), axis=0, keepdims=True)
        present[kind * frame_tokens : (kind + 1) * frame_tokens, :] = jnp.broadcast_to(
            named, (frame_tokens, rows)
        ).astype(BF16)
    above = lax.broadcasted_iota(jnp.int32, (rows, rows), 0)
    below = lax.broadcasted_iota(jnp.int32, (rows, rows), 1)
    earlier = (
        ((above & 31) == 0)
        & (lax.shift_right_logical(above, 5) < lax.shift_right_logical(below, 5))
    ).astype(F32).astype(BF16)
    rank = dot(present[...], earlier)
    token = lax.broadcasted_iota(jnp.int32, (frame_tokens, rows), 0)
    column_token = lax.broadcasted_iota(jnp.int32, (frame_tokens, rows), 1) & 31
    same_token = (token == column_token).astype(F32)
    for kind in range(4):
        span = slice(kind * frame_tokens, (kind + 1) * frame_tokens)
        here = present[span, :].astype(F32) * same_token
        for slot in range(slots):
            first = (kind * slots + slot) * frame_tokens
            pick[first : first + frame_tokens, :] = (
                here * (rank[span, :] == slot).astype(F32)
            ).astype(BF16)

    tile = 512

    def tiled(body):
        def step(i, carry):
            body(pl.ds(pl.multiple_of(i * tile, tile), tile))
            return carry

        lax.fori_loop(0, width // tile, step, 0)

    def span_of(kind):
        return pl.ds(kind * far_rows, far_rows)

    def pick_keys(cols):
        send_k[:, cols] = dot(pick[...], k_ref[:, cols]).astype(BF16)

    def pick_values(cols):
        send_v[:, cols] = dot(pick[...], v_ref[:, cols]).astype(BF16)

    frames_in = []
    tiled(pick_keys)
    for kind in (PARTNER, DIAG, MATE):
        frames_in.append(send(send_k.at[span_of(kind)], far_k.at[span_of(kind)], to(kind)))
    tiled(pick_values)
    for kind in (PARTNER, DIAG, MATE):
        frames_in.append(send(send_v.at[span_of(kind)], far_v.at[span_of(kind)], to(kind)))
    far_k[0:far_rows, :] = send_k[0:far_rows, :]
    far_v[0:far_rows, :] = send_v[0:far_rows, :]


    hop_start(0, 0)
    hop_start(0, 1)
    for copy in halves_in:
        copy.wait_recv()
    mine = pl.ds(pl.multiple_of(h * half_rows, half_rows), half_rows)
    columns_in = {}
    for kind in (PARTNER, DIAG):
        peer = peers[kind]
        columns_in[kind] = send(
            og_halves.at[peer // 2, peer % 2, mine], columns.at[kind, mine], to(kind)
        )
    columns_in[MATE] = send(og_halves.at[mate // 2, mate % 2], columns.at[MATE], to(MATE))
    columns[SELF] = og_halves[t // 2, t % 2]
    hop_start(0, 2)
    hop_start(1, 0)
    hop_start(1, 1)

    for copy in frames_in:
        copy.wait_recv()

    def forward(i, carry):
        cols = pl.ds(pl.multiple_of(i * HD, HD), HD)
        fk = far_k[:, cols]
        fv = far_v[:, cols]
        for g in range(groups):
            span = slice(g * group_rows, (g + 1) * group_rows)
            q = q_ref[span, cols]
            near = dotx(q, k_ref[span, cols], NT) * scale
            far = dotx(q, fk, NT) * scale
            top = jnp.maximum(
                jnp.max(near, axis=1, keepdims=True), jnp.max(far, axis=1, keepdims=True)
            )
            near = jnp.exp(near - top)
            far = jnp.exp(far - top)
            total = jnp.sum(near, axis=1, keepdims=True) + jnp.sum(far, axis=1, keepdims=True)
            near = near / total
            far = far / total
            prob[i, span, 0:group_rows] = near
            prob[i, span, group_rows:] = far
            out = dot(near.astype(BF16), v_ref[span, cols]) + dot(far.astype(BF16), fv)
            attn[SELF, span, cols] = out.astype(BF16)
        return carry

    each = heads // chunks
    attn_partner = []
    attn_mate = []
    for chunk in range(chunks):
        lax.fori_loop(chunk * each, (chunk + 1) * each, forward, 0)
        own = attn.at[SELF, :, chunk_cols(chunk)]
        attn_mate.append(send(own, attn.at[MATE, :, chunk_cols(chunk)], to(MATE)))
        attn_partner.append(send(own, attn.at[PARTNER, :, chunk_cols(chunk)], to(PARTNER)))
        if chunk == 0:
            hop_start(1, 2)
            hop_wait(0, 2)
            diag_w = [send(w_in.at[PARTNER, 0], w_in.at[DIAG, 0], to(MATE))]
    swapped = []
    for kind in (PARTNER, DIAG):
        columns_in[kind].wait_recv()
        swapped.append(send(columns.at[kind, mine], columns.at[kind, mine], {"head": 1 - h}))

    def backward(i, carry):
        cols = pl.ds(pl.multiple_of(i * HD, HD), HD)
        fk = far_k[:, cols]
        fv = far_v[:, cols]
        far_dk = None
        far_dv = None
        for g in range(groups):
            span = slice(g * group_rows, (g + 1) * group_rows)
            q = q_ref[span, cols]
            do = grad[span, cols]
            row_dot = jnp.sum(
                do.astype(F32) * attn[SELF, span, cols].astype(F32), axis=1, keepdims=True
            )
            near = prob[i, span, 0:group_rows]
            far = prob[i, span, group_rows:]
            near_ds = (near * (dotx(do, v_ref[span, cols], NT) - row_dot)).astype(BF16)
            far_ds = (far * (dotx(do, fv, NT) - row_dot)).astype(BF16)
            near_p = near.astype(BF16)
            far_p = far.astype(BF16)
            dq_ref[span, cols] = (
                (dot(near_ds, k_ref[span, cols]) + dot(far_ds, fk)) * scale
            ).astype(BF16)
            own_k[span, cols] = dotx(near_ds, q, TN) * scale
            own_v[span, cols] = dotx(near_p, do, TN)
            more_k = dotx(far_ds, q, TN)
            more_v = dotx(far_p, do, TN)
            far_dk = more_k if g == 0 else far_dk + more_k
            far_dv = more_v if g == 0 else far_dv + more_v
        back_k[:, cols] = (far_dk * scale).astype(BF16)
        back_v[:, cols] = far_dv.astype(BF16)
        return carry

    returned = []
    step_width = 384
    for chunk in range(chunks):
        if chunk == 1:
            hop_wait(1, 2)
            diag_w.append(send(w_in.at[PARTNER, 1], w_in.at[DIAG, 1], to(MATE)))
        mate_w[chunk].wait_recv()
        diag_w[chunk].wait_recv()

        def project(i, carry):
            local = pl.ds(pl.multiple_of(i * step_width, step_width), step_width)
            there = pl.ds(
                pl.multiple_of(chunk * span_width + i * step_width, step_width), step_width
            )
            total = dot(og_halves[t // 2, t % 2], w_ref[:, there])
            for kind in (MATE, PARTNER, DIAG):
                peer = peers[kind]
                total += dot(og_halves[peer // 2, peer % 2], w_in[kind, chunk, :, local])
            grad[:, there] = total.astype(BF16)
            return carry

        lax.fori_loop(0, span_width // step_width, project, 0)
        lax.fori_loop(chunk * each, (chunk + 1) * each, backward, 0)
        cols = chunk_cols(chunk)
        for kind in (PARTNER, DIAG, MATE):
            for out, into in ((back_k, came_k), (back_v, came_v)):
                returned.append(
                    send(out.at[span_of(kind), cols], into.at[span_of(kind), cols], to(kind))
                )
    came_k[0:far_rows, :] = back_k[0:far_rows, :]
    came_v[0:far_rows, :] = back_v[0:far_rows, :]
    attn_diag = []
    for chunk in range(chunks):
        attn_partner[chunk].wait_recv()
        held = attn.at[PARTNER, :, chunk_cols(chunk)]
        attn_diag.append(send(held, attn.at[DIAG, :, chunk_cols(chunk)], to(MATE)))
    columns_in[MATE].wait_recv()
    for copy in swapped:
        copy.wait_recv()
    for kind in range(4):
        columns_t[kind] = columns[kind].T
    for copy in attn_mate + attn_diag:
        copy.wait_recv()

    def weight_part(cols):
        total = dot(columns_t[SELF], attn[SELF, :, cols])
        for kind in (MATE, PARTNER, DIAG):
            total += dot(columns_t[kind], attn[kind, :, cols])
        dw_ref[:, cols] = total.astype(BF16)

    tiled(weight_part)
    for copy in returned:
        copy.wait_recv()

    def add_returned(cols):
        dk_ref[:, cols] = (own_k[:, cols] + dotx(pick[...], came_k[:, cols], TN)).astype(BF16)
        dv_ref[:, cols] = (own_v[:, cols] + dotx(pick[...], came_v[:, cols], TN)).astype(BF16)

    tiled(add_returned)
    for copy in started:
        copy.wait_send()
    for chunk in range(chunks):
        for step in range(line - 1):
            for upward in (True, False):

                @pl.when(hop_sent(step, upward))
                def left():
                    hop(chunk, step, upward).wait_send()


def finish_kernel(dq_ref, dk_ref, dv_ref, dw_ref, dq_out, dk_out, dv_out, dw_out):
    dq_out[...] = dq_ref[...]
    dk_out[...] = dk_ref[...]
    dv_out[...] = dv_ref[...]
    dw_out[...] = dw_ref[...].astype(F32)


def finish(dq, dk, dv, dw):
    steps = 4
    rows, width = dq.shape
    depth = dw.shape[0]
    small = pl.BlockSpec((rows // steps, width), lambda i: (i, 0))
    large = pl.BlockSpec((depth // steps, width), lambda i: (i, 0))
    return pl.pallas_call(
        finish_kernel,
        grid=(steps,),
        out_shape=[jax.ShapeDtypeStruct((rows, width), BF16)] * 3
        + [jax.ShapeDtypeStruct((depth, width), F32)],
        in_specs=[small, small, small, large],
        out_specs=[small, small, small, large],
        compiler_params=pltpu.CompilerParams(vmem_limit_bytes=32 * 1024 * 1024),
        cost_estimate=pl.CostEstimate(flops=10**6, bytes_accessed=12 * 10**6, transcendentals=0),
    )(dq, dk, dv, dw)


def fused(queries, keys, values, out_grad, out_weight, lists):
    frames, frame_tokens, width = queries.shape
    rows = frames * frame_tokens
    depth = out_weight.shape[0]
    slots = RET // 4
    heads = width // HD
    flat = [x.reshape(rows, width) for x in (queries, keys, values, out_grad)]
    line = lax.axis_size("dp")
    vmem = pl.BlockSpec(memory_space=pltpu.VMEM)
    far = 4 * slots * frame_tokens

    def low(*shape):
        return pltpu.VMEM(shape, BF16)

    def wide(*shape):
        return pltpu.VMEM(shape, F32)

    dq, dk, dv, dw = pl.pallas_call(
        functools.partial(fused_kernel, slots, line),
        out_shape=[jax.ShapeDtypeStruct((rows, width), BF16)] * 3
        + [jax.ShapeDtypeStruct((depth, width), BF16)],
        in_specs=[pl.BlockSpec(memory_space=pltpu.SMEM)] + [vmem] * 5,
        out_specs=[vmem] * 4,
        scratch_shapes=[
            pltpu.VMEM((lists.size, rows), jnp.int32),
            pltpu.VMEM((4, lists.size, rows), jnp.int32),
            low(4 * frame_tokens, rows),
            low(far, rows),
            low(far, width),
            low(far, width),
            low(far, width),
            low(far, width),
            low(2, 2, rows, depth),
            low(4, rows, depth),
            low(4, depth, rows),
            low(4, 2, depth, width // 2),
            low(rows, width),
            low(4, rows, width),
            wide(heads, rows, CF * frame_tokens + far),
            wide(rows, width),
            wide(rows, width),
            low(far, width),
            low(far, width),
            low(far, width),
            low(far, width),
            pltpu.SemaphoreType.DMA((48,)),
            pltpu.SemaphoreType.DMA((48,)),
            pltpu.SemaphoreType.DMA((2, line - 1)),
            pltpu.SemaphoreType.DMA((2, line - 1)),
            pltpu.SemaphoreType.DMA((2, line - 1)),
            pltpu.SemaphoreType.DMA((2, line - 1)),
        ],
        compiler_params=pltpu.CompilerParams(
            collective_id=0, has_side_effects=True, vmem_limit_bytes=60 * 1024 * 1024
        ),
        cost_estimate=pl.CostEstimate(
            flops=7 * 10**9, bytes_accessed=16 * 10**6, transcendentals=10**6
        ),
    )(lists, *flat, out_weight)
    dq, dk, dv, dw = finish(dq, dk, dv, dw)
    back = [x.reshape(frames, frame_tokens, width) for x in (dq, dk, dv)]
    return (*back, dw)


def solution(mesh):
    whole_fits = dict(mesh.shape) == {"dp": 4, "tm": 4, "head": 2}
    return jax.shard_map(
        fused if whole_fits else per_device,
        mesh=mesh,
        in_specs=(
            P(("dp", "tm"), None, "head"),
            P(("dp", "tm"), None, "head"),
            P(("dp", "tm"), None, "head"),
            P(("dp", "tm"), None, "head"),
            P("tm", "head"),
            P(("dp", "tm"), None),
        ),
        out_specs=(
            P(("dp", "tm"), None, "head"),
            P(("dp", "tm"), None, "head"),
            P(("dp", "tm"), None, "head"),
            P(("dp", "tm"), "head"),
        ),
        check_vma=False,
    )
```

```python
import functools

import jax
import jax.numpy as jnp
from jax import lax
from jax.experimental import pallas as pl
from jax.experimental.pallas import tpu as pltpu
from jax.sharding import PartitionSpec as P

HD = 128
CF = 4
RET = 8


def slot_tables(owners, local_frame, slot_index, occupied, myself, capacity):
    slot_range = jnp.arange(capacity, dtype=jnp.int32)
    matches = (
        occupied[:, None, :]
        & (owners[:, None, :] == myself)
        & (slot_index[:, None, :] == slot_range[None, :, None])
    )
    source = jnp.sum(jnp.where(matches, local_frame[:, None, :], 0), axis=2)
    filled = jnp.any(matches, axis=2)
    return (source.reshape(-1), filled.reshape(-1))


def pack_slots(frame_rows, source, filled):
    picked = jnp.take(frame_rows, source, axis=0)
    return jnp.where(filled[:, None, None], picked, jnp.zeros_like(picked))


def per_device(queries, keys, values, out_grad, out_weight, lists):
    frames_dev, frame_tokens, width = queries.shape
    heads_dev = width // HD
    tm_count = lax.axis_size("tm")
    myself = lax.axis_index("tm")
    groups_dev = frames_dev // CF
    entry_count = groups_dev * RET
    token_rows = frames_dev * frame_tokens
    group_rows = CF * frame_tokens
    score_factor = HD ** (-0.5)
    per_owner = max(1, RET // tm_count)
    every_list = lax.all_gather(lists, "tm", axis=0, tiled=True)
    wanted = every_list.reshape(tm_count, entry_count)
    owners = wanted // frames_dev
    local_frame = wanted - owners * frames_dev
    position = jnp.arange(entry_count, dtype=jnp.int32)
    before = (position[:, None] < position[None, :])[None]
    same_owner = owners[:, :, None] == owners[:, None, :]
    same_frame = wanted[:, :, None] == wanted[:, None, :]
    first_seen = jnp.logical_not(jnp.any(same_frame & before, axis=1))
    entry_slot = jnp.sum(same_owner & before, axis=1)
    frame_first = jnp.sum(same_owner & before & first_seen[:, :, None], axis=1)
    frame_slot = jnp.sum(
        jnp.where(same_frame & first_seen[:, :, None], frame_first[:, :, None], 0), axis=1
    )
    my_owner = lax.dynamic_index_in_dim(owners, myself, 0, keepdims=False)
    my_entry_slot = lax.dynamic_index_in_dim(entry_slot, myself, 0, keepdims=False)
    my_frame_slot = lax.dynamic_index_in_dim(frame_slot, myself, 0, keepdims=False)
    frame_source, frame_filled = slot_tables(
        owners, local_frame, frame_slot, first_seen, myself, per_owner
    )
    capacity = groups_dev * per_owner
    source, filled = slot_tables(
        owners, local_frame, entry_slot, jnp.ones_like(first_seen), myself, capacity
    )
    got_keys, got_values = (
        lax.all_to_all(
            pack_slots(keys, source, filled), "tm", split_axis=0, concat_axis=0, tiled=True
        ),
        lax.all_to_all(
            pack_slots(values, source, filled), "tm", split_axis=0, concat_axis=0, tiled=True
        ),
    )
    lookup = my_owner * capacity + my_entry_slot
    grad_full = lax.all_gather(out_grad, "head", axis=2, tiled=True)
    grad_rows = grad_full.reshape(token_rows, grad_full.shape[2])
    columns = grad_rows
    attn_grad = jnp.dot(
        columns,
        lax.all_gather(out_weight, "tm", axis=0, tiled=True),
        preferred_element_type=jnp.float32,
    ).astype(jnp.bfloat16)
    far_keys = jnp.take(got_keys, lookup, axis=0)
    far_values = jnp.take(got_values, lookup, axis=0)
    far_span = RET * frame_tokens
    query_blocks = queries.reshape(groups_dev, group_rows, heads_dev, HD)
    key_set = jnp.concatenate(
        [
            keys.reshape(groups_dev, group_rows, heads_dev, HD),
            far_keys.reshape(groups_dev, far_span, heads_dev, HD),
        ],
        axis=1,
    )
    value_set = jnp.concatenate(
        [
            values.reshape(groups_dev, group_rows, heads_dev, HD),
            far_values.reshape(groups_dev, far_span, heads_dev, HD),
        ],
        axis=1,
    )
    scores = (
        jnp.einsum("cqhd,ckhd->chqk", query_blocks, key_set, preferred_element_type=jnp.float32)
        * score_factor
    )
    row_top = jnp.max(scores, axis=3, keepdims=True)
    weighted = jnp.exp(scores - row_top)
    prob = weighted / jnp.sum(weighted, axis=3, keepdims=True)
    prob_low = prob.astype(jnp.bfloat16)
    attn_out = jnp.einsum(
        "chqk,ckhd->cqhd", prob_low, value_set, preferred_element_type=jnp.float32
    ).astype(jnp.bfloat16)
    grad_blocks = attn_grad.reshape(groups_dev, group_rows, heads_dev, HD)
    row_dot = jnp.sum(grad_blocks.astype(jnp.float32) * attn_out.astype(jnp.float32), axis=3)
    row_dot = jnp.transpose(row_dot, (0, 2, 1))[..., None]
    prob_grad = jnp.einsum(
        "cqhd,ckhd->chqk", grad_blocks, value_set, preferred_element_type=jnp.float32
    )
    score_grad = (prob * (prob_grad - row_dot)).astype(jnp.bfloat16)
    query_grad = (
        jnp.einsum("chqk,ckhd->cqhd", score_grad, key_set, preferred_element_type=jnp.float32)
        * score_factor
    ).astype(jnp.bfloat16)
    key_term = (
        jnp.einsum("chqk,cqhd->ckhd", score_grad, query_blocks, preferred_element_type=jnp.float32)
        * score_factor
    )
    value_term = jnp.einsum(
        "chqk,cqhd->ckhd", prob_low, grad_blocks, preferred_element_type=jnp.float32
    )
    own_dk = key_term[:, :group_rows].reshape(frames_dev, frame_tokens, width)
    own_dv = value_term[:, :group_rows].reshape(frames_dev, frame_tokens, width)
    far_dk = key_term[:, group_rows:].reshape(entry_count, frame_tokens, width)
    far_dv = value_term[:, group_rows:].reshape(entry_count, frame_tokens, width)
    back_slot = my_owner * per_owner + my_frame_slot
    empty = jnp.zeros((tm_count * per_owner, frame_tokens, width), jnp.float32)
    back_keys = empty.at[back_slot].add(far_dk).astype(jnp.bfloat16)
    back_values = empty.at[back_slot].add(far_dv).astype(jnp.bfloat16)
    came_keys, came_values = (
        lax.all_to_all(back_keys, "tm", split_axis=0, concat_axis=0, tiled=True),
        lax.all_to_all(back_values, "tm", split_axis=0, concat_axis=0, tiled=True),
    )
    selector = (
        (frame_source[None, :] == jnp.arange(frames_dev, dtype=jnp.int32)[:, None])
        & frame_filled[None, :]
    ).astype(jnp.bfloat16)
    into_keys = jnp.dot(
        selector, came_keys.reshape(tm_count * per_owner, -1), preferred_element_type=jnp.float32
    )
    into_values = jnp.dot(
        selector, came_values.reshape(tm_count * per_owner, -1), preferred_element_type=jnp.float32
    )
    key_grad = (own_dk + into_keys.reshape(frames_dev, frame_tokens, width)).astype(jnp.bfloat16)
    value_grad = (own_dv + into_values.reshape(frames_dev, frame_tokens, width)).astype(
        jnp.bfloat16
    )
    attn_rows = attn_out.reshape(token_rows, width)
    columns = grad_rows
    weight_grad = lax.psum_scatter(
        lax.dot_general(
            columns, attn_rows, (((0,), (0,)), ((), ())), preferred_element_type=jnp.float32
        ).astype(jnp.bfloat16),
        "tm",
        scatter_dimension=0,
        tiled=True,
    ).astype(jnp.float32)
    return (query_grad.reshape(frames_dev, frame_tokens, width), key_grad, value_grad, weight_grad)


SELF, MATE, PARTNER, DIAG = 0, 1, 2, 3
F32 = jnp.float32
BF16 = jnp.bfloat16
NT = (((1,), (1,)), ((), ()))
TN = (((0,), (0,)), ((), ()))


def dot(a, b):
    return jnp.dot(a, b, preferred_element_type=F32)


def dotx(a, b, dims):
    return lax.dot_general(a, b, dims, preferred_element_type=F32)


def fused_kernel(
    slots, line, lists_ref, q_hbm, k_hbm, v_hbm, og_hbm, w_hbm,
    dq_hbm, dk_hbm, dv_hbm, dw_hbm,
    q_ref, k_ref, v_ref, w_ref, dq_ref, dk_ref, dv_ref, dw_ref,
    my_list, every_list, present, pick, send_k, send_v, far_k, far_v, og_halves, columns,
    columns_t, w_in, grad, attn, prob,
    own_k, own_v, back_k, back_v, came_k, came_v,
    send_sem, recv_sem, up_send, up_recv, down_send, down_recv, load_sem, store_sem,
):
    rows, width = q_ref.shape
    heads = width // HD
    entries = my_list.shape[0]
    frame_tokens = 32
    group_rows = CF * frame_tokens
    groups = rows // group_rows
    far_rows = slots * frame_tokens
    depth = w_ref.shape[0]
    chunks = 2
    span_width = width // chunks
    piece = depth // line
    half_rows = rows // 2
    scale = HD ** (-0.5)
    t = lax.axis_index("tm")
    h = lax.axis_index("head")
    z = lax.axis_index("dp")
    mate = t + 1 - 2 * (t % 2)
    partner = (t + 2) % 4
    diag = (mate + 2) % 4
    peers = (t, mate, partner, diag)

    barrier = pltpu.get_barrier_semaphore()
    for kind in (MATE, PARTNER, DIAG):
        pl.semaphore_signal(barrier, inc=1, device_id={"tm": peers[kind]})
    pl.semaphore_signal(barrier, inc=1, device_id={"head": 1 - h})

    for move in (1, line - 1):
        pl.semaphore_signal(barrier, inc=1, device_id={"dp": (z + move) % line})

    loads = []
    for source, target in (
        (k_hbm, k_ref),
        (v_hbm, v_ref),
        (og_hbm.at[:, pl.ds(0, depth)], og_halves.at[h, 0]),
        (og_hbm.at[:, pl.ds(depth, depth)], og_halves.at[h, 1]),
        (q_hbm, q_ref),
        (w_hbm, w_ref),
    ):
        loads.append(pltpu.make_async_copy(source, target, load_sem.at[len(loads)]))
        loads[-1].start()
    load_k, load_v, load_og0, load_og1, load_q, load_w = loads

    for entry in range(entries):
        named = lists_ref[entry // RET, entry % RET]
        my_list[entry : entry + 1, :] = jnp.full((1, rows), named, jnp.int32)
        every_list[SELF, entry : entry + 1, :] = jnp.full((1, rows), named, jnp.int32)
    pl.semaphore_wait(barrier, 6)

    started = []

    def send(src, dst, target):
        number = len(started)
        copy = pltpu.make_async_remote_copy(
            src_ref=src, dst_ref=dst, send_sem=send_sem.at[number], recv_sem=recv_sem.at[number],
            device_id=target,
        )
        copy.start()
        started.append(copy)
        return copy

    def to(kind):
        return {"tm": peers[kind]}

    lists_in = [
        send(my_list, every_list.at[kind], to(kind)) for kind in (PARTNER, DIAG, MATE)
    ]

    def chunk_cols(chunk):
        return pl.ds(chunk * span_width, span_width)

    def piece_rows(index):
        return pl.ds(pl.multiple_of(index * piece, piece), piece)

    crossing = []
    for chunk in range(chunks):
        crossing.append(
            send(
                w_hbm.at[piece_rows(z), chunk_cols(chunk)],
                w_in.at[PARTNER, chunk, piece_rows(z)],
                to(PARTNER),
            )
        )
    def hop(chunk, step, upward):
        move = 1 if upward else -1
        index = z - step if upward else z + step
        index = jnp.clip(index, 0, line - 1)
        held = w_in.at[PARTNER, chunk, piece_rows(index)]
        sends, recvs = (up_send, up_recv) if upward else (down_send, down_recv)
        return pltpu.make_async_remote_copy(
            src_ref=held, dst_ref=held, send_sem=sends.at[chunk, step],
            recv_sem=recvs.at[chunk, step], device_id={"dp": z + move},
        )

    def hop_sent(step, upward):
        if upward:
            return (z - step >= 0) & (z < line - 1)
        return (z + step < line) & (z > 0)

    def hop_received(step, upward):
        if upward:
            return z - 1 - step >= 0
        return z + 1 + step < line

    def hop_wait(chunk, step):
        for upward in (True, False):

            @pl.when(hop_received(step, upward))
            def arrived():
                hop(chunk, step, upward).wait_recv()

    def hop_start(chunk, step):
        if step == 0:
            crossing[chunk].wait_recv()
        else:
            hop_wait(chunk, step - 1)
        for upward in (True, False):

            @pl.when(hop_sent(step, upward))
            def onward():
                hop(chunk, step, upward).start()

    halves_in = []
    for part in range(2):
        halves_in.append(
            send(
                og_hbm.at[:, pl.ds(part * depth, depth)], og_halves.at[h, part], {"head": 1 - h}
            )
        )
    for copy in lists_in:
        copy.wait_recv()

    lanes = lax.broadcasted_iota(jnp.int32, (entries, rows), 1)
    my_frame = t * (rows // frame_tokens) + lax.shift_right_logical(lanes, 5)
    for kind in range(4):
        named = jnp.max((every_list[kind] == my_frame).astype(F32), axis=0, keepdims=True)
        present[kind * frame_tokens : (kind + 1) * frame_tokens, :] = jnp.broadcast_to(
            named, (frame_tokens, rows)
        ).astype(BF16)
    above = lax.broadcasted_iota(jnp.int32, (rows, rows), 0)
    below = lax.broadcasted_iota(jnp.int32, (rows, rows), 1)
    earlier = (
        ((above & 31) == 0)
        & (lax.shift_right_logical(above, 5) < lax.shift_right_logical(below, 5))
    ).astype(F32).astype(BF16)
    rank = dot(present[...], earlier)
    token = lax.broadcasted_iota(jnp.int32, (frame_tokens, rows), 0)
    column_token = lax.broadcasted_iota(jnp.int32, (frame_tokens, rows), 1) & 31
    same_token = (token == column_token).astype(F32)
    for kind in range(4):
        span = slice(kind * frame_tokens, (kind + 1) * frame_tokens)
        here = present[span, :].astype(F32) * same_token
        for slot in range(slots):
            first = (kind * slots + slot) * frame_tokens
            pick[first : first + frame_tokens, :] = (
                here * (rank[span, :] == slot).astype(F32)
            ).astype(BF16)

    tile = 512

    def tiled(body):
        def step(i, carry):
            body(pl.ds(pl.multiple_of(i * tile, tile), tile))
            return carry

        lax.fori_loop(0, width // tile, step, 0)

    def span_of(kind):
        return pl.ds(kind * far_rows, far_rows)

    def pick_keys(cols):
        send_k[:, cols] = dot(pick[...], k_ref[:, cols]).astype(BF16)

    def pick_values(cols):
        send_v[:, cols] = dot(pick[...], v_ref[:, cols]).astype(BF16)

    frames_in = []
    load_k.wait()
    tiled(pick_keys)
    for kind in (PARTNER, DIAG, MATE):
        frames_in.append(send(send_k.at[span_of(kind)], far_k.at[span_of(kind)], to(kind)))
    load_v.wait()
    tiled(pick_values)
    for kind in (PARTNER, DIAG, MATE):
        frames_in.append(send(send_v.at[span_of(kind)], far_v.at[span_of(kind)], to(kind)))
    far_k[0:far_rows, :] = send_k[0:far_rows, :]
    far_v[0:far_rows, :] = send_v[0:far_rows, :]


    hop_start(0, 0)
    hop_start(0, 1)
    load_og0.wait()
    load_og1.wait()
    for copy in halves_in:
        copy.wait_recv()
    mine = pl.ds(pl.multiple_of(h * half_rows, half_rows), half_rows)
    columns_in = {}
    for kind in (PARTNER, DIAG):
        peer = peers[kind]
        columns_in[kind] = send(
            og_halves.at[peer // 2, peer % 2, mine], columns.at[kind, mine], to(kind)
        )
    columns_in[MATE] = send(og_halves.at[mate // 2, mate % 2], columns.at[MATE], to(MATE))
    columns[SELF] = og_halves[t // 2, t % 2]
    hop_start(0, 2)
    hop_start(1, 0)
    mate_w = [
        send(w_hbm.at[:, chunk_cols(chunk)], w_in.at[MATE, chunk], to(MATE))
        for chunk in range(chunks)
    ]
    hop_start(1, 1)

    load_q.wait()
    for copy in frames_in:
        copy.wait_recv()

    def forward(i, carry):
        cols = pl.ds(pl.multiple_of(i * HD, HD), HD)
        fk = far_k[:, cols]
        fv = far_v[:, cols]
        for g in range(groups):
            span = slice(g * group_rows, (g + 1) * group_rows)
            q = q_ref[span, cols]
            near = dotx(q, k_ref[span, cols], NT) * scale
            far = dotx(q, fk, NT) * scale
            top = jnp.maximum(
                jnp.max(near, axis=1, keepdims=True), jnp.max(far, axis=1, keepdims=True)
            )
            near = jnp.exp(near - top)
            far = jnp.exp(far - top)
            total = jnp.sum(near, axis=1, keepdims=True) + jnp.sum(far, axis=1, keepdims=True)
            near = near / total
            far = far / total
            prob[i, span, 0:group_rows] = near
            prob[i, span, group_rows:] = far
            out = dot(near.astype(BF16), v_ref[span, cols]) + dot(far.astype(BF16), fv)
            attn[SELF, span, cols] = out.astype(BF16)
        return carry

    each = heads // chunks
    attn_partner = []
    attn_mate = []
    for chunk in range(chunks):
        lax.fori_loop(chunk * each, (chunk + 1) * each, forward, 0)
        own = attn.at[SELF, :, chunk_cols(chunk)]
        attn_mate.append(send(own, attn.at[MATE, :, chunk_cols(chunk)], to(MATE)))
        attn_partner.append(send(own, attn.at[PARTNER, :, chunk_cols(chunk)], to(PARTNER)))
        if chunk == 0:
            hop_start(1, 2)
            hop_wait(0, 2)
            diag_w = [send(w_in.at[PARTNER, 0], w_in.at[DIAG, 0], to(MATE))]
    swapped = []
    for kind in (PARTNER, DIAG):
        columns_in[kind].wait_recv()
        swapped.append(send(columns.at[kind, mine], columns.at[kind, mine], {"head": 1 - h}))

    def backward(i, carry):
        cols = pl.ds(pl.multiple_of(i * HD, HD), HD)
        fk = far_k[:, cols]
        fv = far_v[:, cols]
        far_dk = None
        far_dv = None
        for g in range(groups):
            span = slice(g * group_rows, (g + 1) * group_rows)
            q = q_ref[span, cols]
            do = grad[span, cols]
            row_dot = jnp.sum(
                do.astype(F32) * attn[SELF, span, cols].astype(F32), axis=1, keepdims=True
            )
            near = prob[i, span, 0:group_rows]
            far = prob[i, span, group_rows:]
            near_ds = (near * (dotx(do, v_ref[span, cols], NT) - row_dot)).astype(BF16)
            far_ds = (far * (dotx(do, fv, NT) - row_dot)).astype(BF16)
            near_p = near.astype(BF16)
            far_p = far.astype(BF16)
            dq_ref[span, cols] = (
                (dot(near_ds, k_ref[span, cols]) + dot(far_ds, fk)) * scale
            ).astype(BF16)
            own_k[span, cols] = dotx(near_ds, q, TN) * scale
            own_v[span, cols] = dotx(near_p, do, TN)
            more_k = dotx(far_ds, q, TN)
            more_v = dotx(far_p, do, TN)
            far_dk = more_k if g == 0 else far_dk + more_k
            far_dv = more_v if g == 0 else far_dv + more_v
        back_k[:, cols] = (far_dk * scale).astype(BF16)
        back_v[:, cols] = far_dv.astype(BF16)
        return carry

    stores = []

    def store(source, target):
        stores.append(pltpu.make_async_copy(source, target, store_sem.at[len(stores)]))
        stores[-1].start()

    load_w.wait()
    returned = []
    step_width = 384
    for chunk in range(chunks):
        if chunk == 1:
            hop_wait(1, 2)
            diag_w.append(send(w_in.at[PARTNER, 1], w_in.at[DIAG, 1], to(MATE)))
        mate_w[chunk].wait_recv()
        diag_w[chunk].wait_recv()

        def project(i, carry):
            local = pl.ds(pl.multiple_of(i * step_width, step_width), step_width)
            there = pl.ds(
                pl.multiple_of(chunk * span_width + i * step_width, step_width), step_width
            )
            total = dot(og_halves[t // 2, t % 2], w_ref[:, there])
            for kind in (MATE, PARTNER, DIAG):
                peer = peers[kind]
                total += dot(og_halves[peer // 2, peer % 2], w_in[kind, chunk, :, local])
            grad[:, there] = total.astype(BF16)
            return carry

        lax.fori_loop(0, span_width // step_width, project, 0)
        lax.fori_loop(chunk * each, (chunk + 1) * each, backward, 0)
        cols = chunk_cols(chunk)
        for kind in (PARTNER, DIAG, MATE):
            for out, into in ((back_k, came_k), (back_v, came_v)):
                returned.append(
                    send(out.at[span_of(kind), cols], into.at[span_of(kind), cols], to(kind))
                )
        store(dq_ref.at[:, cols], dq_hbm.at[:, cols])
    came_k[0:far_rows, :] = back_k[0:far_rows, :]
    came_v[0:far_rows, :] = back_v[0:far_rows, :]
    attn_diag = []
    for chunk in range(chunks):
        attn_partner[chunk].wait_recv()
        held = attn.at[PARTNER, :, chunk_cols(chunk)]
        attn_diag.append(send(held, attn.at[DIAG, :, chunk_cols(chunk)], to(MATE)))
    columns_in[MATE].wait_recv()
    for copy in swapped:
        copy.wait_recv()
    for kind in range(4):
        columns_t[kind] = columns[kind].T
    for copy in attn_mate + attn_diag:
        copy.wait_recv()

    def weight_part(cols):
        total = dot(columns_t[SELF], attn[SELF, :, cols])
        for kind in (MATE, PARTNER, DIAG):
            total += dot(columns_t[kind], attn[kind, :, cols])
        dw_ref[:, cols] = total.astype(BF16)

    tiled(weight_part)
    store(dw_ref, dw_hbm)

    def add_returned(i, carry):
        cols = pl.ds(pl.multiple_of(i * step_width, step_width), step_width)
        dk_ref[:, cols] = (own_k[:, cols] + dotx(pick[...], came_k[:, cols], TN)).astype(BF16)
        dv_ref[:, cols] = (own_v[:, cols] + dotx(pick[...], came_v[:, cols], TN)).astype(BF16)
        return carry

    per_chunk = len(returned) // chunks
    for chunk in range(chunks):
        for copy in returned[chunk * per_chunk : (chunk + 1) * per_chunk]:
            copy.wait_recv()
        steps = span_width // step_width
        lax.fori_loop(chunk * steps, (chunk + 1) * steps, add_returned, 0)
        cols = chunk_cols(chunk)
        store(dk_ref.at[:, cols], dk_hbm.at[:, cols])
        store(dv_ref.at[:, cols], dv_hbm.at[:, cols])
    for copy in started:
        copy.wait_send()
    for chunk in range(chunks):
        for step in range(line - 1):
            for upward in (True, False):

                @pl.when(hop_sent(step, upward))
                def left():
                    hop(chunk, step, upward).wait_send()

    for copy in stores:
        copy.wait()


def finish_kernel(dq_ref, dk_ref, dv_ref, dw_ref, dq_out, dk_out, dv_out, dw_out):
    dq_out[...] = dq_ref[...]
    dk_out[...] = dk_ref[...]
    dv_out[...] = dv_ref[...]
    dw_out[...] = dw_ref[...].astype(F32)


def finish(dq, dk, dv, dw):
    steps = 4
    rows, width = dq.shape
    depth = dw.shape[0]
    small = pl.BlockSpec((rows // steps, width), lambda i: (i, 0))
    large = pl.BlockSpec((depth // steps, width), lambda i: (i, 0))
    return pl.pallas_call(
        finish_kernel,
        grid=(steps,),
        out_shape=[jax.ShapeDtypeStruct((rows, width), BF16)] * 3
        + [jax.ShapeDtypeStruct((depth, width), F32)],
        in_specs=[small, small, small, large],
        out_specs=[small, small, small, large],
        compiler_params=pltpu.CompilerParams(vmem_limit_bytes=60 * 1024 * 1024),
        cost_estimate=pl.CostEstimate(flops=10**6, bytes_accessed=12 * 10**6, transcendentals=0),
    )(dq, dk, dv, dw)


def fused(queries, keys, values, out_grad, out_weight, lists):
    frames, frame_tokens, width = queries.shape
    rows = frames * frame_tokens
    depth = out_weight.shape[0]
    slots = RET // 4
    heads = width // HD
    flat = [x.reshape(rows, width) for x in (queries, keys, values, out_grad)]
    line = lax.axis_size("dp")
    hbm = pl.BlockSpec(memory_space=pl.ANY)
    far = 4 * slots * frame_tokens

    def low(*shape):
        return pltpu.VMEM(shape, BF16)

    def wide(*shape):
        return pltpu.VMEM(shape, F32)

    dq, dk, dv, dw = pl.pallas_call(
        functools.partial(fused_kernel, slots, line),
        out_shape=[jax.ShapeDtypeStruct((rows, width), BF16)] * 3
        + [jax.ShapeDtypeStruct((depth, width), BF16)],
        in_specs=[pl.BlockSpec(memory_space=pltpu.SMEM)] + [hbm] * 5,
        out_specs=[hbm] * 4,
        scratch_shapes=[
            low(rows, width),
            low(rows, width),
            low(rows, width),
            low(depth, width),
            low(rows, width),
            low(rows, width),
            low(rows, width),
            low(depth, width),
            pltpu.VMEM((lists.size, rows), jnp.int32),
            pltpu.VMEM((4, lists.size, rows), jnp.int32),
            low(4 * frame_tokens, rows),
            low(far, rows),
            low(far, width),
            low(far, width),
            low(far, width),
            low(far, width),
            low(2, 2, rows, depth),
            low(4, rows, depth),
            low(4, depth, rows),
            low(4, 2, depth, width // 2),
            low(rows, width),
            low(4, rows, width),
            wide(heads, rows, CF * frame_tokens + far),
            wide(rows, width),
            wide(rows, width),
            low(far, width),
            low(far, width),
            low(far, width),
            low(far, width),
            pltpu.SemaphoreType.DMA((48,)),
            pltpu.SemaphoreType.DMA((48,)),
            pltpu.SemaphoreType.DMA((2, line - 1)),
            pltpu.SemaphoreType.DMA((2, line - 1)),
            pltpu.SemaphoreType.DMA((2, line - 1)),
            pltpu.SemaphoreType.DMA((2, line - 1)),
            pltpu.SemaphoreType.DMA((6,)),
            pltpu.SemaphoreType.DMA((7,)),
        ],
        compiler_params=pltpu.CompilerParams(
            collective_id=0, has_side_effects=True, vmem_limit_bytes=60 * 1024 * 1024
        ),
        cost_estimate=pl.CostEstimate(
            flops=7 * 10**9, bytes_accessed=16 * 10**6, transcendentals=10**6
        ),
    )(lists, *flat, out_weight)
    dq, dk, dv, dw = finish(dq, dk, dv, dw)
    back = [x.reshape(frames, frame_tokens, width) for x in (dq, dk, dv)]
    return (*back, dw)


def solution(mesh):
    whole_fits = dict(mesh.shape) == {"dp": 4, "tm": 4, "head": 2}
    return jax.shard_map(
        fused if whole_fits else per_device,
        mesh=mesh,
        in_specs=(
            P(("dp", "tm"), None, "head"),
            P(("dp", "tm"), None, "head"),
            P(("dp", "tm"), None, "head"),
            P(("dp", "tm"), None, "head"),
            P("tm", "head"),
            P(("dp", "tm"), None),
        ),
        out_specs=(
            P(("dp", "tm"), None, "head"),
            P(("dp", "tm"), None, "head"),
            P(("dp", "tm"), None, "head"),
            P(("dp", "tm"), "head"),
        ),
        check_vma=False,
    )
```

```python
import functools

import jax
import jax.numpy as jnp
from jax import lax
from jax.experimental import pallas as pl
from jax.experimental.pallas import tpu as pltpu
from jax.sharding import PartitionSpec as P

HD = 128
CF = 4
RET = 8


def slot_tables(owners, local_frame, slot_index, occupied, myself, capacity):
    slot_range = jnp.arange(capacity, dtype=jnp.int32)
    matches = (
        occupied[:, None, :]
        & (owners[:, None, :] == myself)
        & (slot_index[:, None, :] == slot_range[None, :, None])
    )
    source = jnp.sum(jnp.where(matches, local_frame[:, None, :], 0), axis=2)
    filled = jnp.any(matches, axis=2)
    return (source.reshape(-1), filled.reshape(-1))


def pack_slots(frame_rows, source, filled):
    picked = jnp.take(frame_rows, source, axis=0)
    return jnp.where(filled[:, None, None], picked, jnp.zeros_like(picked))


def per_device(queries, keys, values, out_grad, out_weight, lists):
    frames_dev, frame_tokens, width = queries.shape
    heads_dev = width // HD
    tm_count = lax.axis_size("tm")
    myself = lax.axis_index("tm")
    groups_dev = frames_dev // CF
    entry_count = groups_dev * RET
    token_rows = frames_dev * frame_tokens
    group_rows = CF * frame_tokens
    score_factor = HD ** (-0.5)
    per_owner = max(1, RET // tm_count)
    every_list = lax.all_gather(lists, "tm", axis=0, tiled=True)
    wanted = every_list.reshape(tm_count, entry_count)
    owners = wanted // frames_dev
    local_frame = wanted - owners * frames_dev
    position = jnp.arange(entry_count, dtype=jnp.int32)
    before = (position[:, None] < position[None, :])[None]
    same_owner = owners[:, :, None] == owners[:, None, :]
    same_frame = wanted[:, :, None] == wanted[:, None, :]
    first_seen = jnp.logical_not(jnp.any(same_frame & before, axis=1))
    entry_slot = jnp.sum(same_owner & before, axis=1)
    frame_first = jnp.sum(same_owner & before & first_seen[:, :, None], axis=1)
    frame_slot = jnp.sum(
        jnp.where(same_frame & first_seen[:, :, None], frame_first[:, :, None], 0), axis=1
    )
    my_owner = lax.dynamic_index_in_dim(owners, myself, 0, keepdims=False)
    my_entry_slot = lax.dynamic_index_in_dim(entry_slot, myself, 0, keepdims=False)
    my_frame_slot = lax.dynamic_index_in_dim(frame_slot, myself, 0, keepdims=False)
    frame_source, frame_filled = slot_tables(
        owners, local_frame, frame_slot, first_seen, myself, per_owner
    )
    capacity = groups_dev * per_owner
    source, filled = slot_tables(
        owners, local_frame, entry_slot, jnp.ones_like(first_seen), myself, capacity
    )
    got_keys, got_values = (
        lax.all_to_all(
            pack_slots(keys, source, filled), "tm", split_axis=0, concat_axis=0, tiled=True
        ),
        lax.all_to_all(
            pack_slots(values, source, filled), "tm", split_axis=0, concat_axis=0, tiled=True
        ),
    )
    lookup = my_owner * capacity + my_entry_slot
    grad_full = lax.all_gather(out_grad, "head", axis=2, tiled=True)
    grad_rows = grad_full.reshape(token_rows, grad_full.shape[2])
    columns = grad_rows
    attn_grad = jnp.dot(
        columns,
        lax.all_gather(out_weight, "tm", axis=0, tiled=True),
        preferred_element_type=jnp.float32,
    ).astype(jnp.bfloat16)
    far_keys = jnp.take(got_keys, lookup, axis=0)
    far_values = jnp.take(got_values, lookup, axis=0)
    far_span = RET * frame_tokens
    query_blocks = queries.reshape(groups_dev, group_rows, heads_dev, HD)
    key_set = jnp.concatenate(
        [
            keys.reshape(groups_dev, group_rows, heads_dev, HD),
            far_keys.reshape(groups_dev, far_span, heads_dev, HD),
        ],
        axis=1,
    )
    value_set = jnp.concatenate(
        [
            values.reshape(groups_dev, group_rows, heads_dev, HD),
            far_values.reshape(groups_dev, far_span, heads_dev, HD),
        ],
        axis=1,
    )
    scores = (
        jnp.einsum("cqhd,ckhd->chqk", query_blocks, key_set, preferred_element_type=jnp.float32)
        * score_factor
    )
    row_top = jnp.max(scores, axis=3, keepdims=True)
    weighted = jnp.exp(scores - row_top)
    prob = weighted / jnp.sum(weighted, axis=3, keepdims=True)
    prob_low = prob.astype(jnp.bfloat16)
    attn_out = jnp.einsum(
        "chqk,ckhd->cqhd", prob_low, value_set, preferred_element_type=jnp.float32
    ).astype(jnp.bfloat16)
    grad_blocks = attn_grad.reshape(groups_dev, group_rows, heads_dev, HD)
    row_dot = jnp.sum(grad_blocks.astype(jnp.float32) * attn_out.astype(jnp.float32), axis=3)
    row_dot = jnp.transpose(row_dot, (0, 2, 1))[..., None]
    prob_grad = jnp.einsum(
        "cqhd,ckhd->chqk", grad_blocks, value_set, preferred_element_type=jnp.float32
    )
    score_grad = (prob * (prob_grad - row_dot)).astype(jnp.bfloat16)
    query_grad = (
        jnp.einsum("chqk,ckhd->cqhd", score_grad, key_set, preferred_element_type=jnp.float32)
        * score_factor
    ).astype(jnp.bfloat16)
    key_term = (
        jnp.einsum("chqk,cqhd->ckhd", score_grad, query_blocks, preferred_element_type=jnp.float32)
        * score_factor
    )
    value_term = jnp.einsum(
        "chqk,cqhd->ckhd", prob_low, grad_blocks, preferred_element_type=jnp.float32
    )
    own_dk = key_term[:, :group_rows].reshape(frames_dev, frame_tokens, width)
    own_dv = value_term[:, :group_rows].reshape(frames_dev, frame_tokens, width)
    far_dk = key_term[:, group_rows:].reshape(entry_count, frame_tokens, width)
    far_dv = value_term[:, group_rows:].reshape(entry_count, frame_tokens, width)
    back_slot = my_owner * per_owner + my_frame_slot
    empty = jnp.zeros((tm_count * per_owner, frame_tokens, width), jnp.float32)
    back_keys = empty.at[back_slot].add(far_dk).astype(jnp.bfloat16)
    back_values = empty.at[back_slot].add(far_dv).astype(jnp.bfloat16)
    came_keys, came_values = (
        lax.all_to_all(back_keys, "tm", split_axis=0, concat_axis=0, tiled=True),
        lax.all_to_all(back_values, "tm", split_axis=0, concat_axis=0, tiled=True),
    )
    selector = (
        (frame_source[None, :] == jnp.arange(frames_dev, dtype=jnp.int32)[:, None])
        & frame_filled[None, :]
    ).astype(jnp.bfloat16)
    into_keys = jnp.dot(
        selector, came_keys.reshape(tm_count * per_owner, -1), preferred_element_type=jnp.float32
    )
    into_values = jnp.dot(
        selector, came_values.reshape(tm_count * per_owner, -1), preferred_element_type=jnp.float32
    )
    key_grad = (own_dk + into_keys.reshape(frames_dev, frame_tokens, width)).astype(jnp.bfloat16)
    value_grad = (own_dv + into_values.reshape(frames_dev, frame_tokens, width)).astype(
        jnp.bfloat16
    )
    attn_rows = attn_out.reshape(token_rows, width)
    columns = grad_rows
    weight_grad = lax.psum_scatter(
        lax.dot_general(
            columns, attn_rows, (((0,), (0,)), ((), ())), preferred_element_type=jnp.float32
        ).astype(jnp.bfloat16),
        "tm",
        scatter_dimension=0,
        tiled=True,
    ).astype(jnp.float32)
    return (query_grad.reshape(frames_dev, frame_tokens, width), key_grad, value_grad, weight_grad)


SELF, MATE, PARTNER, DIAG = 0, 1, 2, 3
F32 = jnp.float32
BF16 = jnp.bfloat16
NT = (((1,), (1,)), ((), ()))
TN = (((0,), (0,)), ((), ()))


def dot(a, b):
    return jnp.dot(a, b, preferred_element_type=F32)


def dotx(a, b, dims):
    return lax.dot_general(a, b, dims, preferred_element_type=F32)


def fused_kernel(
    slots, line, lists_ref, q_hbm, k_hbm, v_hbm, og_hbm, w_hbm,
    dq_ref, dk_ref, dv_ref, dw_ref,
    q_ref, k_ref, v_ref, w_ref,
    my_list, every_list, present, pick, send_k, send_v, far_k, far_v, og_halves, columns,
    columns_t, w_in, grad, attn, prob,
    own_k, own_v, back_k, back_v, came_k, came_v,
    send_sem, recv_sem, up_send, up_recv, down_send, down_recv, load_sem,
    relay_send, relay_recv,
):
    rows, width = q_ref.shape
    heads = width // HD
    entries = my_list.shape[0]
    frame_tokens = 32
    group_rows = CF * frame_tokens
    groups = rows // group_rows
    far_rows = slots * frame_tokens
    depth = w_ref.shape[0]
    chunks = 2
    span_width = width // chunks
    piece = depth // line
    half_rows = rows // 2
    scale = HD ** (-0.5)
    t = lax.axis_index("tm")
    h = lax.axis_index("head")
    z = lax.axis_index("dp")
    mate = t + 1 - 2 * (t % 2)
    partner = (t + 2) % 4
    diag = (mate + 2) % 4
    peers = (t, mate, partner, diag)

    barrier = pltpu.get_barrier_semaphore()
    for kind in (MATE, PARTNER, DIAG):
        pl.semaphore_signal(barrier, inc=1, device_id={"tm": peers[kind]})
    pl.semaphore_signal(barrier, inc=1, device_id={"head": 1 - h})

    for move in (1, line - 1):
        pl.semaphore_signal(barrier, inc=1, device_id={"dp": (z + move) % line})

    loads = []
    for source, target in (
        (k_hbm, k_ref),
        (v_hbm, v_ref),
        (og_hbm.at[:, pl.ds(0, depth)], og_halves.at[h, 0]),
        (og_hbm.at[:, pl.ds(depth, depth)], og_halves.at[h, 1]),
        (q_hbm, q_ref),
        (w_hbm, w_ref),
    ):
        loads.append(pltpu.make_async_copy(source, target, load_sem.at[len(loads)]))
        loads[-1].start()
    load_k, load_v, load_og0, load_og1, load_q, load_w = loads

    for entry in range(entries):
        named = lists_ref[entry // RET, entry % RET]
        my_list[entry : entry + 1, :] = jnp.full((1, rows), named, jnp.int32)
        every_list[SELF, entry : entry + 1, :] = jnp.full((1, rows), named, jnp.int32)
    pl.semaphore_wait(barrier, 6)

    started = []

    def send(src, dst, target):
        number = len(started)
        copy = pltpu.make_async_remote_copy(
            src_ref=src, dst_ref=dst, send_sem=send_sem.at[number], recv_sem=recv_sem.at[number],
            device_id=target,
        )
        copy.start()
        started.append(copy)
        return copy

    def to(kind):
        return {"tm": peers[kind]}

    lists_in = [
        send(my_list, every_list.at[kind], to(kind)) for kind in (PARTNER, DIAG, MATE)
    ]

    def chunk_cols(chunk):
        return pl.ds(chunk * span_width, span_width)

    def piece_rows(index):
        return pl.ds(pl.multiple_of(index * piece, piece), piece)

    crossing = []
    for chunk in range(chunks):
        crossing.append(
            send(
                w_hbm.at[piece_rows(z), chunk_cols(chunk)],
                w_in.at[PARTNER, chunk, piece_rows(z)],
                to(PARTNER),
            )
        )
    def hop(chunk, step, upward):
        move = 1 if upward else -1
        index = z - step if upward else z + step
        index = jnp.clip(index, 0, line - 1)
        held = w_in.at[PARTNER, chunk, piece_rows(index)]
        sends, recvs = (up_send, up_recv) if upward else (down_send, down_recv)
        return pltpu.make_async_remote_copy(
            src_ref=held, dst_ref=held, send_sem=sends.at[chunk, step],
            recv_sem=recvs.at[chunk, step], device_id={"dp": z + move},
        )

    def hop_sent(step, upward):
        if upward:
            return (z - step >= 0) & (z < line - 1)
        return (z + step < line) & (z > 0)

    def hop_received(step, upward):
        if upward:
            return z - 1 - step >= 0
        return z + 1 + step < line

    def relay(chunk, step, upward):
        index = jnp.clip(z - 1 - step if upward else z + 1 + step, 0, line - 1)
        place = 2 * step + (0 if upward else 1)
        return pltpu.make_async_remote_copy(
            src_ref=w_in.at[PARTNER, chunk, piece_rows(index)],
            dst_ref=w_in.at[DIAG, chunk, piece_rows(index)],
            send_sem=relay_send.at[chunk, place], recv_sem=relay_recv.at[chunk, place],
            device_id=to(MATE),
        )

    def relay_done(chunk, received):
        for step in range(line - 1):
            for upward in (True, False):

                @pl.when(hop_received(step, upward))
                def done():
                    if received:
                        relay(chunk, step, upward).wait_recv()
                    else:
                        relay(chunk, step, upward).wait_send()

    def hop_wait(chunk, step):
        for upward in (True, False):

            @pl.when(hop_received(step, upward))
            def arrived():
                hop(chunk, step, upward).wait_recv()
                relay(chunk, step, upward).start()

    diag_w = []

    def hop_start(chunk, step):
        if step == 0:
            crossing[chunk].wait_recv()
        else:
            hop_wait(chunk, step - 1)
        for upward in (True, False):

            @pl.when(hop_sent(step, upward))
            def onward():
                hop(chunk, step, upward).start()

        if step == 0:
            diag_w.append(
                send(
                    w_in.at[PARTNER, chunk, piece_rows(z)],
                    w_in.at[DIAG, chunk, piece_rows(z)],
                    to(MATE),
                )
            )

    halves_in = []
    for part in range(2):
        halves_in.append(
            send(
                og_hbm.at[:, pl.ds(part * depth, depth)], og_halves.at[h, part], {"head": 1 - h}
            )
        )
    for copy in lists_in:
        copy.wait_recv()

    lanes = lax.broadcasted_iota(jnp.int32, (entries, rows), 1)
    my_frame = t * (rows // frame_tokens) + lax.shift_right_logical(lanes, 5)
    for kind in range(4):
        named = jnp.max((every_list[kind] == my_frame).astype(F32), axis=0, keepdims=True)
        present[kind * frame_tokens : (kind + 1) * frame_tokens, :] = jnp.broadcast_to(
            named, (frame_tokens, rows)
        ).astype(BF16)
    above = lax.broadcasted_iota(jnp.int32, (rows, rows), 0)
    below = lax.broadcasted_iota(jnp.int32, (rows, rows), 1)
    earlier = (
        ((above & 31) == 0)
        & (lax.shift_right_logical(above, 5) < lax.shift_right_logical(below, 5))
    ).astype(F32).astype(BF16)
    rank = dot(present[...], earlier)
    token = lax.broadcasted_iota(jnp.int32, (frame_tokens, rows), 0)
    column_token = lax.broadcasted_iota(jnp.int32, (frame_tokens, rows), 1) & 31
    same_token = (token == column_token).astype(F32)
    for kind in range(4):
        span = slice(kind * frame_tokens, (kind + 1) * frame_tokens)
        here = present[span, :].astype(F32) * same_token
        for slot in range(slots):
            first = (kind * slots + slot) * frame_tokens
            pick[first : first + frame_tokens, :] = (
                here * (rank[span, :] == slot).astype(F32)
            ).astype(BF16)

    tile = 512

    def tiled(body):
        def step(i, carry):
            body(pl.ds(pl.multiple_of(i * tile, tile), tile))
            return carry

        lax.fori_loop(0, width // tile, step, 0)

    def span_of(kind):
        return pl.ds(kind * far_rows, far_rows)

    def pick_keys(cols):
        send_k[:, cols] = dot(pick[...], k_ref[:, cols]).astype(BF16)

    def pick_values(cols):
        send_v[:, cols] = dot(pick[...], v_ref[:, cols]).astype(BF16)

    frames_in = []
    load_k.wait()
    tiled(pick_keys)
    for kind in (PARTNER, DIAG, MATE):
        frames_in.append(send(send_k.at[span_of(kind)], far_k.at[span_of(kind)], to(kind)))
    load_v.wait()
    tiled(pick_values)
    for kind in (PARTNER, DIAG, MATE):
        frames_in.append(send(send_v.at[span_of(kind)], far_v.at[span_of(kind)], to(kind)))
    far_k[0:far_rows, :] = send_k[0:far_rows, :]
    far_v[0:far_rows, :] = send_v[0:far_rows, :]


    hop_start(0, 0)
    hop_start(0, 1)
    load_og0.wait()
    load_og1.wait()
    for copy in halves_in:
        copy.wait_recv()
    mine = pl.ds(pl.multiple_of(h * half_rows, half_rows), half_rows)
    columns_in = {}
    for kind in (PARTNER, DIAG):
        peer = peers[kind]
        columns_in[kind] = send(
            og_halves.at[peer // 2, peer % 2, mine], columns.at[kind, mine], to(kind)
        )
    columns_in[MATE] = send(og_halves.at[mate // 2, mate % 2], columns.at[MATE], to(MATE))
    columns[SELF] = og_halves[t // 2, t % 2]
    hop_start(0, 2)
    hop_start(1, 0)
    mate_w = [
        send(w_hbm.at[:, chunk_cols(chunk)], w_in.at[MATE, chunk], to(MATE))
        for chunk in range(chunks)
    ]
    hop_start(1, 1)

    load_q.wait()
    for copy in frames_in:
        copy.wait_recv()

    def forward(i, carry):
        cols = pl.ds(pl.multiple_of(i * HD, HD), HD)
        fk = far_k[:, cols]
        fv = far_v[:, cols]
        for g in range(groups):
            span = slice(g * group_rows, (g + 1) * group_rows)
            q = q_ref[span, cols]
            near = dotx(q, k_ref[span, cols], NT) * scale
            far = dotx(q, fk, NT) * scale
            top = jnp.maximum(
                jnp.max(near, axis=1, keepdims=True), jnp.max(far, axis=1, keepdims=True)
            )
            near = jnp.exp(near - top)
            far = jnp.exp(far - top)
            total = jnp.sum(near, axis=1, keepdims=True) + jnp.sum(far, axis=1, keepdims=True)
            near = near / total
            far = far / total
            prob[i, span, 0:group_rows] = near
            prob[i, span, group_rows:] = far
            out = dot(near.astype(BF16), v_ref[span, cols]) + dot(far.astype(BF16), fv)
            attn[SELF, span, cols] = out.astype(BF16)
        return carry

    each = heads // chunks
    attn_partner = []
    attn_mate = []
    for chunk in range(chunks):
        lax.fori_loop(chunk * each, (chunk + 1) * each, forward, 0)
        own = attn.at[SELF, :, chunk_cols(chunk)]
        attn_mate.append(send(own, attn.at[MATE, :, chunk_cols(chunk)], to(MATE)))
        attn_partner.append(send(own, attn.at[PARTNER, :, chunk_cols(chunk)], to(PARTNER)))
        if chunk == 0:
            hop_start(1, 2)
            hop_wait(0, 2)
    swapped = []
    for kind in (PARTNER, DIAG):
        columns_in[kind].wait_recv()
        swapped.append(send(columns.at[kind, mine], columns.at[kind, mine], {"head": 1 - h}))

    def backward(i, carry):
        cols = pl.ds(pl.multiple_of(i * HD, HD), HD)
        fk = far_k[:, cols]
        fv = far_v[:, cols]
        far_dk = None
        far_dv = None
        for g in range(groups):
            span = slice(g * group_rows, (g + 1) * group_rows)
            q = q_ref[span, cols]
            do = grad[span, cols]
            row_dot = jnp.sum(
                do.astype(F32) * attn[SELF, span, cols].astype(F32), axis=1, keepdims=True
            )
            near = prob[i, span, 0:group_rows]
            far = prob[i, span, group_rows:]
            near_ds = (near * (dotx(do, v_ref[span, cols], NT) - row_dot)).astype(BF16)
            far_ds = (far * (dotx(do, fv, NT) - row_dot)).astype(BF16)
            near_p = near.astype(BF16)
            far_p = far.astype(BF16)
            dq_ref[span, cols] = (
                (dot(near_ds, k_ref[span, cols]) + dot(far_ds, fk)) * scale
            ).astype(BF16)
            own_k[span, cols] = dotx(near_ds, q, TN) * scale
            own_v[span, cols] = dotx(near_p, do, TN)
            more_k = dotx(far_ds, q, TN)
            more_v = dotx(far_p, do, TN)
            far_dk = more_k if g == 0 else far_dk + more_k
            far_dv = more_v if g == 0 else far_dv + more_v
        back_k[:, cols] = (far_dk * scale).astype(BF16)
        back_v[:, cols] = far_dv.astype(BF16)
        return carry

    load_w.wait()
    returned = []
    step_width = span_width // 2
    for part in range(2 * chunks):
        chunk = part // 2
        if part % 2 == 0:
            if chunk == 1:
                hop_wait(1, 2)
            mate_w[chunk].wait_recv()
            diag_w[chunk].wait_recv()
            relay_done(chunk, True)
        local = pl.ds(part % 2 * step_width, step_width)
        cols = pl.ds(part * step_width, step_width)
        total = dot(og_halves[t // 2, t % 2], w_ref[:, cols])
        for kind in (MATE, PARTNER, DIAG):
            peer = peers[kind]
            total += dot(og_halves[peer // 2, peer % 2], w_in[kind, chunk, :, local])
        grad[:, cols] = total.astype(BF16)
        lax.fori_loop(part * each // 2, (part + 1) * each // 2, backward, 0)
        for kind in (PARTNER, DIAG, MATE):
            for out, into in ((back_k, came_k), (back_v, came_v)):
                returned.append(
                    send(out.at[span_of(kind), cols], into.at[span_of(kind), cols], to(kind))
                )
    came_k[0:far_rows, :] = back_k[0:far_rows, :]
    came_v[0:far_rows, :] = back_v[0:far_rows, :]
    attn_diag = []
    for chunk in range(chunks):
        attn_partner[chunk].wait_recv()
        held = attn.at[PARTNER, :, chunk_cols(chunk)]
        attn_diag.append(send(held, attn.at[DIAG, :, chunk_cols(chunk)], to(MATE)))
    columns_in[MATE].wait_recv()
    for copy in swapped:
        copy.wait_recv()
    for kind in range(4):
        columns_t[kind] = columns[kind].T
    for copy in attn_mate + attn_diag:
        copy.wait_recv()

    def weight_part(cols):
        total = dot(columns_t[SELF], attn[SELF, :, cols])
        for kind in (MATE, PARTNER, DIAG):
            total += dot(columns_t[kind], attn[kind, :, cols])
        dw_ref[:, cols] = total

    tiled(weight_part)

    per_part = len(returned) // (2 * chunks)
    for part in range(2 * chunks):
        for copy in returned[part * per_part : (part + 1) * per_part]:
            copy.wait_recv()
        cols = pl.ds(part * step_width, step_width)
        dk_ref[:, cols] = (own_k[:, cols] + dotx(pick[...], came_k[:, cols], TN)).astype(BF16)
        dv_ref[:, cols] = (own_v[:, cols] + dotx(pick[...], came_v[:, cols], TN)).astype(BF16)
    for copy in started:
        copy.wait_send()
    for chunk in range(chunks):
        for step in range(line - 1):
            for upward in (True, False):

                @pl.when(hop_sent(step, upward))
                def left():
                    hop(chunk, step, upward).wait_send()

    for chunk in range(chunks):
        relay_done(chunk, False)


def finish_kernel(dq_ref, dk_ref, dv_ref, dw_ref, dq_out, dk_out, dv_out, dw_out, sem):
    copies = [
        pltpu.make_async_copy(source, target, sem.at[number])
        for number, (source, target) in enumerate(
            ((dw_ref, dw_out), (dq_ref, dq_out), (dk_ref, dk_out), (dv_ref, dv_out))
        )
    ]
    for copy in copies:
        copy.start()
    for copy in copies:
        copy.wait()


def finish(dq, dk, dv, dw):
    rows, width = dq.shape
    depth = dw.shape[0]
    vmem = pl.BlockSpec(memory_space=pltpu.VMEM)
    hbm = pl.BlockSpec(memory_space=pltpu.HBM)
    return pl.pallas_call(
        finish_kernel,
        out_shape=[jax.ShapeDtypeStruct((rows, width), BF16)] * 3
        + [jax.ShapeDtypeStruct((depth, width), F32)],
        in_specs=[vmem] * 4,
        out_specs=[hbm] * 4,
        scratch_shapes=[pltpu.SemaphoreType.DMA((4,))],
        compiler_params=pltpu.CompilerParams(vmem_limit_bytes=16 * 1024 * 1024),
        cost_estimate=pl.CostEstimate(flops=0, bytes_accessed=7 * 10**6, transcendentals=0),
    )(dq, dk, dv, dw)


def fused(queries, keys, values, out_grad, out_weight, lists):
    frames, frame_tokens, width = queries.shape
    rows = frames * frame_tokens
    depth = out_weight.shape[0]
    slots = RET // 4
    heads = width // HD
    flat = [x.reshape(rows, width) for x in (queries, keys, values, out_grad)]
    line = lax.axis_size("dp")
    hbm = pl.BlockSpec(memory_space=pltpu.HBM)
    far = 4 * slots * frame_tokens

    def low(*shape):
        return pltpu.VMEM(shape, BF16)

    def wide(*shape):
        return pltpu.VMEM(shape, F32)

    dq, dk, dv, dw = pl.pallas_call(
        functools.partial(fused_kernel, slots, line),
        out_shape=[pltpu.VMEM((rows, width), BF16)] * 3 + [pltpu.VMEM((depth, width), F32)],
        in_specs=[pl.BlockSpec(memory_space=pltpu.SMEM)] + [hbm] * 5,
        out_specs=[pl.BlockSpec(memory_space=pltpu.VMEM)] * 4,
        scratch_shapes=[
            low(rows, width),
            low(rows, width),
            low(rows, width),
            low(depth, width),
            pltpu.VMEM((lists.size, rows), jnp.int32),
            pltpu.VMEM((4, lists.size, rows), jnp.int32),
            low(4 * frame_tokens, rows),
            low(far, rows),
            low(far, width),
            low(far, width),
            low(far, width),
            low(far, width),
            low(2, 2, rows, depth),
            low(4, rows, depth),
            low(4, depth, rows),
            low(4, 2, depth, width // 2),
            low(rows, width),
            low(4, rows, width),
            wide(heads, rows, CF * frame_tokens + far),
            wide(rows, width),
            wide(rows, width),
            low(far, width),
            low(far, width),
            low(far, width),
            low(far, width),
            pltpu.SemaphoreType.DMA((64,)),
            pltpu.SemaphoreType.DMA((64,)),
            pltpu.SemaphoreType.DMA((2, line - 1)),
            pltpu.SemaphoreType.DMA((2, line - 1)),
            pltpu.SemaphoreType.DMA((2, line - 1)),
            pltpu.SemaphoreType.DMA((2, line - 1)),
            pltpu.SemaphoreType.DMA((6,)),
            pltpu.SemaphoreType.DMA((2, 2 * (line - 1))),
            pltpu.SemaphoreType.DMA((2, 2 * (line - 1))),
        ],
        compiler_params=pltpu.CompilerParams(
            collective_id=0, has_side_effects=True, vmem_limit_bytes=50 * 1024 * 1024
        ),
        cost_estimate=pl.CostEstimate(
            flops=7 * 10**9, bytes_accessed=16 * 10**6, transcendentals=10**6
        ),
    )(lists, *flat, out_weight)
    dq, dk, dv, dw = finish(dq, dk, dv, dw)
    back = [x.reshape(frames, frame_tokens, width) for x in (dq, dk, dv)]
    return (*back, dw)


def solution(mesh):
    whole_fits = dict(mesh.shape) == {"dp": 4, "tm": 4, "head": 2}
    return jax.shard_map(
        fused if whole_fits else per_device,
        mesh=mesh,
        in_specs=(
            P(("dp", "tm"), None, "head"),
            P(("dp", "tm"), None, "head"),
            P(("dp", "tm"), None, "head"),
            P(("dp", "tm"), None, "head"),
            P("tm", "head"),
            P(("dp", "tm"), None),
        ),
        out_specs=(
            P(("dp", "tm"), None, "head"),
            P(("dp", "tm"), None, "head"),
            P(("dp", "tm"), None, "head"),
            P(("dp", "tm"), "head"),
        ),
        check_vma=False,
    )
```

```python
import functools

import jax
import jax.numpy as jnp
from jax import lax
from jax.experimental import pallas as pl
from jax.experimental.pallas import tpu as pltpu
from jax.sharding import PartitionSpec as P

HD = 128
CF = 4
RET = 8


def slot_tables(owners, local_frame, slot_index, occupied, myself, capacity):
    slot_range = jnp.arange(capacity, dtype=jnp.int32)
    matches = (
        occupied[:, None, :]
        & (owners[:, None, :] == myself)
        & (slot_index[:, None, :] == slot_range[None, :, None])
    )
    source = jnp.sum(jnp.where(matches, local_frame[:, None, :], 0), axis=2)
    filled = jnp.any(matches, axis=2)
    return (source.reshape(-1), filled.reshape(-1))


def pack_slots(frame_rows, source, filled):
    picked = jnp.take(frame_rows, source, axis=0)
    return jnp.where(filled[:, None, None], picked, jnp.zeros_like(picked))


def per_device(queries, keys, values, out_grad, out_weight, lists):
    frames_dev, frame_tokens, width = queries.shape
    heads_dev = width // HD
    tm_count = lax.axis_size("tm")
    myself = lax.axis_index("tm")
    groups_dev = frames_dev // CF
    entry_count = groups_dev * RET
    token_rows = frames_dev * frame_tokens
    group_rows = CF * frame_tokens
    score_factor = HD ** (-0.5)
    per_owner = max(1, RET // tm_count)
    every_list = lax.all_gather(lists, "tm", axis=0, tiled=True)
    wanted = every_list.reshape(tm_count, entry_count)
    owners = wanted // frames_dev
    local_frame = wanted - owners * frames_dev
    position = jnp.arange(entry_count, dtype=jnp.int32)
    before = (position[:, None] < position[None, :])[None]
    same_owner = owners[:, :, None] == owners[:, None, :]
    same_frame = wanted[:, :, None] == wanted[:, None, :]
    first_seen = jnp.logical_not(jnp.any(same_frame & before, axis=1))
    entry_slot = jnp.sum(same_owner & before, axis=1)
    frame_first = jnp.sum(same_owner & before & first_seen[:, :, None], axis=1)
    frame_slot = jnp.sum(
        jnp.where(same_frame & first_seen[:, :, None], frame_first[:, :, None], 0), axis=1
    )
    my_owner = lax.dynamic_index_in_dim(owners, myself, 0, keepdims=False)
    my_entry_slot = lax.dynamic_index_in_dim(entry_slot, myself, 0, keepdims=False)
    my_frame_slot = lax.dynamic_index_in_dim(frame_slot, myself, 0, keepdims=False)
    frame_source, frame_filled = slot_tables(
        owners, local_frame, frame_slot, first_seen, myself, per_owner
    )
    capacity = groups_dev * per_owner
    source, filled = slot_tables(
        owners, local_frame, entry_slot, jnp.ones_like(first_seen), myself, capacity
    )
    got_keys, got_values = (
        lax.all_to_all(
            pack_slots(keys, source, filled), "tm", split_axis=0, concat_axis=0, tiled=True
        ),
        lax.all_to_all(
            pack_slots(values, source, filled), "tm", split_axis=0, concat_axis=0, tiled=True
        ),
    )
    lookup = my_owner * capacity + my_entry_slot
    grad_full = lax.all_gather(out_grad, "head", axis=2, tiled=True)
    grad_rows = grad_full.reshape(token_rows, grad_full.shape[2])
    columns = grad_rows
    attn_grad = jnp.dot(
        columns,
        lax.all_gather(out_weight, "tm", axis=0, tiled=True),
        preferred_element_type=jnp.float32,
    ).astype(jnp.bfloat16)
    far_keys = jnp.take(got_keys, lookup, axis=0)
    far_values = jnp.take(got_values, lookup, axis=0)
    far_span = RET * frame_tokens
    query_blocks = queries.reshape(groups_dev, group_rows, heads_dev, HD)
    key_set = jnp.concatenate(
        [
            keys.reshape(groups_dev, group_rows, heads_dev, HD),
            far_keys.reshape(groups_dev, far_span, heads_dev, HD),
        ],
        axis=1,
    )
    value_set = jnp.concatenate(
        [
            values.reshape(groups_dev, group_rows, heads_dev, HD),
            far_values.reshape(groups_dev, far_span, heads_dev, HD),
        ],
        axis=1,
    )
    scores = (
        jnp.einsum("cqhd,ckhd->chqk", query_blocks, key_set, preferred_element_type=jnp.float32)
        * score_factor
    )
    row_top = jnp.max(scores, axis=3, keepdims=True)
    weighted = jnp.exp(scores - row_top)
    prob = weighted / jnp.sum(weighted, axis=3, keepdims=True)
    prob_low = prob.astype(jnp.bfloat16)
    attn_out = jnp.einsum(
        "chqk,ckhd->cqhd", prob_low, value_set, preferred_element_type=jnp.float32
    ).astype(jnp.bfloat16)
    grad_blocks = attn_grad.reshape(groups_dev, group_rows, heads_dev, HD)
    row_dot = jnp.sum(grad_blocks.astype(jnp.float32) * attn_out.astype(jnp.float32), axis=3)
    row_dot = jnp.transpose(row_dot, (0, 2, 1))[..., None]
    prob_grad = jnp.einsum(
        "cqhd,ckhd->chqk", grad_blocks, value_set, preferred_element_type=jnp.float32
    )
    score_grad = (prob * (prob_grad - row_dot)).astype(jnp.bfloat16)
    query_grad = (
        jnp.einsum("chqk,ckhd->cqhd", score_grad, key_set, preferred_element_type=jnp.float32)
        * score_factor
    ).astype(jnp.bfloat16)
    key_term = (
        jnp.einsum("chqk,cqhd->ckhd", score_grad, query_blocks, preferred_element_type=jnp.float32)
        * score_factor
    )
    value_term = jnp.einsum(
        "chqk,cqhd->ckhd", prob_low, grad_blocks, preferred_element_type=jnp.float32
    )
    own_dk = key_term[:, :group_rows].reshape(frames_dev, frame_tokens, width)
    own_dv = value_term[:, :group_rows].reshape(frames_dev, frame_tokens, width)
    far_dk = key_term[:, group_rows:].reshape(entry_count, frame_tokens, width)
    far_dv = value_term[:, group_rows:].reshape(entry_count, frame_tokens, width)
    back_slot = my_owner * per_owner + my_frame_slot
    empty = jnp.zeros((tm_count * per_owner, frame_tokens, width), jnp.float32)
    back_keys = empty.at[back_slot].add(far_dk).astype(jnp.bfloat16)
    back_values = empty.at[back_slot].add(far_dv).astype(jnp.bfloat16)
    came_keys, came_values = (
        lax.all_to_all(back_keys, "tm", split_axis=0, concat_axis=0, tiled=True),
        lax.all_to_all(back_values, "tm", split_axis=0, concat_axis=0, tiled=True),
    )
    selector = (
        (frame_source[None, :] == jnp.arange(frames_dev, dtype=jnp.int32)[:, None])
        & frame_filled[None, :]
    ).astype(jnp.bfloat16)
    into_keys = jnp.dot(
        selector, came_keys.reshape(tm_count * per_owner, -1), preferred_element_type=jnp.float32
    )
    into_values = jnp.dot(
        selector, came_values.reshape(tm_count * per_owner, -1), preferred_element_type=jnp.float32
    )
    key_grad = (own_dk + into_keys.reshape(frames_dev, frame_tokens, width)).astype(jnp.bfloat16)
    value_grad = (own_dv + into_values.reshape(frames_dev, frame_tokens, width)).astype(
        jnp.bfloat16
    )
    attn_rows = attn_out.reshape(token_rows, width)
    columns = grad_rows
    weight_grad = lax.psum_scatter(
        lax.dot_general(
            columns, attn_rows, (((0,), (0,)), ((), ())), preferred_element_type=jnp.float32
        ).astype(jnp.bfloat16),
        "tm",
        scatter_dimension=0,
        tiled=True,
    ).astype(jnp.float32)
    return (query_grad.reshape(frames_dev, frame_tokens, width), key_grad, value_grad, weight_grad)


SELF, MATE, PARTNER, DIAG = 0, 1, 2, 3
F32 = jnp.float32
BF16 = jnp.bfloat16
NT = (((1,), (1,)), ((), ()))
TN = (((0,), (0,)), ((), ()))


def dot(a, b):
    return jnp.dot(a, b, preferred_element_type=F32)


def dotx(a, b, dims):
    return lax.dot_general(a, b, dims, preferred_element_type=F32)


def fused_kernel(
    slots, line, lists_ref, q_hbm, k_hbm, v_hbm, og_hbm, w_hbm,
    dq_ref, dk_ref, dv_ref, dw_ref,
    q_ref, k_ref, v_ref, w_ref,
    my_list, every_list, present, pick, send_k, send_v, far_k, far_v, og_halves, columns,
    columns_t, w_in, grad, attn, prob,
    own_k, own_v, back_k, back_v, came_k, came_v,
    send_sem, recv_sem, up_send, up_recv, down_send, down_recv, load_sem,
    relay_send, relay_recv,
):
    rows, width = q_ref.shape
    heads = width // HD
    entries, lanes = my_list.shape
    frame_tokens = 32
    group_rows = CF * frame_tokens
    groups = rows // group_rows
    far_rows = slots * frame_tokens
    depth = w_ref.shape[0]
    chunks = 2
    span_width = width // chunks
    piece = depth // line
    half_rows = rows // 2
    scale = HD ** (-0.5)
    t = lax.axis_index("tm")
    h = lax.axis_index("head")
    z = lax.axis_index("dp")
    mate = t + 1 - 2 * (t % 2)
    partner = (t + 2) % 4
    diag = (mate + 2) % 4
    peers = (t, mate, partner, diag)

    barrier = pltpu.get_barrier_semaphore()
    for kind in (MATE, PARTNER, DIAG):
        pl.semaphore_signal(barrier, inc=1, device_id={"tm": peers[kind]})
    pl.semaphore_signal(barrier, inc=1, device_id={"head": 1 - h})

    @pl.when(z > 0)
    def greet_below():
        pl.semaphore_signal(barrier, inc=1, device_id={"dp": z - 1})

    @pl.when(z < line - 1)
    def greet_above():
        pl.semaphore_signal(barrier, inc=1, device_id={"dp": z + 1})

    loads = []
    for source, target in (
        (k_hbm, k_ref),
        (v_hbm, v_ref),
        (og_hbm.at[:, pl.ds(0, depth)], og_halves.at[h, 0]),
        (og_hbm.at[:, pl.ds(depth, depth)], og_halves.at[h, 1]),
        (q_hbm, q_ref),
        (w_hbm, w_ref),
    ):
        loads.append(pltpu.make_async_copy(source, target, load_sem.at[len(loads)]))
        loads[-1].start()
    load_k, load_v, load_og0, load_og1, load_q, load_w = loads

    for entry in range(entries):
        named = lists_ref[entry // RET, entry % RET]
        my_list[entry : entry + 1, :] = jnp.full((1, lanes), named, jnp.int32)
        every_list[SELF, entry : entry + 1, :] = jnp.full((1, lanes), named, jnp.int32)
    sides = (z + line - 1) // line + (2 * line - 2 - z) // line
    pl.semaphore_wait(barrier, 4 + sides)

    started = []

    def send(src, dst, target):
        number = len(started)
        copy = pltpu.make_async_remote_copy(
            src_ref=src, dst_ref=dst, send_sem=send_sem.at[number], recv_sem=recv_sem.at[number],
            device_id=target,
        )
        copy.start()
        started.append(copy)
        return copy

    def to(kind):
        return {"tm": peers[kind]}

    lists_in = [
        send(my_list, every_list.at[kind], to(kind)) for kind in (PARTNER, DIAG, MATE)
    ]

    def chunk_cols(chunk):
        return pl.ds(chunk * span_width, span_width)

    def piece_rows(index):
        return pl.ds(pl.multiple_of(index * piece, piece), piece)

    crossing = []
    for chunk in range(chunks):
        crossing.append(
            send(
                w_hbm.at[piece_rows(z), chunk_cols(chunk)],
                w_in.at[PARTNER, chunk, piece_rows(z)],
                to(PARTNER),
            )
        )
    def hop(chunk, step, upward):
        move = 1 if upward else -1
        index = z - step if upward else z + step
        index = jnp.clip(index, 0, line - 1)
        held = w_in.at[PARTNER, chunk, piece_rows(index)]
        sends, recvs = (up_send, up_recv) if upward else (down_send, down_recv)
        return pltpu.make_async_remote_copy(
            src_ref=held, dst_ref=held, send_sem=sends.at[chunk, step],
            recv_sem=recvs.at[chunk, step], device_id={"dp": z + move},
        )

    def hop_sent(step, upward):
        if upward:
            return (z - step >= 0) & (z < line - 1)
        return (z + step < line) & (z > 0)

    def hop_received(step, upward):
        if upward:
            return z - 1 - step >= 0
        return z + 1 + step < line

    def relay(chunk, step, upward):
        index = jnp.clip(z - 1 - step if upward else z + 1 + step, 0, line - 1)
        place = 2 * step + (0 if upward else 1)
        return pltpu.make_async_remote_copy(
            src_ref=w_in.at[PARTNER, chunk, piece_rows(index)],
            dst_ref=w_in.at[DIAG, chunk, piece_rows(index)],
            send_sem=relay_send.at[chunk, place], recv_sem=relay_recv.at[chunk, place],
            device_id=to(MATE),
        )

    def relay_done(chunk, received):
        for step in range(line - 1):
            for upward in (True, False):

                @pl.when(hop_received(step, upward))
                def done():
                    if received:
                        relay(chunk, step, upward).wait_recv()
                    else:
                        relay(chunk, step, upward).wait_send()

    def hop_wait(chunk, step):
        for upward in (True, False):

            @pl.when(hop_received(step, upward))
            def arrived():
                hop(chunk, step, upward).wait_recv()
                relay(chunk, step, upward).start()

    diag_w = []

    def hop_start(chunk, step):
        if step == 0:
            crossing[chunk].wait_recv()
        else:
            hop_wait(chunk, step - 1)
        for upward in (True, False):

            @pl.when(hop_sent(step, upward))
            def onward():
                hop(chunk, step, upward).start()

        if step == 0:
            diag_w.append(
                send(
                    w_in.at[PARTNER, chunk, piece_rows(z)],
                    w_in.at[DIAG, chunk, piece_rows(z)],
                    to(MATE),
                )
            )

    halves_in = []
    for part in range(2):
        halves_in.append(
            send(
                og_hbm.at[:, pl.ds(part * depth, depth)], og_halves.at[h, part], {"head": 1 - h}
            )
        )
    for copy in lists_in:
        copy.wait_recv()

    lane_frame = lax.shift_right_logical(
        lax.broadcasted_iota(jnp.int32, (entries, lanes), 1), 5
    )
    for side in range(rows // lanes):
        my_frame = (t * rows + side * lanes) // frame_tokens + lane_frame
        for kind in range(4):
            named = jnp.max((every_list[kind] == my_frame).astype(F32), axis=0, keepdims=True)
            present[
                kind * frame_tokens : (kind + 1) * frame_tokens,
                side * lanes : (side + 1) * lanes,
            ] = jnp.broadcast_to(named, (frame_tokens, lanes)).astype(BF16)
    above = lax.broadcasted_iota(jnp.int32, (rows, rows), 0)
    below = lax.broadcasted_iota(jnp.int32, (rows, rows), 1)
    earlier = (
        ((above & 31) == 0)
        & (lax.shift_right_logical(above, 5) < lax.shift_right_logical(below, 5))
    ).astype(F32).astype(BF16)
    rank = dot(present[...], earlier)
    token = lax.broadcasted_iota(jnp.int32, (frame_tokens, rows), 0)
    column_token = lax.broadcasted_iota(jnp.int32, (frame_tokens, rows), 1) & 31
    same_token = (token == column_token).astype(F32)
    for kind in range(4):
        span = slice(kind * frame_tokens, (kind + 1) * frame_tokens)
        here = present[span, :].astype(F32) * same_token
        for slot in range(slots):
            first = (kind * slots + slot) * frame_tokens
            pick[first : first + frame_tokens, :] = (
                here * (rank[span, :] == slot).astype(F32)
            ).astype(BF16)

    tile = 512

    def tiled(body):
        def step(i, carry):
            body(pl.ds(pl.multiple_of(i * tile, tile), tile))
            return carry

        lax.fori_loop(0, width // tile, step, 0)

    def span_of(kind):
        return pl.ds(kind * far_rows, far_rows)

    def pick_keys(cols):
        send_k[:, cols] = dot(pick[...], k_ref[:, cols]).astype(BF16)

    def pick_values(cols):
        send_v[:, cols] = dot(pick[...], v_ref[:, cols]).astype(BF16)

    frames_in = []
    load_k.wait()
    tiled(pick_keys)
    for kind in (PARTNER, DIAG, MATE):
        frames_in.append(send(send_k.at[span_of(kind)], far_k.at[span_of(kind)], to(kind)))
    load_v.wait()
    tiled(pick_values)
    for kind in (PARTNER, DIAG, MATE):
        frames_in.append(send(send_v.at[span_of(kind)], far_v.at[span_of(kind)], to(kind)))
    far_k[0:far_rows, :] = send_k[0:far_rows, :]
    far_v[0:far_rows, :] = send_v[0:far_rows, :]


    hop_start(0, 0)
    hop_start(0, 1)
    load_og0.wait()
    load_og1.wait()
    for copy in halves_in:
        copy.wait_recv()
    mine = pl.ds(pl.multiple_of(h * half_rows, half_rows), half_rows)
    columns_in = {}
    for kind in (PARTNER, DIAG):
        peer = peers[kind]
        columns_in[kind] = send(
            og_halves.at[peer // 2, peer % 2, mine], columns.at[kind, mine], to(kind)
        )
    columns_in[MATE] = send(og_halves.at[mate // 2, mate % 2], columns.at[MATE], to(MATE))
    columns[SELF] = og_halves[t // 2, t % 2]
    hop_start(0, 2)
    hop_start(1, 0)
    mate_w = [
        send(w_hbm.at[:, chunk_cols(chunk)], w_in.at[MATE, chunk], to(MATE))
        for chunk in range(chunks)
    ]
    hop_start(1, 1)

    load_q.wait()
    for copy in frames_in:
        copy.wait_recv()

    def forward(i, carry):
        cols = pl.ds(pl.multiple_of(i * HD, HD), HD)
        fk = far_k[:, cols]
        fv = far_v[:, cols]
        for g in range(groups):
            span = slice(g * group_rows, (g + 1) * group_rows)
            q = q_ref[span, cols]
            near = dotx(q, k_ref[span, cols], NT) * scale
            far = dotx(q, fk, NT) * scale
            top = jnp.maximum(
                jnp.max(near, axis=1, keepdims=True), jnp.max(far, axis=1, keepdims=True)
            )
            near = jnp.exp(near - top)
            far = jnp.exp(far - top)
            total = jnp.sum(near, axis=1, keepdims=True) + jnp.sum(far, axis=1, keepdims=True)
            near = near / total
            far = far / total
            prob[i, span, 0:group_rows] = near
            prob[i, span, group_rows:] = far
            out = dot(near.astype(BF16), v_ref[span, cols]) + dot(far.astype(BF16), fv)
            attn[SELF, span, cols] = out.astype(BF16)
        return carry

    each = heads // chunks
    attn_partner = []
    attn_mate = []
    for chunk in range(chunks):
        lax.fori_loop(chunk * each, (chunk + 1) * each, forward, 0)
        own = attn.at[SELF, :, chunk_cols(chunk)]
        attn_mate.append(send(own, attn.at[MATE, :, chunk_cols(chunk)], to(MATE)))
        attn_partner.append(send(own, attn.at[PARTNER, :, chunk_cols(chunk)], to(PARTNER)))
        if chunk == 0:
            hop_start(1, 2)
            hop_wait(0, 2)
    swapped = []
    for kind in (PARTNER, DIAG):
        columns_in[kind].wait_recv()
        swapped.append(send(columns.at[kind, mine], columns.at[kind, mine], {"head": 1 - h}))

    def backward(i, carry):
        cols = pl.ds(pl.multiple_of(i * HD, HD), HD)
        fk = far_k[:, cols]
        fv = far_v[:, cols]
        far_dk = None
        far_dv = None
        for g in range(groups):
            span = slice(g * group_rows, (g + 1) * group_rows)
            q = q_ref[span, cols]
            do = grad[span, cols]
            row_dot = jnp.sum(
                do.astype(F32) * attn[SELF, span, cols].astype(F32), axis=1, keepdims=True
            )
            near = prob[i, span, 0:group_rows]
            far = prob[i, span, group_rows:]
            near_ds = (near * (dotx(do, v_ref[span, cols], NT) - row_dot)).astype(BF16)
            far_ds = (far * (dotx(do, fv, NT) - row_dot)).astype(BF16)
            near_p = near.astype(BF16)
            far_p = far.astype(BF16)
            dq_ref[span, cols] = (
                (dot(near_ds, k_ref[span, cols]) + dot(far_ds, fk)) * scale
            ).astype(BF16)
            own_k[span, cols] = dotx(near_ds, q, TN) * scale
            own_v[span, cols] = dotx(near_p, do, TN)
            more_k = dotx(far_ds, q, TN)
            more_v = dotx(far_p, do, TN)
            far_dk = more_k if g == 0 else far_dk + more_k
            far_dv = more_v if g == 0 else far_dv + more_v
        back_k[:, cols] = (far_dk * scale).astype(BF16)
        back_v[:, cols] = far_dv.astype(BF16)
        return carry

    load_w.wait()
    returned = []
    step_width = span_width // 2
    for part in range(2 * chunks):
        chunk = part // 2
        if part % 2 == 0:
            if chunk == 1:
                hop_wait(1, 2)
            mate_w[chunk].wait_recv()
            diag_w[chunk].wait_recv()
            relay_done(chunk, True)
        local = pl.ds(part % 2 * step_width, step_width)
        cols = pl.ds(part * step_width, step_width)
        total = dot(og_halves[t // 2, t % 2], w_ref[:, cols])
        for kind in (MATE, PARTNER, DIAG):
            peer = peers[kind]
            total += dot(og_halves[peer // 2, peer % 2], w_in[kind, chunk, :, local])
        grad[:, cols] = total.astype(BF16)
        lax.fori_loop(part * each // 2, (part + 1) * each // 2, backward, 0)
        for kind in (PARTNER, DIAG, MATE):
            for out, into in ((back_k, came_k), (back_v, came_v)):
                returned.append(
                    send(out.at[span_of(kind), cols], into.at[span_of(kind), cols], to(kind))
                )
    came_k[0:far_rows, :] = back_k[0:far_rows, :]
    came_v[0:far_rows, :] = back_v[0:far_rows, :]
    attn_diag = []
    for chunk in range(chunks):
        attn_partner[chunk].wait_recv()
        held = attn.at[PARTNER, :, chunk_cols(chunk)]
        attn_diag.append(send(held, attn.at[DIAG, :, chunk_cols(chunk)], to(MATE)))
    columns_in[MATE].wait_recv()
    for copy in swapped:
        copy.wait_recv()
    for kind in range(4):
        columns_t[kind] = columns[kind].T
    for copy in attn_mate + attn_diag:
        copy.wait_recv()

    def weight_part(cols):
        total = dot(columns_t[SELF], attn[SELF, :, cols])
        for kind in (MATE, PARTNER, DIAG):
            total += dot(columns_t[kind], attn[kind, :, cols])
        dw_ref[:, cols] = total

    tiled(weight_part)

    per_part = len(returned) // (2 * chunks)
    for part in range(2 * chunks):
        for copy in returned[part * per_part : (part + 1) * per_part]:
            copy.wait_recv()
        cols = pl.ds(part * step_width, step_width)
        dk_ref[:, cols] = (own_k[:, cols] + dotx(pick[...], came_k[:, cols], TN)).astype(BF16)
        dv_ref[:, cols] = (own_v[:, cols] + dotx(pick[...], came_v[:, cols], TN)).astype(BF16)
    for copy in started:
        copy.wait_send()
    for chunk in range(chunks):
        for step in range(line - 1):
            for upward in (True, False):

                @pl.when(hop_sent(step, upward))
                def left():
                    hop(chunk, step, upward).wait_send()

    for chunk in range(chunks):
        relay_done(chunk, False)


def finish_kernel(dq_ref, dk_ref, dv_ref, dw_ref, dq_out, dk_out, dv_out, dw_out, sem):
    parts = 4
    piece = dw_ref.shape[0] // parts
    pairs = [
        (dw_ref.at[pl.ds(i * piece, piece)], dw_out.at[pl.ds(i * piece, piece)])
        for i in range(parts)
    ]
    pairs += [(dq_ref, dq_out), (dk_ref, dk_out), (dv_ref, dv_out)]
    copies = [
        pltpu.make_async_copy(source, target, sem.at[number])
        for number, (source, target) in enumerate(pairs)
    ]
    for copy in copies:
        copy.start()
    for copy in copies:
        copy.wait()


def finish(dq, dk, dv, dw):
    rows, width = dq.shape
    depth = dw.shape[0]
    vmem = pl.BlockSpec(memory_space=pltpu.VMEM)
    hbm = pl.BlockSpec(memory_space=pltpu.HBM)
    return pl.pallas_call(
        finish_kernel,
        out_shape=[jax.ShapeDtypeStruct((rows, width), BF16)] * 3
        + [jax.ShapeDtypeStruct((depth, width), F32)],
        in_specs=[vmem] * 4,
        out_specs=[hbm] * 4,
        scratch_shapes=[pltpu.SemaphoreType.DMA((7,))],
        compiler_params=pltpu.CompilerParams(vmem_limit_bytes=16 * 1024 * 1024),
        cost_estimate=pl.CostEstimate(flops=0, bytes_accessed=7 * 10**6, transcendentals=0),
    )(dq, dk, dv, dw)


def fused(queries, keys, values, out_grad, out_weight, lists):
    frames, frame_tokens, width = queries.shape
    rows = frames * frame_tokens
    depth = out_weight.shape[0]
    slots = RET // 4
    heads = width // HD
    flat = [x.reshape(rows, width) for x in (queries, keys, values, out_grad)]
    line = lax.axis_size("dp")
    hbm = pl.BlockSpec(memory_space=pltpu.HBM)
    far = 4 * slots * frame_tokens

    def low(*shape):
        return pltpu.VMEM(shape, BF16)

    def wide(*shape):
        return pltpu.VMEM(shape, F32)

    dq, dk, dv, dw = pl.pallas_call(
        functools.partial(fused_kernel, slots, line),
        out_shape=[pltpu.VMEM((rows, width), BF16)] * 3 + [pltpu.VMEM((depth, width), F32)],
        in_specs=[pl.BlockSpec(memory_space=pltpu.SMEM)] + [hbm] * 5,
        out_specs=[pl.BlockSpec(memory_space=pltpu.VMEM)] * 4,
        scratch_shapes=[
            low(rows, width),
            low(rows, width),
            low(rows, width),
            low(depth, width),
            pltpu.VMEM((lists.size, 128), jnp.int32),
            pltpu.VMEM((4, lists.size, 128), jnp.int32),
            low(4 * frame_tokens, rows),
            low(far, rows),
            low(far, width),
            low(far, width),
            low(far, width),
            low(far, width),
            low(2, 2, rows, depth),
            low(4, rows, depth),
            low(4, depth, rows),
            low(4, 2, depth, width // 2),
            low(rows, width),
            low(4, rows, width),
            wide(heads, rows, CF * frame_tokens + far),
            wide(rows, width),
            wide(rows, width),
            low(far, width),
            low(far, width),
            low(far, width),
            low(far, width),
            pltpu.SemaphoreType.DMA((64,)),
            pltpu.SemaphoreType.DMA((64,)),
            pltpu.SemaphoreType.DMA((2, line - 1)),
            pltpu.SemaphoreType.DMA((2, line - 1)),
            pltpu.SemaphoreType.DMA((2, line - 1)),
            pltpu.SemaphoreType.DMA((2, line - 1)),
            pltpu.SemaphoreType.DMA((6,)),
            pltpu.SemaphoreType.DMA((2, 2 * (line - 1))),
            pltpu.SemaphoreType.DMA((2, 2 * (line - 1))),
        ],
        compiler_params=pltpu.CompilerParams(
            collective_id=0, has_side_effects=True, vmem_limit_bytes=50 * 1024 * 1024
        ),
        cost_estimate=pl.CostEstimate(
            flops=7 * 10**9, bytes_accessed=16 * 10**6, transcendentals=10**6
        ),
    )(lists, *flat, out_weight)
    dq, dk, dv, dw = finish(dq, dk, dv, dw)
    back = [x.reshape(frames, frame_tokens, width) for x in (dq, dk, dv)]
    return (*back, dw)


def solution(mesh):
    whole_fits = dict(mesh.shape) == {"dp": 4, "tm": 4, "head": 2}
    return jax.shard_map(
        fused if whole_fits else per_device,
        mesh=mesh,
        in_specs=(
            P(("dp", "tm"), None, "head"),
            P(("dp", "tm"), None, "head"),
            P(("dp", "tm"), None, "head"),
            P(("dp", "tm"), None, "head"),
            P("tm", "head"),
            P(("dp", "tm"), None),
        ),
        out_specs=(
            P(("dp", "tm"), None, "head"),
            P(("dp", "tm"), None, "head"),
            P(("dp", "tm"), None, "head"),
            P(("dp", "tm"), "head"),
        ),
        check_vma=False,
    )
```

```python
import functools

import jax
import jax.numpy as jnp
from jax import lax
from jax.experimental import pallas as pl
from jax.experimental.pallas import tpu as pltpu
from jax.sharding import PartitionSpec as P

HD = 128
CF = 4
RET = 8


def slot_tables(owners, local_frame, slot_index, occupied, myself, capacity):
    slot_range = jnp.arange(capacity, dtype=jnp.int32)
    matches = (
        occupied[:, None, :]
        & (owners[:, None, :] == myself)
        & (slot_index[:, None, :] == slot_range[None, :, None])
    )
    source = jnp.sum(jnp.where(matches, local_frame[:, None, :], 0), axis=2)
    filled = jnp.any(matches, axis=2)
    return (source.reshape(-1), filled.reshape(-1))


def pack_slots(frame_rows, source, filled):
    picked = jnp.take(frame_rows, source, axis=0)
    return jnp.where(filled[:, None, None], picked, jnp.zeros_like(picked))


def per_device(queries, keys, values, out_grad, out_weight, lists):
    frames_dev, frame_tokens, width = queries.shape
    heads_dev = width // HD
    tm_count = lax.axis_size("tm")
    myself = lax.axis_index("tm")
    groups_dev = frames_dev // CF
    entry_count = groups_dev * RET
    token_rows = frames_dev * frame_tokens
    group_rows = CF * frame_tokens
    score_factor = HD ** (-0.5)
    per_owner = max(1, RET // tm_count)
    every_list = lax.all_gather(lists, "tm", axis=0, tiled=True)
    wanted = every_list.reshape(tm_count, entry_count)
    owners = wanted // frames_dev
    local_frame = wanted - owners * frames_dev
    position = jnp.arange(entry_count, dtype=jnp.int32)
    before = (position[:, None] < position[None, :])[None]
    same_owner = owners[:, :, None] == owners[:, None, :]
    same_frame = wanted[:, :, None] == wanted[:, None, :]
    first_seen = jnp.logical_not(jnp.any(same_frame & before, axis=1))
    entry_slot = jnp.sum(same_owner & before, axis=1)
    frame_first = jnp.sum(same_owner & before & first_seen[:, :, None], axis=1)
    frame_slot = jnp.sum(
        jnp.where(same_frame & first_seen[:, :, None], frame_first[:, :, None], 0), axis=1
    )
    my_owner = lax.dynamic_index_in_dim(owners, myself, 0, keepdims=False)
    my_entry_slot = lax.dynamic_index_in_dim(entry_slot, myself, 0, keepdims=False)
    my_frame_slot = lax.dynamic_index_in_dim(frame_slot, myself, 0, keepdims=False)
    frame_source, frame_filled = slot_tables(
        owners, local_frame, frame_slot, first_seen, myself, per_owner
    )
    capacity = groups_dev * per_owner
    source, filled = slot_tables(
        owners, local_frame, entry_slot, jnp.ones_like(first_seen), myself, capacity
    )
    got_keys, got_values = (
        lax.all_to_all(
            pack_slots(keys, source, filled), "tm", split_axis=0, concat_axis=0, tiled=True
        ),
        lax.all_to_all(
            pack_slots(values, source, filled), "tm", split_axis=0, concat_axis=0, tiled=True
        ),
    )
    lookup = my_owner * capacity + my_entry_slot
    grad_full = lax.all_gather(out_grad, "head", axis=2, tiled=True)
    grad_rows = grad_full.reshape(token_rows, grad_full.shape[2])
    columns = grad_rows
    attn_grad = jnp.dot(
        columns,
        lax.all_gather(out_weight, "tm", axis=0, tiled=True),
        preferred_element_type=jnp.float32,
    ).astype(jnp.bfloat16)
    far_keys = jnp.take(got_keys, lookup, axis=0)
    far_values = jnp.take(got_values, lookup, axis=0)
    far_span = RET * frame_tokens
    query_blocks = queries.reshape(groups_dev, group_rows, heads_dev, HD)
    key_set = jnp.concatenate(
        [
            keys.reshape(groups_dev, group_rows, heads_dev, HD),
            far_keys.reshape(groups_dev, far_span, heads_dev, HD),
        ],
        axis=1,
    )
    value_set = jnp.concatenate(
        [
            values.reshape(groups_dev, group_rows, heads_dev, HD),
            far_values.reshape(groups_dev, far_span, heads_dev, HD),
        ],
        axis=1,
    )
    scores = (
        jnp.einsum("cqhd,ckhd->chqk", query_blocks, key_set, preferred_element_type=jnp.float32)
        * score_factor
    )
    row_top = jnp.max(scores, axis=3, keepdims=True)
    weighted = jnp.exp(scores - row_top)
    prob = weighted / jnp.sum(weighted, axis=3, keepdims=True)
    prob_low = prob.astype(jnp.bfloat16)
    attn_out = jnp.einsum(
        "chqk,ckhd->cqhd", prob_low, value_set, preferred_element_type=jnp.float32
    ).astype(jnp.bfloat16)
    grad_blocks = attn_grad.reshape(groups_dev, group_rows, heads_dev, HD)
    row_dot = jnp.sum(grad_blocks.astype(jnp.float32) * attn_out.astype(jnp.float32), axis=3)
    row_dot = jnp.transpose(row_dot, (0, 2, 1))[..., None]
    prob_grad = jnp.einsum(
        "cqhd,ckhd->chqk", grad_blocks, value_set, preferred_element_type=jnp.float32
    )
    score_grad = (prob * (prob_grad - row_dot)).astype(jnp.bfloat16)
    query_grad = (
        jnp.einsum("chqk,ckhd->cqhd", score_grad, key_set, preferred_element_type=jnp.float32)
        * score_factor
    ).astype(jnp.bfloat16)
    key_term = (
        jnp.einsum("chqk,cqhd->ckhd", score_grad, query_blocks, preferred_element_type=jnp.float32)
        * score_factor
    )
    value_term = jnp.einsum(
        "chqk,cqhd->ckhd", prob_low, grad_blocks, preferred_element_type=jnp.float32
    )
    own_dk = key_term[:, :group_rows].reshape(frames_dev, frame_tokens, width)
    own_dv = value_term[:, :group_rows].reshape(frames_dev, frame_tokens, width)
    far_dk = key_term[:, group_rows:].reshape(entry_count, frame_tokens, width)
    far_dv = value_term[:, group_rows:].reshape(entry_count, frame_tokens, width)
    back_slot = my_owner * per_owner + my_frame_slot
    empty = jnp.zeros((tm_count * per_owner, frame_tokens, width), jnp.float32)
    back_keys = empty.at[back_slot].add(far_dk).astype(jnp.bfloat16)
    back_values = empty.at[back_slot].add(far_dv).astype(jnp.bfloat16)
    came_keys, came_values = (
        lax.all_to_all(back_keys, "tm", split_axis=0, concat_axis=0, tiled=True),
        lax.all_to_all(back_values, "tm", split_axis=0, concat_axis=0, tiled=True),
    )
    selector = (
        (frame_source[None, :] == jnp.arange(frames_dev, dtype=jnp.int32)[:, None])
        & frame_filled[None, :]
    ).astype(jnp.bfloat16)
    into_keys = jnp.dot(
        selector, came_keys.reshape(tm_count * per_owner, -1), preferred_element_type=jnp.float32
    )
    into_values = jnp.dot(
        selector, came_values.reshape(tm_count * per_owner, -1), preferred_element_type=jnp.float32
    )
    key_grad = (own_dk + into_keys.reshape(frames_dev, frame_tokens, width)).astype(jnp.bfloat16)
    value_grad = (own_dv + into_values.reshape(frames_dev, frame_tokens, width)).astype(
        jnp.bfloat16
    )
    attn_rows = attn_out.reshape(token_rows, width)
    columns = grad_rows
    weight_grad = lax.psum_scatter(
        lax.dot_general(
            columns, attn_rows, (((0,), (0,)), ((), ())), preferred_element_type=jnp.float32
        ).astype(jnp.bfloat16),
        "tm",
        scatter_dimension=0,
        tiled=True,
    ).astype(jnp.float32)
    return (query_grad.reshape(frames_dev, frame_tokens, width), key_grad, value_grad, weight_grad)


SELF, MATE, PARTNER, DIAG = 0, 1, 2, 3
F32 = jnp.float32
BF16 = jnp.bfloat16
NT = (((1,), (1,)), ((), ()))
TN = (((0,), (0,)), ((), ()))


def dot(a, b):
    return jnp.dot(a, b, preferred_element_type=F32)


def dotx(a, b, dims):
    return lax.dot_general(a, b, dims, preferred_element_type=F32)


def fused_kernel(
    slots, line, lists_ref, q_hbm, k_hbm, v_hbm, og_hbm, w_hbm,
    dq_ref, dk_ref, dv_ref, dw_ref,
    q_ref, k_ref, v_ref, w_ref,
    my_list, every_list, present, pick, send_k, send_v, far_k, far_v, og_halves, columns,
    columns_t, w_in, grad, attn, prob,
    own_k, own_v, back_k, back_v, came_k, came_v,
    send_sem, recv_sem, up_send, up_recv, down_send, down_recv, load_sem,
    relay_send, relay_recv,
):
    rows, width = q_ref.shape
    heads = width // HD
    entries, lanes = my_list.shape
    frame_tokens = 32
    group_rows = CF * frame_tokens
    groups = rows // group_rows
    far_rows = slots * frame_tokens
    depth = w_ref.shape[0]
    chunks = 2
    span_width = width // chunks
    piece = depth // line
    half_rows = rows // 2
    scale = HD ** (-0.5)
    t = lax.axis_index("tm")
    h = lax.axis_index("head")
    z = lax.axis_index("dp")
    mate = t + 1 - 2 * (t % 2)
    partner = (t + 2) % 4
    diag = (mate + 2) % 4
    peers = (t, mate, partner, diag)

    barrier = pltpu.get_barrier_semaphore()
    for kind in (MATE, PARTNER, DIAG):
        pl.semaphore_signal(barrier, inc=1, device_id={"tm": peers[kind]})
    pl.semaphore_signal(barrier, inc=1, device_id={"head": 1 - h})

    @pl.when(z > 0)
    def greet_below():
        pl.semaphore_signal(barrier, inc=1, device_id={"dp": z - 1})

    @pl.when(z < line - 1)
    def greet_above():
        pl.semaphore_signal(barrier, inc=1, device_id={"dp": z + 1})

    loads = []
    for source, target in (
        (k_hbm, k_ref),
        (v_hbm, v_ref),
        (og_hbm.at[:, pl.ds(0, depth)], og_halves.at[h, 0]),
        (og_hbm.at[:, pl.ds(depth, depth)], og_halves.at[h, 1]),
        (q_hbm, q_ref),
        (w_hbm, w_ref),
    ):
        loads.append(pltpu.make_async_copy(source, target, load_sem.at[len(loads)]))
        loads[-1].start()
    load_k, load_v, load_og0, load_og1, load_q, load_w = loads

    for entry in range(entries):
        named = lists_ref[entry // RET, entry % RET]
        my_list[entry : entry + 1, :] = jnp.full((1, lanes), named, jnp.int32)
        every_list[SELF, entry : entry + 1, :] = jnp.full((1, lanes), named, jnp.int32)
    sides = (z + line - 1) // line + (2 * line - 2 - z) // line
    pl.semaphore_wait(barrier, 4 + sides)

    started = []

    def send(src, dst, target):
        number = len(started)
        copy = pltpu.make_async_remote_copy(
            src_ref=src, dst_ref=dst, send_sem=send_sem.at[number], recv_sem=recv_sem.at[number],
            device_id=target,
        )
        copy.start()
        started.append(copy)
        return copy

    def to(kind):
        return {"tm": peers[kind]}

    lists_in = [
        send(my_list, every_list.at[kind], to(kind)) for kind in (PARTNER, DIAG, MATE)
    ]

    def chunk_cols(chunk):
        return pl.ds(chunk * span_width, span_width)

    def piece_rows(index):
        return pl.ds(pl.multiple_of(index * piece, piece), piece)

    crossing = []
    for chunk in range(chunks):
        crossing.append(
            send(
                w_hbm.at[piece_rows(z), chunk_cols(chunk)],
                w_in.at[PARTNER, chunk, piece_rows(z)],
                to(PARTNER),
            )
        )
    def hop(chunk, step, upward):
        move = 1 if upward else -1
        index = z - step if upward else z + step
        index = jnp.clip(index, 0, line - 1)
        held = w_in.at[PARTNER, chunk, piece_rows(index)]
        sends, recvs = (up_send, up_recv) if upward else (down_send, down_recv)
        return pltpu.make_async_remote_copy(
            src_ref=held, dst_ref=held, send_sem=sends.at[chunk, step],
            recv_sem=recvs.at[chunk, step], device_id={"dp": z + move},
        )

    def hop_sent(step, upward):
        if upward:
            return (z - step >= 0) & (z < line - 1)
        return (z + step < line) & (z > 0)

    def hop_received(step, upward):
        if upward:
            return z - 1 - step >= 0
        return z + 1 + step < line

    def relay(chunk, step, upward):
        index = jnp.clip(z - 1 - step if upward else z + 1 + step, 0, line - 1)
        place = 2 * step + (0 if upward else 1)
        return pltpu.make_async_remote_copy(
            src_ref=w_in.at[PARTNER, chunk, piece_rows(index)],
            dst_ref=w_in.at[DIAG, chunk, piece_rows(index)],
            send_sem=relay_send.at[chunk, place], recv_sem=relay_recv.at[chunk, place],
            device_id=to(MATE),
        )

    def relay_done(chunk, received):
        for step in range(line - 1):
            for upward in (True, False):

                @pl.when(hop_received(step, upward))
                def done():
                    if received:
                        relay(chunk, step, upward).wait_recv()
                    else:
                        relay(chunk, step, upward).wait_send()

    def hop_wait(chunk, step):
        for upward in (True, False):

            @pl.when(hop_received(step, upward))
            def arrived():
                hop(chunk, step, upward).wait_recv()
                relay(chunk, step, upward).start()

    diag_w = []

    def hop_start(chunk, step):
        if step == 0:
            crossing[chunk].wait_recv()
        else:
            hop_wait(chunk, step - 1)
        for upward in (True, False):

            @pl.when(hop_sent(step, upward))
            def onward():
                hop(chunk, step, upward).start()

        if step == 0:
            diag_w.append(
                send(
                    w_in.at[PARTNER, chunk, piece_rows(z)],
                    w_in.at[DIAG, chunk, piece_rows(z)],
                    to(MATE),
                )
            )

    halves_in = []
    for part in range(2):
        halves_in.append(
            send(
                og_hbm.at[:, pl.ds(part * depth, depth)], og_halves.at[h, part], {"head": 1 - h}
            )
        )
    for copy in lists_in:
        copy.wait_recv()

    lane_frame = lax.shift_right_logical(
        lax.broadcasted_iota(jnp.int32, (entries, lanes), 1), 5
    )
    for side in range(rows // lanes):
        my_frame = (t * rows + side * lanes) // frame_tokens + lane_frame
        for kind in range(4):
            named = jnp.max((every_list[kind] == my_frame).astype(F32), axis=0, keepdims=True)
            present[
                kind * frame_tokens : (kind + 1) * frame_tokens,
                side * lanes : (side + 1) * lanes,
            ] = jnp.broadcast_to(named, (frame_tokens, lanes)).astype(BF16)
    above = lax.broadcasted_iota(jnp.int32, (rows, rows), 0)
    below = lax.broadcasted_iota(jnp.int32, (rows, rows), 1)
    earlier = (
        ((above & 31) == 0)
        & (lax.shift_right_logical(above, 5) < lax.shift_right_logical(below, 5))
    ).astype(F32).astype(BF16)
    rank = dot(present[...], earlier)
    token = lax.broadcasted_iota(jnp.int32, (frame_tokens, rows), 0)
    column_token = lax.broadcasted_iota(jnp.int32, (frame_tokens, rows), 1) & 31
    same_token = (token == column_token).astype(F32)
    for kind in range(4):
        span = slice(kind * frame_tokens, (kind + 1) * frame_tokens)
        here = present[span, :].astype(F32) * same_token
        for slot in range(slots):
            first = (kind * slots + slot) * frame_tokens
            pick[first : first + frame_tokens, :] = (
                here * (rank[span, :] == slot).astype(F32)
            ).astype(BF16)

    tile = 512

    def tiled(body):
        def step(i, carry):
            body(pl.ds(pl.multiple_of(i * tile, tile), tile))
            return carry

        lax.fori_loop(0, width // tile, step, 0)

    def span_of(kind):
        return pl.ds(kind * far_rows, far_rows)

    def pick_keys(cols):
        send_k[:, cols] = dot(pick[...], k_ref[:, cols]).astype(BF16)

    def pick_values(cols):
        send_v[:, cols] = dot(pick[...], v_ref[:, cols]).astype(BF16)

    frames_in = []
    load_k.wait()
    tiled(pick_keys)
    for kind in (PARTNER, DIAG, MATE):
        frames_in.append(send(send_k.at[span_of(kind)], far_k.at[span_of(kind)], to(kind)))
    load_v.wait()
    tiled(pick_values)
    for kind in (PARTNER, DIAG, MATE):
        frames_in.append(send(send_v.at[span_of(kind)], far_v.at[span_of(kind)], to(kind)))
    far_k[0:far_rows, :] = send_k[0:far_rows, :]
    far_v[0:far_rows, :] = send_v[0:far_rows, :]


    hop_start(0, 0)
    hop_start(0, 1)
    load_og0.wait()
    load_og1.wait()
    for copy in halves_in:
        copy.wait_recv()
    mine = pl.ds(pl.multiple_of(h * half_rows, half_rows), half_rows)
    columns_in = {}
    for kind in (PARTNER, DIAG):
        peer = peers[kind]
        columns_in[kind] = send(
            og_halves.at[peer // 2, peer % 2, mine], columns.at[kind, mine], to(kind)
        )
    columns_in[MATE] = send(og_halves.at[mate // 2, mate % 2], columns.at[MATE], to(MATE))
    columns[SELF] = og_halves[t // 2, t % 2]
    hop_start(0, 2)
    hop_start(1, 0)
    mate_w = [
        send(w_hbm.at[:, chunk_cols(chunk)], w_in.at[MATE, chunk], to(MATE))
        for chunk in range(chunks)
    ]
    hop_start(1, 1)

    load_q.wait()
    for copy in frames_in:
        copy.wait_recv()

    spans = [slice(g * group_rows, (g + 1) * group_rows) for g in range(groups)]

    def by_group(product):
        return jnp.concatenate([product(span) for span in spans], axis=0)

    def forward_head(i):
        cols = pl.ds(pl.multiple_of(i * HD, HD), HD)
        near = by_group(lambda span: dotx(q_ref[span, cols], k_ref[span, cols], NT)) * scale
        far = dotx(q_ref[:, cols], far_k[:, cols], NT) * scale
        top = jnp.maximum(
            jnp.max(near, axis=1, keepdims=True), jnp.max(far, axis=1, keepdims=True)
        )
        near = jnp.exp(near - top)
        far = jnp.exp(far - top)
        total = jnp.sum(near, axis=1, keepdims=True) + jnp.sum(far, axis=1, keepdims=True)
        near = near / total
        far = far / total
        prob[i, :, 0:group_rows] = near
        prob[i, :, group_rows:] = far
        near_low = near.astype(BF16)
        out = by_group(lambda span: dot(near_low[span], v_ref[span, cols]))
        attn[SELF, :, cols] = (out + dot(far.astype(BF16), far_v[:, cols])).astype(BF16)

    together = 3

    def several(head):
        def body(i, carry):
            for place in range(together):
                head(i * together + place)
            return carry

        return body

    forward = several(forward_head)
    each = heads // chunks
    attn_partner = []
    attn_mate = []
    for chunk in range(chunks):
        lax.fori_loop(chunk * each // together, (chunk + 1) * each // together, forward, 0)
        own = attn.at[SELF, :, chunk_cols(chunk)]
        attn_mate.append(send(own, attn.at[MATE, :, chunk_cols(chunk)], to(MATE)))
        attn_partner.append(send(own, attn.at[PARTNER, :, chunk_cols(chunk)], to(PARTNER)))
        if chunk == 0:
            hop_start(1, 2)
            hop_wait(0, 2)
    swapped = []
    for kind in (PARTNER, DIAG):
        columns_in[kind].wait_recv()
        swapped.append(send(columns.at[kind, mine], columns.at[kind, mine], {"head": 1 - h}))

    def backward_head(i):
        cols = pl.ds(pl.multiple_of(i * HD, HD), HD)
        q = q_ref[:, cols]
        do = grad[:, cols]
        row_dot = jnp.sum(
            do.astype(F32) * attn[SELF, :, cols].astype(F32), axis=1, keepdims=True
        )
        near = prob[i, :, 0:group_rows]
        far = prob[i, :, group_rows:]
        near_dp = by_group(lambda span: dotx(do[span], v_ref[span, cols], NT))
        near_ds = (near * (near_dp - row_dot)).astype(BF16)
        far_ds = (far * (dotx(do, far_v[:, cols], NT) - row_dot)).astype(BF16)
        near_p = near.astype(BF16)
        near_dq = by_group(lambda span: dot(near_ds[span], k_ref[span, cols]))
        dq_ref[:, cols] = ((near_dq + dot(far_ds, far_k[:, cols])) * scale).astype(BF16)
        own_k[:, cols] = by_group(lambda span: dotx(near_ds[span], q[span], TN)) * scale
        own_v[:, cols] = by_group(lambda span: dotx(near_p[span], do[span], TN))
        back_k[:, cols] = (dotx(far_ds, q, TN) * scale).astype(BF16)
        back_v[:, cols] = dotx(far.astype(BF16), do, TN).astype(BF16)

    backward = several(backward_head)
    load_w.wait()
    returned = []
    step_width = span_width // 2
    for part in range(2 * chunks):
        chunk = part // 2
        if part % 2 == 0:
            if chunk == 1:
                hop_wait(1, 2)
            mate_w[chunk].wait_recv()
            diag_w[chunk].wait_recv()
            relay_done(chunk, True)
        local = pl.ds(part % 2 * step_width, step_width)
        cols = pl.ds(part * step_width, step_width)
        total = dot(og_halves[t // 2, t % 2], w_ref[:, cols])
        for kind in (MATE, PARTNER, DIAG):
            peer = peers[kind]
            total += dot(og_halves[peer // 2, peer % 2], w_in[kind, chunk, :, local])
        grad[:, cols] = total.astype(BF16)
        lax.fori_loop(
            part * each // 2 // together, (part + 1) * each // 2 // together, backward, 0
        )
        for kind in (PARTNER, DIAG, MATE):
            for out, into in ((back_k, came_k), (back_v, came_v)):
                returned.append(
                    send(out.at[span_of(kind), cols], into.at[span_of(kind), cols], to(kind))
                )
    came_k[0:far_rows, :] = back_k[0:far_rows, :]
    came_v[0:far_rows, :] = back_v[0:far_rows, :]
    attn_diag = []
    for chunk in range(chunks):
        attn_partner[chunk].wait_recv()
        held = attn.at[PARTNER, :, chunk_cols(chunk)]
        attn_diag.append(send(held, attn.at[DIAG, :, chunk_cols(chunk)], to(MATE)))
    columns_in[MATE].wait_recv()
    for copy in swapped:
        copy.wait_recv()
    for kind in range(4):
        columns_t[kind] = columns[kind].T
    for copy in attn_mate + attn_diag:
        copy.wait_recv()

    def weight_part(cols):
        total = dot(columns_t[SELF], attn[SELF, :, cols])
        for kind in (MATE, PARTNER, DIAG):
            total += dot(columns_t[kind], attn[kind, :, cols])
        dw_ref[:, cols] = total

    tiled(weight_part)

    per_part = len(returned) // (2 * chunks)
    for part in range(2 * chunks):
        for copy in returned[part * per_part : (part + 1) * per_part]:
            copy.wait_recv()
        cols = pl.ds(part * step_width, step_width)
        dk_ref[:, cols] = (own_k[:, cols] + dotx(pick[...], came_k[:, cols], TN)).astype(BF16)
        dv_ref[:, cols] = (own_v[:, cols] + dotx(pick[...], came_v[:, cols], TN)).astype(BF16)
    for copy in started:
        copy.wait_send()
    for chunk in range(chunks):
        for step in range(line - 1):
            for upward in (True, False):

                @pl.when(hop_sent(step, upward))
                def left():
                    hop(chunk, step, upward).wait_send()

    for chunk in range(chunks):
        relay_done(chunk, False)


def finish_kernel(dq_ref, dk_ref, dv_ref, dw_ref, dq_out, dk_out, dv_out, dw_out, sem):
    parts = 4
    piece = dw_ref.shape[0] // parts
    pairs = [
        (dw_ref.at[pl.ds(i * piece, piece)], dw_out.at[pl.ds(i * piece, piece)])
        for i in range(parts)
    ]
    pairs += [(dq_ref, dq_out), (dk_ref, dk_out), (dv_ref, dv_out)]
    copies = [
        pltpu.make_async_copy(source, target, sem.at[number])
        for number, (source, target) in enumerate(pairs)
    ]
    for copy in copies:
        copy.start()
    for copy in copies:
        copy.wait()


def finish(dq, dk, dv, dw):
    rows, width = dq.shape
    depth = dw.shape[0]
    vmem = pl.BlockSpec(memory_space=pltpu.VMEM)
    hbm = pl.BlockSpec(memory_space=pltpu.HBM)
    return pl.pallas_call(
        finish_kernel,
        out_shape=[jax.ShapeDtypeStruct((rows, width), BF16)] * 3
        + [jax.ShapeDtypeStruct((depth, width), F32)],
        in_specs=[vmem] * 4,
        out_specs=[hbm] * 4,
        scratch_shapes=[pltpu.SemaphoreType.DMA((7,))],
        compiler_params=pltpu.CompilerParams(vmem_limit_bytes=16 * 1024 * 1024),
        cost_estimate=pl.CostEstimate(flops=0, bytes_accessed=7 * 10**6, transcendentals=0),
    )(dq, dk, dv, dw)


def fused(queries, keys, values, out_grad, out_weight, lists):
    frames, frame_tokens, width = queries.shape
    rows = frames * frame_tokens
    depth = out_weight.shape[0]
    slots = RET // 4
    heads = width // HD
    flat = [x.reshape(rows, width) for x in (queries, keys, values, out_grad)]
    line = lax.axis_size("dp")
    hbm = pl.BlockSpec(memory_space=pltpu.HBM)
    far = 4 * slots * frame_tokens

    def low(*shape):
        return pltpu.VMEM(shape, BF16)

    def wide(*shape):
        return pltpu.VMEM(shape, F32)

    dq, dk, dv, dw = pl.pallas_call(
        functools.partial(fused_kernel, slots, line),
        out_shape=[pltpu.VMEM((rows, width), BF16)] * 3 + [pltpu.VMEM((depth, width), F32)],
        in_specs=[pl.BlockSpec(memory_space=pltpu.SMEM)] + [hbm] * 5,
        out_specs=[pl.BlockSpec(memory_space=pltpu.VMEM)] * 4,
        scratch_shapes=[
            low(rows, width),
            low(rows, width),
            low(rows, width),
            low(depth, width),
            pltpu.VMEM((lists.size, 128), jnp.int32),
            pltpu.VMEM((4, lists.size, 128), jnp.int32),
            low(4 * frame_tokens, rows),
            low(far, rows),
            low(far, width),
            low(far, width),
            low(far, width),
            low(far, width),
            low(2, 2, rows, depth),
            low(4, rows, depth),
            low(4, depth, rows),
            low(4, 2, depth, width // 2),
            low(rows, width),
            low(4, rows, width),
            wide(heads, rows, CF * frame_tokens + far),
            wide(rows, width),
            wide(rows, width),
            low(far, width),
            low(far, width),
            low(far, width),
            low(far, width),
            pltpu.SemaphoreType.DMA((64,)),
            pltpu.SemaphoreType.DMA((64,)),
            pltpu.SemaphoreType.DMA((2, line - 1)),
            pltpu.SemaphoreType.DMA((2, line - 1)),
            pltpu.SemaphoreType.DMA((2, line - 1)),
            pltpu.SemaphoreType.DMA((2, line - 1)),
            pltpu.SemaphoreType.DMA((6,)),
            pltpu.SemaphoreType.DMA((2, 2 * (line - 1))),
            pltpu.SemaphoreType.DMA((2, 2 * (line - 1))),
        ],
        compiler_params=pltpu.CompilerParams(
            collective_id=0, has_side_effects=True, vmem_limit_bytes=50 * 1024 * 1024
        ),
        cost_estimate=pl.CostEstimate(
            flops=7 * 10**9, bytes_accessed=16 * 10**6, transcendentals=10**6
        ),
    )(lists, *flat, out_weight)
    dq, dk, dv, dw = finish(dq, dk, dv, dw)
    back = [x.reshape(frames, frame_tokens, width) for x in (dq, dk, dv)]
    return (*back, dw)


def solution(mesh):
    whole_fits = dict(mesh.shape) == {"dp": 4, "tm": 4, "head": 2}
    return jax.shard_map(
        fused if whole_fits else per_device,
        mesh=mesh,
        in_specs=(
            P(("dp", "tm"), None, "head"),
            P(("dp", "tm"), None, "head"),
            P(("dp", "tm"), None, "head"),
            P(("dp", "tm"), None, "head"),
            P("tm", "head"),
            P(("dp", "tm"), None),
        ),
        out_specs=(
            P(("dp", "tm"), None, "head"),
            P(("dp", "tm"), None, "head"),
            P(("dp", "tm"), None, "head"),
            P(("dp", "tm"), "head"),
        ),
        check_vma=False,
    )
```

```python
import functools

import jax
import jax.numpy as jnp
from jax import lax
from jax.experimental import pallas as pl
from jax.experimental.pallas import tpu as pltpu
from jax.sharding import PartitionSpec as P

HD = 128
CF = 4
RET = 8


def slot_tables(owners, local_frame, slot_index, occupied, myself, capacity):
    slot_range = jnp.arange(capacity, dtype=jnp.int32)
    matches = (
        occupied[:, None, :]
        & (owners[:, None, :] == myself)
        & (slot_index[:, None, :] == slot_range[None, :, None])
    )
    source = jnp.sum(jnp.where(matches, local_frame[:, None, :], 0), axis=2)
    filled = jnp.any(matches, axis=2)
    return (source.reshape(-1), filled.reshape(-1))


def pack_slots(frame_rows, source, filled):
    picked = jnp.take(frame_rows, source, axis=0)
    return jnp.where(filled[:, None, None], picked, jnp.zeros_like(picked))


def per_device(queries, keys, values, out_grad, out_weight, lists):
    frames_dev, frame_tokens, width = queries.shape
    heads_dev = width // HD
    tm_count = lax.axis_size("tm")
    myself = lax.axis_index("tm")
    groups_dev = frames_dev // CF
    entry_count = groups_dev * RET
    token_rows = frames_dev * frame_tokens
    group_rows = CF * frame_tokens
    score_factor = HD ** (-0.5)
    per_owner = max(1, RET // tm_count)
    every_list = lax.all_gather(lists, "tm", axis=0, tiled=True)
    wanted = every_list.reshape(tm_count, entry_count)
    owners = wanted // frames_dev
    local_frame = wanted - owners * frames_dev
    position = jnp.arange(entry_count, dtype=jnp.int32)
    before = (position[:, None] < position[None, :])[None]
    same_owner = owners[:, :, None] == owners[:, None, :]
    same_frame = wanted[:, :, None] == wanted[:, None, :]
    first_seen = jnp.logical_not(jnp.any(same_frame & before, axis=1))
    entry_slot = jnp.sum(same_owner & before, axis=1)
    frame_first = jnp.sum(same_owner & before & first_seen[:, :, None], axis=1)
    frame_slot = jnp.sum(
        jnp.where(same_frame & first_seen[:, :, None], frame_first[:, :, None], 0), axis=1
    )
    my_owner = lax.dynamic_index_in_dim(owners, myself, 0, keepdims=False)
    my_entry_slot = lax.dynamic_index_in_dim(entry_slot, myself, 0, keepdims=False)
    my_frame_slot = lax.dynamic_index_in_dim(frame_slot, myself, 0, keepdims=False)
    frame_source, frame_filled = slot_tables(
        owners, local_frame, frame_slot, first_seen, myself, per_owner
    )
    capacity = groups_dev * per_owner
    source, filled = slot_tables(
        owners, local_frame, entry_slot, jnp.ones_like(first_seen), myself, capacity
    )
    got_keys, got_values = (
        lax.all_to_all(
            pack_slots(keys, source, filled), "tm", split_axis=0, concat_axis=0, tiled=True
        ),
        lax.all_to_all(
            pack_slots(values, source, filled), "tm", split_axis=0, concat_axis=0, tiled=True
        ),
    )
    lookup = my_owner * capacity + my_entry_slot
    grad_full = lax.all_gather(out_grad, "head", axis=2, tiled=True)
    grad_rows = grad_full.reshape(token_rows, grad_full.shape[2])
    columns = grad_rows
    attn_grad = jnp.dot(
        columns,
        lax.all_gather(out_weight, "tm", axis=0, tiled=True),
        preferred_element_type=jnp.float32,
    ).astype(jnp.bfloat16)
    far_keys = jnp.take(got_keys, lookup, axis=0)
    far_values = jnp.take(got_values, lookup, axis=0)
    far_span = RET * frame_tokens
    query_blocks = queries.reshape(groups_dev, group_rows, heads_dev, HD)
    key_set = jnp.concatenate(
        [
            keys.reshape(groups_dev, group_rows, heads_dev, HD),
            far_keys.reshape(groups_dev, far_span, heads_dev, HD),
        ],
        axis=1,
    )
    value_set = jnp.concatenate(
        [
            values.reshape(groups_dev, group_rows, heads_dev, HD),
            far_values.reshape(groups_dev, far_span, heads_dev, HD),
        ],
        axis=1,
    )
    scores = (
        jnp.einsum("cqhd,ckhd->chqk", query_blocks, key_set, preferred_element_type=jnp.float32)
        * score_factor
    )
    row_top = jnp.max(scores, axis=3, keepdims=True)
    weighted = jnp.exp(scores - row_top)
    prob = weighted / jnp.sum(weighted, axis=3, keepdims=True)
    prob_low = prob.astype(jnp.bfloat16)
    attn_out = jnp.einsum(
        "chqk,ckhd->cqhd", prob_low, value_set, preferred_element_type=jnp.float32
    ).astype(jnp.bfloat16)
    grad_blocks = attn_grad.reshape(groups_dev, group_rows, heads_dev, HD)
    row_dot = jnp.sum(grad_blocks.astype(jnp.float32) * attn_out.astype(jnp.float32), axis=3)
    row_dot = jnp.transpose(row_dot, (0, 2, 1))[..., None]
    prob_grad = jnp.einsum(
        "cqhd,ckhd->chqk", grad_blocks, value_set, preferred_element_type=jnp.float32
    )
    score_grad = (prob * (prob_grad - row_dot)).astype(jnp.bfloat16)
    query_grad = (
        jnp.einsum("chqk,ckhd->cqhd", score_grad, key_set, preferred_element_type=jnp.float32)
        * score_factor
    ).astype(jnp.bfloat16)
    key_term = (
        jnp.einsum("chqk,cqhd->ckhd", score_grad, query_blocks, preferred_element_type=jnp.float32)
        * score_factor
    )
    value_term = jnp.einsum(
        "chqk,cqhd->ckhd", prob_low, grad_blocks, preferred_element_type=jnp.float32
    )
    own_dk = key_term[:, :group_rows].reshape(frames_dev, frame_tokens, width)
    own_dv = value_term[:, :group_rows].reshape(frames_dev, frame_tokens, width)
    far_dk = key_term[:, group_rows:].reshape(entry_count, frame_tokens, width)
    far_dv = value_term[:, group_rows:].reshape(entry_count, frame_tokens, width)
    back_slot = my_owner * per_owner + my_frame_slot
    empty = jnp.zeros((tm_count * per_owner, frame_tokens, width), jnp.float32)
    back_keys = empty.at[back_slot].add(far_dk).astype(jnp.bfloat16)
    back_values = empty.at[back_slot].add(far_dv).astype(jnp.bfloat16)
    came_keys, came_values = (
        lax.all_to_all(back_keys, "tm", split_axis=0, concat_axis=0, tiled=True),
        lax.all_to_all(back_values, "tm", split_axis=0, concat_axis=0, tiled=True),
    )
    selector = (
        (frame_source[None, :] == jnp.arange(frames_dev, dtype=jnp.int32)[:, None])
        & frame_filled[None, :]
    ).astype(jnp.bfloat16)
    into_keys = jnp.dot(
        selector, came_keys.reshape(tm_count * per_owner, -1), preferred_element_type=jnp.float32
    )
    into_values = jnp.dot(
        selector, came_values.reshape(tm_count * per_owner, -1), preferred_element_type=jnp.float32
    )
    key_grad = (own_dk + into_keys.reshape(frames_dev, frame_tokens, width)).astype(jnp.bfloat16)
    value_grad = (own_dv + into_values.reshape(frames_dev, frame_tokens, width)).astype(
        jnp.bfloat16
    )
    attn_rows = attn_out.reshape(token_rows, width)
    columns = grad_rows
    weight_grad = lax.psum_scatter(
        lax.dot_general(
            columns, attn_rows, (((0,), (0,)), ((), ())), preferred_element_type=jnp.float32
        ).astype(jnp.bfloat16),
        "tm",
        scatter_dimension=0,
        tiled=True,
    ).astype(jnp.float32)
    return (query_grad.reshape(frames_dev, frame_tokens, width), key_grad, value_grad, weight_grad)


SELF, MATE, PARTNER, DIAG = 0, 1, 2, 3
F32 = jnp.float32
BF16 = jnp.bfloat16
NT = (((1,), (1,)), ((), ()))
TN = (((0,), (0,)), ((), ()))


def dot(a, b):
    return jnp.dot(a, b, preferred_element_type=F32)


def dotx(a, b, dims):
    return lax.dot_general(a, b, dims, preferred_element_type=F32)


def fused_kernel(
    slots, line, lists_ref, q_hbm, k_hbm, v_hbm, og_hbm, w_hbm,
    dq_ref, dk_ref, dv_ref, dw_ref,
    q_ref, k_ref, v_ref, w_ref,
    my_list, every_list, present, pick, send_k, send_v, far_k, far_v, og_halves, columns,
    columns_t, w_in, grad, attn, prob,
    own_k, own_v, back_k, back_v, came_k, came_v,
    send_sem, recv_sem, up_send, up_recv, down_send, down_recv, load_sem,
    relay_send, relay_recv,
):
    rows, width = q_ref.shape
    heads = width // HD
    entries, lanes = my_list.shape
    frame_tokens = 32
    group_rows = CF * frame_tokens
    groups = rows // group_rows
    far_rows = slots * frame_tokens
    depth = w_ref.shape[0]
    chunks = 2
    span_width = width // chunks
    piece = depth // line
    half_rows = rows // 2
    scale = HD ** (-0.5)
    t = lax.axis_index("tm")
    h = lax.axis_index("head")
    z = lax.axis_index("dp")
    mate = t + 1 - 2 * (t % 2)
    partner = (t + 2) % 4
    diag = (mate + 2) % 4
    peers = (t, mate, partner, diag)

    barrier = pltpu.get_barrier_semaphore()
    for kind in (MATE, PARTNER, DIAG):
        pl.semaphore_signal(barrier, inc=1, device_id={"tm": peers[kind]})
    pl.semaphore_signal(barrier, inc=1, device_id={"head": 1 - h})

    @pl.when(z > 0)
    def greet_below():
        pl.semaphore_signal(barrier, inc=1, device_id={"dp": z - 1})

    @pl.when(z < line - 1)
    def greet_above():
        pl.semaphore_signal(barrier, inc=1, device_id={"dp": z + 1})

    loads = []
    for source, target in (
        (k_hbm, k_ref),
        (v_hbm, v_ref),
        (og_hbm.at[:, pl.ds(0, depth)], og_halves.at[h, 0]),
        (og_hbm.at[:, pl.ds(depth, depth)], og_halves.at[h, 1]),
        (q_hbm, q_ref),
        (w_hbm, w_ref),
    ):
        loads.append(pltpu.make_async_copy(source, target, load_sem.at[len(loads)]))
        loads[-1].start()
    load_k, load_v, load_og0, load_og1, load_q, load_w = loads

    for entry in range(entries):
        named = lists_ref[entry // RET, entry % RET]
        my_list[entry : entry + 1, :] = jnp.full((1, lanes), named, jnp.int32)
        every_list[SELF, entry : entry + 1, :] = jnp.full((1, lanes), named, jnp.int32)
    sides = (z + line - 1) // line + (2 * line - 2 - z) // line
    pl.semaphore_wait(barrier, 4 + sides)

    started = []

    def send(src, dst, target):
        number = len(started)
        copy = pltpu.make_async_remote_copy(
            src_ref=src, dst_ref=dst, send_sem=send_sem.at[number], recv_sem=recv_sem.at[number],
            device_id=target,
        )
        copy.start()
        started.append(copy)
        return copy

    def to(kind):
        return {"tm": peers[kind]}

    lists_in = [
        send(my_list, every_list.at[kind], to(kind)) for kind in (PARTNER, DIAG, MATE)
    ]

    def chunk_cols(chunk):
        return pl.ds(chunk * span_width, span_width)

    def piece_rows(index):
        return pl.ds(pl.multiple_of(index * piece, piece), piece)

    crossing = []
    for chunk in range(chunks):
        crossing.append(
            send(
                w_hbm.at[piece_rows(z), chunk_cols(chunk)],
                w_in.at[PARTNER, chunk, piece_rows(z)],
                to(PARTNER),
            )
        )
    def hop(chunk, step, upward):
        move = 1 if upward else -1
        index = z - step if upward else z + step
        index = jnp.clip(index, 0, line - 1)
        held = w_in.at[PARTNER, chunk, piece_rows(index)]
        sends, recvs = (up_send, up_recv) if upward else (down_send, down_recv)
        return pltpu.make_async_remote_copy(
            src_ref=held, dst_ref=held, send_sem=sends.at[chunk, step],
            recv_sem=recvs.at[chunk, step], device_id={"dp": z + move},
        )

    def hop_sent(step, upward):
        if upward:
            return (z - step >= 0) & (z < line - 1)
        return (z + step < line) & (z > 0)

    def hop_received(step, upward):
        if upward:
            return z - 1 - step >= 0
        return z + 1 + step < line

    def relay(chunk, step, upward):
        index = jnp.clip(z - 1 - step if upward else z + 1 + step, 0, line - 1)
        place = 2 * step + (0 if upward else 1)
        return pltpu.make_async_remote_copy(
            src_ref=w_in.at[PARTNER, chunk, piece_rows(index)],
            dst_ref=w_in.at[DIAG, chunk, piece_rows(index)],
            send_sem=relay_send.at[chunk, place], recv_sem=relay_recv.at[chunk, place],
            device_id=to(MATE),
        )

    def relay_done(chunk, received):
        for step in range(line - 1):
            for upward in (True, False):

                @pl.when(hop_received(step, upward))
                def done():
                    if received:
                        relay(chunk, step, upward).wait_recv()
                    else:
                        relay(chunk, step, upward).wait_send()

    def hop_wait(chunk, step):
        for upward in (True, False):

            @pl.when(hop_received(step, upward))
            def arrived():
                hop(chunk, step, upward).wait_recv()
                relay(chunk, step, upward).start()

    diag_w = []

    def hop_start(chunk, step):
        if step == 0:
            crossing[chunk].wait_recv()
        else:
            hop_wait(chunk, step - 1)
        for upward in (True, False):

            @pl.when(hop_sent(step, upward))
            def onward():
                hop(chunk, step, upward).start()

        if step == 0:
            diag_w.append(
                send(
                    w_in.at[PARTNER, chunk, piece_rows(z)],
                    w_in.at[DIAG, chunk, piece_rows(z)],
                    to(MATE),
                )
            )

    halves_in = []
    for part in range(2):
        halves_in.append(
            send(
                og_hbm.at[:, pl.ds(part * depth, depth)], og_halves.at[h, part], {"head": 1 - h}
            )
        )
    for copy in lists_in:
        copy.wait_recv()

    lane_frame = lax.shift_right_logical(
        lax.broadcasted_iota(jnp.int32, (entries, lanes), 1), 5
    )
    for side in range(rows // lanes):
        my_frame = (t * rows + side * lanes) // frame_tokens + lane_frame
        for kind in range(4):
            named = jnp.max((every_list[kind] == my_frame).astype(F32), axis=0, keepdims=True)
            present[
                kind * frame_tokens : (kind + 1) * frame_tokens,
                side * lanes : (side + 1) * lanes,
            ] = jnp.broadcast_to(named, (frame_tokens, lanes)).astype(BF16)
    above = lax.broadcasted_iota(jnp.int32, (rows, rows), 0)
    below = lax.broadcasted_iota(jnp.int32, (rows, rows), 1)
    earlier = (
        ((above & 31) == 0)
        & (lax.shift_right_logical(above, 5) < lax.shift_right_logical(below, 5))
    ).astype(F32).astype(BF16)
    rank = dot(present[...], earlier)
    token = lax.broadcasted_iota(jnp.int32, (frame_tokens, rows), 0)
    column_token = lax.broadcasted_iota(jnp.int32, (frame_tokens, rows), 1) & 31
    same_token = (token == column_token).astype(F32)
    for kind in range(4):
        span = slice(kind * frame_tokens, (kind + 1) * frame_tokens)
        here = present[span, :].astype(F32) * same_token
        for slot in range(slots):
            first = (kind * slots + slot) * frame_tokens
            pick[first : first + frame_tokens, :] = (
                here * (rank[span, :] == slot).astype(F32)
            ).astype(BF16)

    tile = 512

    def tiled(body):
        def step(i, carry):
            body(pl.ds(pl.multiple_of(i * tile, tile), tile))
            return carry

        lax.fori_loop(0, width // tile, step, 0)

    def span_of(kind):
        return pl.ds(kind * far_rows, far_rows)

    def pick_keys(cols):
        send_k[:, cols] = dot(pick[...], k_ref[:, cols]).astype(BF16)

    def pick_values(cols):
        send_v[:, cols] = dot(pick[...], v_ref[:, cols]).astype(BF16)

    frames_in = []
    load_k.wait()
    tiled(pick_keys)
    for kind in (PARTNER, DIAG, MATE):
        frames_in.append(send(send_k.at[span_of(kind)], far_k.at[span_of(kind)], to(kind)))
    load_v.wait()
    tiled(pick_values)
    for kind in (PARTNER, DIAG, MATE):
        frames_in.append(send(send_v.at[span_of(kind)], far_v.at[span_of(kind)], to(kind)))
    far_k[0:far_rows, :] = send_k[0:far_rows, :]
    far_v[0:far_rows, :] = send_v[0:far_rows, :]


    hop_start(0, 0)
    hop_start(0, 1)
    load_og0.wait()
    load_og1.wait()
    for copy in halves_in:
        copy.wait_recv()
    mine = pl.ds(pl.multiple_of(h * half_rows, half_rows), half_rows)
    columns_in = {}
    for kind in (PARTNER, DIAG):
        peer = peers[kind]
        columns_in[kind] = send(
            og_halves.at[peer // 2, peer % 2, mine], columns.at[kind, mine], to(kind)
        )
    columns_in[MATE] = send(og_halves.at[mate // 2, mate % 2], columns.at[MATE], to(MATE))
    columns[SELF] = og_halves[t // 2, t % 2]
    hop_start(0, 2)
    hop_start(1, 0)
    mate_w = [
        send(w_hbm.at[:, chunk_cols(chunk)], w_in.at[MATE, chunk], to(MATE))
        for chunk in range(chunks)
    ]
    hop_start(1, 1)

    load_q.wait()
    for copy in frames_in:
        copy.wait_recv()

    spans = [slice(g * group_rows, (g + 1) * group_rows) for g in range(groups)]

    def by_group(product):
        return jnp.concatenate([product(span) for span in spans], axis=0)

    def forward_head(i):
        cols = pl.ds(pl.multiple_of(i * HD, HD), HD)
        near = by_group(lambda span: dotx(q_ref[span, cols], k_ref[span, cols], NT)) * scale
        far = dotx(q_ref[:, cols], far_k[:, cols], NT) * scale
        top = jnp.maximum(
            jnp.max(near, axis=1, keepdims=True), jnp.max(far, axis=1, keepdims=True)
        )
        near = jnp.exp(near - top)
        far = jnp.exp(far - top)
        total = jnp.sum(near, axis=1, keepdims=True) + jnp.sum(far, axis=1, keepdims=True)
        near = near / total
        far = far / total
        prob[i, :, 0:group_rows] = near
        prob[i, :, group_rows:] = far
        near_low = near.astype(BF16)
        out = by_group(lambda span: dot(near_low[span], v_ref[span, cols]))
        attn[SELF, :, cols] = (out + dot(far.astype(BF16), far_v[:, cols])).astype(BF16)

    together = 3

    def several(head):
        def body(i, carry):
            for place in range(together):
                head(i * together + place)
            return carry

        return body

    forward = several(forward_head)
    each = heads // chunks
    attn_partner = []
    attn_mate = []
    part_width = span_width // 2
    for part in range(2 * chunks):
        lax.fori_loop(
            part * each // 2 // together, (part + 1) * each // 2 // together, forward, 0
        )
        cols = pl.ds(part * part_width, part_width)
        own = attn.at[SELF, :, cols]
        attn_partner.append(send(own, attn.at[PARTNER, :, cols], to(PARTNER)))
        attn_mate.append(send(own, attn.at[MATE, :, cols], to(MATE)))
        if part == 1:
            hop_start(1, 2)
            hop_wait(0, 2)
    swapped = []
    for kind in (PARTNER, DIAG):
        columns_in[kind].wait_recv()
        swapped.append(send(columns.at[kind, mine], columns.at[kind, mine], {"head": 1 - h}))

    def backward_head(i):
        cols = pl.ds(pl.multiple_of(i * HD, HD), HD)
        q = q_ref[:, cols]
        do = grad[:, cols]
        row_dot = jnp.sum(
            do.astype(F32) * attn[SELF, :, cols].astype(F32), axis=1, keepdims=True
        )
        near = prob[i, :, 0:group_rows]
        far = prob[i, :, group_rows:]
        near_dp = by_group(lambda span: dotx(do[span], v_ref[span, cols], NT))
        near_ds = (near * (near_dp - row_dot)).astype(BF16)
        far_ds = (far * (dotx(do, far_v[:, cols], NT) - row_dot)).astype(BF16)
        near_p = near.astype(BF16)
        near_dq = by_group(lambda span: dot(near_ds[span], k_ref[span, cols]))
        dq_ref[:, cols] = ((near_dq + dot(far_ds, far_k[:, cols])) * scale).astype(BF16)
        own_k[:, cols] = by_group(lambda span: dotx(near_ds[span], q[span], TN)) * scale
        own_v[:, cols] = by_group(lambda span: dotx(near_p[span], do[span], TN))
        back_k[:, cols] = (dotx(far_ds, q, TN) * scale).astype(BF16)
        back_v[:, cols] = dotx(far.astype(BF16), do, TN).astype(BF16)

    backward = several(backward_head)
    load_w.wait()
    returned = []
    step_width = span_width // 2
    for part in range(2 * chunks):
        chunk = part // 2
        if part % 2 == 0:
            if chunk == 1:
                hop_wait(1, 2)
            mate_w[chunk].wait_recv()
            diag_w[chunk].wait_recv()
            relay_done(chunk, True)
        local = pl.ds(part % 2 * step_width, step_width)
        cols = pl.ds(part * step_width, step_width)
        total = dot(og_halves[t // 2, t % 2], w_ref[:, cols])
        for kind in (MATE, PARTNER, DIAG):
            peer = peers[kind]
            total += dot(og_halves[peer // 2, peer % 2], w_in[kind, chunk, :, local])
        grad[:, cols] = total.astype(BF16)
        lax.fori_loop(
            part * each // 2 // together, (part + 1) * each // 2 // together, backward, 0
        )
        for kind in (PARTNER, DIAG, MATE):
            for out, into in ((back_k, came_k), (back_v, came_v)):
                returned.append(
                    send(out.at[span_of(kind), cols], into.at[span_of(kind), cols], to(kind))
                )
    came_k[0:far_rows, :] = back_k[0:far_rows, :]
    came_v[0:far_rows, :] = back_v[0:far_rows, :]
    attn_diag = []
    for part in range(2 * chunks):
        attn_partner[part].wait_recv()
        cols = pl.ds(part * part_width, part_width)
        attn_diag.append(send(attn.at[PARTNER, :, cols], attn.at[DIAG, :, cols], to(MATE)))
    columns_in[MATE].wait_recv()
    for copy in swapped:
        copy.wait_recv()
    for kind in range(4):
        columns_t[kind] = columns[kind].T
    for copy in attn_mate + attn_diag:
        copy.wait_recv()

    def weight_part(cols):
        total = dot(columns_t[SELF], attn[SELF, :, cols])
        for kind in (MATE, PARTNER, DIAG):
            total += dot(columns_t[kind], attn[kind, :, cols])
        dw_ref[:, cols] = total

    tiled(weight_part)

    per_part = len(returned) // (2 * chunks)
    for part in range(2 * chunks):
        for copy in returned[part * per_part : (part + 1) * per_part]:
            copy.wait_recv()
        cols = pl.ds(part * step_width, step_width)
        dk_ref[:, cols] = (own_k[:, cols] + dotx(pick[...], came_k[:, cols], TN)).astype(BF16)
        dv_ref[:, cols] = (own_v[:, cols] + dotx(pick[...], came_v[:, cols], TN)).astype(BF16)
    for copy in started:
        copy.wait_send()
    for chunk in range(chunks):
        for step in range(line - 1):
            for upward in (True, False):

                @pl.when(hop_sent(step, upward))
                def left():
                    hop(chunk, step, upward).wait_send()

    for chunk in range(chunks):
        relay_done(chunk, False)


def finish_kernel(dq_ref, dk_ref, dv_ref, dw_ref, dq_out, dk_out, dv_out, dw_out, sem):
    parts = 4
    piece = dw_ref.shape[0] // parts
    pairs = [
        (dw_ref.at[pl.ds(i * piece, piece)], dw_out.at[pl.ds(i * piece, piece)])
        for i in range(parts)
    ]
    pairs += [(dq_ref, dq_out), (dk_ref, dk_out), (dv_ref, dv_out)]
    copies = [
        pltpu.make_async_copy(source, target, sem.at[number])
        for number, (source, target) in enumerate(pairs)
    ]
    for copy in copies:
        copy.start()
    for copy in copies:
        copy.wait()


def finish(dq, dk, dv, dw):
    rows, width = dq.shape
    depth = dw.shape[0]
    vmem = pl.BlockSpec(memory_space=pltpu.VMEM)
    hbm = pl.BlockSpec(memory_space=pltpu.HBM)
    return pl.pallas_call(
        finish_kernel,
        out_shape=[jax.ShapeDtypeStruct((rows, width), BF16)] * 3
        + [jax.ShapeDtypeStruct((depth, width), F32)],
        in_specs=[vmem] * 4,
        out_specs=[hbm] * 4,
        scratch_shapes=[pltpu.SemaphoreType.DMA((7,))],
        compiler_params=pltpu.CompilerParams(vmem_limit_bytes=16 * 1024 * 1024),
        cost_estimate=pl.CostEstimate(flops=0, bytes_accessed=7 * 10**6, transcendentals=0),
    )(dq, dk, dv, dw)


def fused(queries, keys, values, out_grad, out_weight, lists):
    frames, frame_tokens, width = queries.shape
    rows = frames * frame_tokens
    depth = out_weight.shape[0]
    slots = RET // 4
    heads = width // HD
    flat = [x.reshape(rows, width) for x in (queries, keys, values, out_grad)]
    line = lax.axis_size("dp")
    hbm = pl.BlockSpec(memory_space=pltpu.HBM)
    far = 4 * slots * frame_tokens

    def low(*shape):
        return pltpu.VMEM(shape, BF16)

    def wide(*shape):
        return pltpu.VMEM(shape, F32)

    dq, dk, dv, dw = pl.pallas_call(
        functools.partial(fused_kernel, slots, line),
        out_shape=[pltpu.VMEM((rows, width), BF16)] * 3 + [pltpu.VMEM((depth, width), F32)],
        in_specs=[pl.BlockSpec(memory_space=pltpu.SMEM)] + [hbm] * 5,
        out_specs=[pl.BlockSpec(memory_space=pltpu.VMEM)] * 4,
        scratch_shapes=[
            low(rows, width),
            low(rows, width),
            low(rows, width),
            low(depth, width),
            pltpu.VMEM((lists.size, 128), jnp.int32),
            pltpu.VMEM((4, lists.size, 128), jnp.int32),
            low(4 * frame_tokens, rows),
            low(far, rows),
            low(far, width),
            low(far, width),
            low(far, width),
            low(far, width),
            low(2, 2, rows, depth),
            low(4, rows, depth),
            low(4, depth, rows),
            low(4, 2, depth, width // 2),
            low(rows, width),
            low(4, rows, width),
            wide(heads, rows, CF * frame_tokens + far),
            wide(rows, width),
            wide(rows, width),
            low(far, width),
            low(far, width),
            low(far, width),
            low(far, width),
            pltpu.SemaphoreType.DMA((64,)),
            pltpu.SemaphoreType.DMA((64,)),
            pltpu.SemaphoreType.DMA((2, line - 1)),
            pltpu.SemaphoreType.DMA((2, line - 1)),
            pltpu.SemaphoreType.DMA((2, line - 1)),
            pltpu.SemaphoreType.DMA((2, line - 1)),
            pltpu.SemaphoreType.DMA((6,)),
            pltpu.SemaphoreType.DMA((2, 2 * (line - 1))),
            pltpu.SemaphoreType.DMA((2, 2 * (line - 1))),
        ],
        compiler_params=pltpu.CompilerParams(
            collective_id=0, has_side_effects=True, vmem_limit_bytes=50 * 1024 * 1024
        ),
        cost_estimate=pl.CostEstimate(
            flops=7 * 10**9, bytes_accessed=16 * 10**6, transcendentals=10**6
        ),
    )(lists, *flat, out_weight)
    dq, dk, dv, dw = finish(dq, dk, dv, dw)
    back = [x.reshape(frames, frame_tokens, width) for x in (dq, dk, dv)]
    return (*back, dw)


def solution(mesh):
    whole_fits = dict(mesh.shape) == {"dp": 4, "tm": 4, "head": 2}
    return jax.shard_map(
        fused if whole_fits else per_device,
        mesh=mesh,
        in_specs=(
            P(("dp", "tm"), None, "head"),
            P(("dp", "tm"), None, "head"),
            P(("dp", "tm"), None, "head"),
            P(("dp", "tm"), None, "head"),
            P("tm", "head"),
            P(("dp", "tm"), None),
        ),
        out_specs=(
            P(("dp", "tm"), None, "head"),
            P(("dp", "tm"), None, "head"),
            P(("dp", "tm"), None, "head"),
            P(("dp", "tm"), "head"),
        ),
        check_vma=False,
    )
```
